256 devices in a mesh: dp: 8 (over x, core), seq: 32 (over y, z).
Axes of the slice: x: 4, y: 4, z: 8, core: 2. Of those that a mesh axis runs over, the one named last changes fastest.
Arguments:
- tokens: bfloat16 [8, 16384, 5120], P('dp', 'seq'), may hold values from -0.059814453 to 0.059814453
- router_weight: float32 [5120], replicated, may hold values from -9 to 9
- routes: int32 [8, 4096], P('dp', 'seq'), may hold values from 0 to 511, as said below
- counts: int32 [8, 32], P('dp', 'seq'), may hold values from 0 to 128, as said below
- query: bfloat16 [8, 4096, 4096], P('dp', 'seq'), may hold values from -120 to 120
- key_in: bfloat16 [8, 4096, 512], P('dp', 'seq'), may hold values from -4 to 4
- value_in: bfloat16 [8, 4096, 512], P('dp', 'seq'), may hold values from -6 to 6
- attn_out: bfloat16 [8, 4096, 4096], P('dp', 'seq'), may hold values from -3 to 3
- grad_out: bfloat16 [8, 4096, 4096], P('dp', 'seq'), may hold values from -6 to 6
Outputs:
- query_grad: bfloat16 [8, 4096, 4096], P('dp', 'seq')
- key_grad: bfloat16 [8, 4096, 512], P('dp', 'seq')
- value_grad: bfloat16 [8, 4096, 512], P('dp', 'seq')
- router_grad: float32 [5120], P(('dp', 'seq'))
The draws below stay inside these ranges and needn't reach their ends.
Inputs may be any that keep to these rules, and one draw needn't show every extreme that they name: In each sequence the 32 counts sum to 2048; some shard's count is 128. `routes`: entries s * 128 to s * 128 + 127 belong to shard s; those below the shard's count hold distinct token indices of that shard, increasing; the others hold 0.
All inputs are finite; a program needn't handle non-finite values.
Results may differ from the reference program's by a relative error of at most 0.017.
Values may be sent and summed in bfloat16 or wider, within the bound.
A program may use at most 64 MiB of HBM per device.

```python
import math
import jax
import jax.numpy as jnp
from jax import lax

D = 5120
HEADS = 32
KV = 4
HD = 128
TOK_DEV = 512
CAP = 128
KEEP = 2048
SLOTS = 4096
SEQLEN = 16384
SEQS = 8
N_SEQ = 32


def shared_counts(key):
    base_key = jax.random.fold_in(key, 101)

    def one_row(row_key):
        order_key, size_key = jax.random.split(row_key)
        shard_order = jax.random.permutation(order_key, N_SEQ)
        first_sizes = jax.random.randint(size_key, (N_SEQ // 2,), 0, CAP + 1)
        first_sizes = first_sizes.at[0].set(CAP)
        filled = jnp.zeros((N_SEQ,), jnp.int32).at[shard_order[0::2]].set(first_sizes)
        return filled.at[shard_order[1::2]].set(CAP - first_sizes)
    return jax.vmap(one_row)(jax.random.split(base_key, SEQS)).astype(jnp.int32)


def shared_keys(key):
    base_key = jax.random.fold_in(key, 303)
    return jnp.clip(jax.random.normal(base_key, (SEQS, SLOTS, KV * HD), jnp.float32), -4.0, 4.0)


def draw_counts(key, part):
    return shared_counts(key)


def draw_routes(key, part):
    count_table = shared_counts(key)
    key = jax.random.fold_in(key, 202)
    shard_keys = jax.random.split(key, SEQS * N_SEQ)

    def one_shard(shard_key, shard_count):
        ranking = jax.random.permutation(shard_key, TOK_DEV)
        places = jnp.arange(TOK_DEV, dtype=jnp.int32)
        ordering = jnp.where(ranking < shard_count, places, TOK_DEV + places)
        picked = jnp.argsort(ordering)[:CAP].astype(jnp.int32)
        return jnp.where(jnp.arange(CAP, dtype=jnp.int32) < shard_count, picked, 0)
    route_table = jax.vmap(one_shard)(shard_keys, count_table.reshape(SEQS * N_SEQ))
    return route_table.reshape(SEQS, N_SEQ * CAP).astype(jnp.int32)


def draw_key_in(key, part):
    key_table = shared_keys(key)
    return key_table.astype(jnp.bfloat16)


def draw_query(key, part):
    key = jax.random.fold_in(key, 505)
    values_drawn = 2.0 * jnp.clip(jax.random.normal(key, (SEQS, SLOTS, HEADS * HD), jnp.float32), -6.0, 6.0)
    return values_drawn.astype(jnp.bfloat16)


def strengthened(drawn, rng, source, target, blocks, factor):
    def block_of(axis_at):
        return (jnp.arange(drawn.shape[axis_at]) // (drawn.shape[axis_at] // blocks)).reshape((-1,) + (1,) * (drawn.ndim - 1 - axis_at))

    first = jax.random.permutation(rng, blocks)[block_of(target)]
    far = (block_of(target) + blocks // 2) % blocks
    return jnp.where((block_of(source) == first) | (block_of(source) == far), factor * drawn, drawn)


def block_scale(key, shape, cuts, low, largest):
    loudness, own = 1.0, jax.random.fold_in(key, 6)
    for axis_at, parts in cuts:
        heights = jnp.exp(jax.random.uniform(jax.random.fold_in(own, axis_at), (parts,), jnp.float32, low / len(cuts), largest / len(cuts)))
        loudness = loudness * jnp.repeat(heights, shape[axis_at] // parts).reshape([-1 if axis == axis_at else 1 for axis in range(len(shape))])
    return loudness


def gaussian(own_key, shape, width, limit, pieces=(), kind=jnp.bfloat16):
    array = jax.random.normal(own_key, shape, jnp.float32) * width
    if len(pieces) > 0:
        array = block_scale(own_key, shape, pieces, -0.22, 0.18) * array
    return jnp.clip(array, min=-limit, max=limit).astype(kind)


def heavy_noise(stream_key, shape, width, limit, pieces, heavy, held_as=jnp.bfloat16):
    entries = width * jax.random.normal(stream_key, shape, jnp.float32)
    if pieces:
        entries = entries * block_scale(stream_key, shape, pieces, -0.22, 0.18)
    return jnp.clip(strengthened(entries, jax.random.fold_in(stream_key, 3), *heavy), -limit, limit).astype(held_as)


def setup_inputs(seed: int = 0) -> dict:
    key_of = jax.random.split(jax.random.key(seed), 10)
    tokens = heavy_noise(key_of[0], (SEQS, SEQLEN, D), 0.01, 0.059814453, ((0, 8), (1, 32)), (1, 2, 32, 2.75))
    router_weight = gaussian(key_of[1], (D,), 1.5, 9.0, (), jnp.float32)
    routes = draw_routes(jax.random.fold_in(key_of[9], 71), 0)
    counts = draw_counts(jax.random.fold_in(key_of[9], 71), 0)
    query = draw_query(jax.random.fold_in(key_of[9], 71), 0)
    key_in = draw_key_in(jax.random.fold_in(key_of[9], 71), 0)
    value_in = gaussian(key_of[6], (SEQS, SLOTS, KV * HD), 1.0, 6.0, ((0, 8), (1, 32)))
    attn_out = gaussian(key_of[7], (SEQS, SLOTS, HEADS * HD), 0.5, 3.0, ((0, 8), (1, 32)))
    grad_out = gaussian(key_of[8], (SEQS, SLOTS, HEADS * HD), 1.0, 6.0, ((0, 8), (1, 32)))
    return dict(tokens=tokens, router_weight=router_weight, routes=routes, counts=counts, query=query, key_in=key_in, value_in=value_in, attn_out=attn_out, grad_out=grad_out)


NEGATIVE = -1e+30

def head_gradients(query_rows, key_rows, value_rows, dout_rows, delta_rows, allowed):
    inverse_root = 1.0 / math.sqrt(HD)
    raw_scores = jnp.dot(query_rows, key_rows.T, preferred_element_type=jnp.float32) * inverse_root
    masked_scores = jnp.where(allowed, raw_scores, NEGATIVE)
    log_total = jax.nn.logsumexp(masked_scores, axis=1)
    probability = jnp.exp(masked_scores - log_total[:, None])
    value_part = jnp.dot(probability.astype(jnp.bfloat16).T, dout_rows, preferred_element_type=jnp.float32)
    prob_grad = jnp.dot(dout_rows, value_rows.T, preferred_element_type=jnp.float32)
    score_grad = (probability * (prob_grad - delta_rows[:, None]) * inverse_root).astype(jnp.bfloat16)
    query_part = jnp.dot(score_grad, key_rows, preferred_element_type=jnp.float32)
    key_part = jnp.dot(score_grad.T, query_rows, preferred_element_type=jnp.float32)
    key_part = lax.optimization_barrier(key_part.astype(jnp.bfloat16)).astype(jnp.float32)
    value_part = lax.optimization_barrier(value_part.astype(jnp.bfloat16)).astype(jnp.float32)
    return (query_part, key_part, value_part)

def reference(tokens, router_weight, routes, counts, query, key_in, value_in, attn_out, grad_out):
    group_size = HEADS // KV

    def one_sequence(seq_items):
        token_rows, route_row, count_row, query_rows, key_rows, value_rows, out_rows, cot_rows = seq_items
        slot_index = jnp.arange(SLOTS, dtype=jnp.int32)
        shard_index = slot_index // CAP
        live_slots = slot_index % CAP < count_row[shard_index]
        position = shard_index * TOK_DEV + route_row
        picked = token_rows[position].astype(jnp.float32)
        logit = jnp.dot(picked, router_weight, precision=lax.Precision.HIGHEST)
        gate_value = jax.nn.sigmoid(logit)
        kept_gate = jnp.where(live_slots, gate_value, 0.0)
        cotangent = cot_rows.astype(jnp.float32)
        scaled_cot = (kept_gate[:, None] * cotangent).astype(jnp.bfloat16)
        gate_grad = lax.optimization_barrier(jnp.sum(cotangent * out_rows.astype(jnp.float32), axis=1))
        logit_grad = jnp.where(live_slots, gate_grad * gate_value * (1.0 - gate_value), 0.0)
        weight_part = jnp.dot(logit_grad, picked, precision=lax.Precision.HIGHEST)
        deltas = lax.optimization_barrier(jnp.sum((scaled_cot.astype(jnp.float32) * out_rows.astype(jnp.float32)).reshape(SLOTS, HEADS, HD), axis=2))
        order_rows = jnp.argsort(jnp.where(live_slots, slot_index, SLOTS + slot_index))
        chosen = order_rows[:KEEP].astype(jnp.int32)
        kept_position = position[chosen]
        allowed = kept_position[None, :] <= kept_position[:, None]
        kept_query = query_rows[chosen].reshape(KEEP, HEADS, HD)
        kept_key = key_rows[chosen].reshape(KEEP, KV, HD)
        kept_value = value_rows[chosen].reshape(KEEP, KV, HD)
        kept_dout = scaled_cot[chosen].reshape(KEEP, HEADS, HD)
        kept_delta = deltas[chosen]

        def per_head(head_index):
            shared_head = head_index // group_size
            return head_gradients(kept_query[:, head_index], kept_key[:, shared_head], kept_value[:, shared_head], kept_dout[:, head_index], kept_delta[:, head_index], allowed)
        query_part, key_part, value_part = lax.map(per_head, jnp.arange(HEADS, dtype=jnp.int32))
        query_part = jnp.transpose(query_part, (1, 0, 2)).reshape(KEEP, HEADS * HD)
        key_part = jnp.transpose(lax.optimization_barrier(jnp.sum(key_part.reshape(KV, group_size, KEEP, HD), axis=1)), (1, 0, 2)).reshape(KEEP, KV * HD)
        value_part = jnp.transpose(lax.optimization_barrier(jnp.sum(value_part.reshape(KV, group_size, KEEP, HD), axis=1)), (1, 0, 2)).reshape(KEEP, KV * HD)
        query_full = jnp.zeros((SLOTS, HEADS * HD), jnp.float32).at[chosen].set(query_part).astype(jnp.bfloat16)
        key_full = jnp.zeros((SLOTS, KV * HD), jnp.float32).at[chosen].set(key_part).astype(jnp.bfloat16)
        value_full = jnp.zeros((SLOTS, KV * HD), jnp.float32).at[chosen].set(value_part).astype(jnp.bfloat16)
        return (query_full, key_full, value_full, weight_part)
    query_all, key_all, value_all, weight_all = lax.map(one_sequence, (tokens, routes, counts, query, key_in, value_in, attn_out, grad_out))
    return (query_all, key_all, value_all, lax.optimization_barrier(jnp.sum(weight_all, axis=0)))
```

```python
import functools
import math

import jax
import jax.numpy as jnp
from jax import lax
from jax.experimental import pallas as pl
from jax.experimental.pallas import tpu as pltpu
from jax.sharding import PartitionSpec as P

HEADS = 32
KV = 4
HD = 128
GROUP = HEADS // KV
WIDE = GROUP * HD
KEEP = 2048
NEGATIVE = -1e30
MESH = pl.DeviceIdType.MESH
MIB = 1024 * 1024


def place(z_count):
    me = lax.axis_index("seq")
    return me // z_count, me % z_count


def remote(src, dst, send_sem, recv_sem, device):
    return pltpu.make_async_remote_copy(
        src_ref=src,
        dst_ref=dst,
        send_sem=send_sem,
        recv_sem=recv_sem,
        device_id=device,
        device_id_type=MESH,
    )


def greet(devices):
    barrier = pltpu.get_barrier_semaphore()
    for device in devices:
        pl.semaphore_signal(barrier, inc=1, device_id=device, device_id_type=MESH)


def ring_plan(z_count):
    longer = z_count // 2
    shorter = z_count - 1 - longer
    return ((0, 1, longer), (1, -1, longer), (1, 1, shorter), (0, -1, shorter))


def gather_kernel(
    y_count, z_count, chunks,
    tokens, weight, routes, counts, query, key_in, value_in, attn_out, grad_out,
    q_all, do_all, de_all, k_all, v_all, c_all, part,
    tok_v, cot_v, attn_v, dout_v, de_v, cnt_v, picked_v,
    tok_sem, in_sem, own_sem, y_send, y_recv, ring_send, ring_recv, c_send, c_recv,
):
    y, z = place(z_count)
    cap = query.shape[0]
    tok_count = tokens.shape[0]
    chunk = tokens.shape[1] // chunks

    def at(y_there, z_there):
        return {"seq": y_there * z_count + z_there}

    right, left = (z + 1) % z_count, (z + z_count - 1) % z_count
    y_peers = [(y + step) % y_count for step in range(1, y_count)]
    greet([at(other, z) for other in y_peers] + [at(y, right), at(y, left)])

    loads = []
    for c in range(chunks):
        loads.append(pltpu.make_async_copy(tokens.at[:, pl.ds(c * chunk, chunk)], tok_v.at[c], tok_sem.at[c]))
        loads[-1].start()
    rows_in = []
    for g in range(y_count):
        for a, (source, target) in enumerate(((grad_out, cot_v), (attn_out, attn_v))):
            rows_in.append(
                pltpu.make_async_copy(source.at[:, pl.ds(g * WIDE, WIDE)], target.at[g], in_sem.at[a, g])
            )
            rows_in[-1].start()
    cnt_v[...] = jnp.full(cnt_v.shape, counts[0, 0], jnp.int32)

    def wide(ref, g):
        return ref.at[:, pl.ds(pl.multiple_of(g * WIDE, WIDE), WIDE)]

    def narrow(ref, g):
        return ref.at[:, pl.ds(pl.multiple_of(g * HD, HD), HD)]

    own = [
        pltpu.make_async_copy(narrow(key_in, y), k_all.at[z, y], own_sem.at[0]),
        pltpu.make_async_copy(narrow(value_in, y), v_all.at[z, y], own_sem.at[1]),
        pltpu.make_async_copy(cnt_v, c_all.at[z, y], own_sem.at[2]),
        pltpu.make_async_copy(wide(query, y), q_all.at[y], own_sem.at[3]),
    ]
    for copy in own:
        copy.start()
    pl.semaphore_wait(pltpu.get_barrier_semaphore(), y_count + 1)

    first = []
    for i, other in enumerate(y_peers):
        there = at(other, z)
        for a, (source, target) in enumerate(
            (
                (narrow(key_in, other), k_all.at[z, y]),
                (narrow(value_in, other), v_all.at[z, y]),
                (cnt_v, c_all.at[z, y]),
            )
        ):
            first.append(remote(source, target, y_send.at[a, i], y_recv.at[a, i], there))
            first[-1].start()
    late = []
    for i, other in enumerate(y_peers):
        late.append(remote(wide(query, other), q_all.at[y], y_send.at[3, i], y_recv.at[3, i], at(other, z)))
        late[-1].start()
    for copy in own[:3]:
        copy.wait()
    for copy in first:
        copy.wait_recv()

    plan = ring_plan(z_count)
    held = (k_all, v_all)

    def ring_copy(lane, step):
        array, way, _ = plan[lane]
        block = (z - way * step + 2 * z_count) % z_count
        there = at(y, right if way == 1 else left)
        ref = held[array].at[block]
        return remote(ref, ref, ring_send.at[lane, step], ring_recv.at[lane, step], there)

    def count_copy(way, step):
        block = (z - way * step + 2 * z_count) % z_count
        there = at(y, right if way == 1 else left)
        ref = c_all.at[block]
        side = (1 - way) // 2
        return remote(ref, ref, c_send.at[side, step], c_recv.at[side, step], there)

    def forward(step):
        for lane, (array, way, steps) in enumerate(plan):
            if 0 < step <= steps:
                ring_copy(lane, step - 1).wait_recv()
            if step < steps:
                ring_copy(lane, step).start()
            if array == 0:
                if 0 < step <= steps:
                    count_copy(way, step - 1).wait_recv()
                if step < steps:
                    count_copy(way, step).start()

    forward(0)

    token_at = lax.broadcasted_iota(jnp.int32, (tok_count, cap), 0)
    hot = jnp.where(token_at == routes[...], 1.0, 0.0).T.astype(jnp.bfloat16)
    logit = jnp.zeros((cap, HD), jnp.float32)
    for c in range(chunks):
        loads[c].wait()
        picked = jnp.dot(hot, tok_v[c], preferred_element_type=jnp.float32)
        picked_v[c] = picked
        scaled = picked * weight[:, c * chunk : (c + 1) * chunk]
        for t in range(chunk // HD):
            logit = logit + scaled[:, t * HD : (t + 1) * HD]
    logit = jnp.sum(logit, axis=1, keepdims=True)
    gate = 1.0 / (1.0 + jnp.exp(-logit))
    live = lax.broadcasted_iota(jnp.int32, (cap, 1), 0) < counts[0, 0]
    kept = jnp.where(live, gate, 0.0)
    for copy in rows_in:
        copy.wait()

    lane_at = lax.broadcasted_iota(jnp.int32, (cap, HD), 1)

    def scale_group(other):
        gate_sum = jnp.zeros((cap, HD), jnp.float32)
        deltas = jnp.zeros((cap, HD), jnp.float32)
        for h in range(GROUP):
            cols = slice(h * HD, (h + 1) * HD)
            cot = cot_v[other, :, cols].astype(jnp.float32)
            out = attn_v[other, :, cols].astype(jnp.float32)
            dout = (kept * cot).astype(jnp.bfloat16)
            dout_v[other, :, cols] = dout
            gate_sum = gate_sum + cot * out
            delta = jnp.sum(dout.astype(jnp.float32) * out, axis=1, keepdims=True)
            deltas = jnp.where(lane_at == h, delta, deltas)
        de_v[other] = deltas.T[:GROUP]
        return gate_sum

    gate_sum = jnp.zeros((cap, HD), jnp.float32)
    for i, other in enumerate(y_peers):
        gate_sum = gate_sum + scale_group(other)
        for a, (source, target) in enumerate(((dout_v, do_all), (de_v, de_all))):
            late.append(
                remote(source.at[other], target.at[y], y_send.at[4 + a, i], y_recv.at[4 + a, i], at(other, z))
            )
            late[-1].start()
    forward(1)
    gate_sum = gate_sum + scale_group(y)
    mine = [
        pltpu.make_async_copy(dout_v.at[y], do_all.at[y], own_sem.at[4]),
        pltpu.make_async_copy(de_v.at[y], de_all.at[y], own_sem.at[5]),
    ]
    for copy in mine:
        copy.start()
    forward(2)
    gate_grad = jnp.sum(gate_sum, axis=1, keepdims=True)
    logit_grad = jnp.where(live, gate_grad * gate * (1.0 - gate), 0.0)
    segments = part.shape[1]
    for c in range(chunks):
        terms = jnp.sum(logit_grad * picked_v[c], axis=0, keepdims=True)
        for t in range(chunk // HD):
            n = c * (chunk // HD) + t
            part[n // segments, n % segments : n % segments + 1, :] = terms[:, t * HD : (t + 1) * HD]
    for step in range(3, max(p[2] for p in plan) + 1):
        forward(step)
    own[3].wait()
    for copy in mine:
        copy.wait()
    for copy in first:
        copy.wait_send()
    for copy in late:
        copy.wait()
    for lane, (array, way, steps) in enumerate(plan):
        for step in range(steps):
            ring_copy(lane, step).wait_send()
            if array == 0:
                count_copy(way, step).wait_send()


def gather(y_count, z_count, dp_count, tokens, weight, routes, counts, query, key_in, value_in, attn_out, grad_out):
    cap = query.shape[0]
    tok_count, width = tokens.shape
    chunks = 5
    longer = z_count // 2
    anywhere = pl.BlockSpec(memory_space=pl.ANY)
    vmem = pl.BlockSpec(memory_space=pltpu.VMEM)
    smem = pl.BlockSpec(memory_space=pltpu.SMEM)
    bf16, f32 = jnp.bfloat16, jnp.float32
    shape = jax.ShapeDtypeStruct
    return pl.pallas_call(
        functools.partial(gather_kernel, y_count, z_count, chunks),
        out_shape=(
            shape((y_count, cap, WIDE), bf16),
            shape((y_count, cap, WIDE), bf16),
            shape((y_count, GROUP, cap), f32),
            shape((z_count, y_count, cap, HD), bf16),
            shape((z_count, y_count, cap, HD), bf16),
            shape((z_count, y_count, 1, HD), jnp.int32),
            shape((dp_count, width // HD // dp_count, HD), f32),
        ),
        in_specs=[anywhere, vmem, vmem, smem] + [anywhere] * 5,
        out_specs=(anywhere,) * 6 + (vmem,),
        scratch_shapes=[
            pltpu.VMEM((chunks, tok_count, width // chunks), bf16),
            pltpu.VMEM((y_count, cap, WIDE), bf16),
            pltpu.VMEM((y_count, cap, WIDE), bf16),
            pltpu.VMEM((y_count, cap, WIDE), bf16),
            pltpu.VMEM((y_count, GROUP, cap), f32),
            pltpu.VMEM((1, HD), jnp.int32),
            pltpu.VMEM((chunks, cap, width // chunks), f32),
            pltpu.SemaphoreType.DMA((chunks,)),
            pltpu.SemaphoreType.DMA((2, y_count)),
            pltpu.SemaphoreType.DMA((6,)),
            pltpu.SemaphoreType.DMA((6, y_count - 1)),
            pltpu.SemaphoreType.DMA((6, y_count - 1)),
            pltpu.SemaphoreType.DMA((4, longer)),
            pltpu.SemaphoreType.DMA((4, longer)),
            pltpu.SemaphoreType.DMA((2, longer)),
            pltpu.SemaphoreType.DMA((2, longer)),
        ],
        compiler_params=pltpu.CompilerParams(
            collective_id=0, has_side_effects=True, vmem_limit_bytes=40 * MIB
        ),
        name="gather",
    )(tokens, weight, routes, counts, query, key_in, value_in, attn_out, grad_out)


def attention_kernel(
    y_count, z_count, block_rows, block_keys,
    counts, q_in, do_in, de_in, k_in, v_in,
    dq_out, dk_out, dv_out,
    row_f, do_f, de_f, q_b, do_b, de_b, k_f, v_f, k_b, v_b, scores, dk_f, dv_f, dq_f,
):
    cap = q_in.shape[1]
    z = lax.axis_index("seq") % z_count
    shard_count = y_count * z_count
    lanes = GROUP * block_rows
    key_blocks = KEEP // block_keys
    root = 1.0 / math.sqrt(HD)
    power = root * math.log2(math.e)
    f32, bf16 = jnp.float32, jnp.bfloat16

    def pack_keys(shard, offset):
        zz, yy = shard % z_count, shard // z_count
        k_f[pl.ds(offset, cap), :] = k_in[zz, yy].astype(f32)
        v_f[pl.ds(offset, cap), :] = v_in[zz, yy].astype(f32)
        return offset + counts[zz, yy, 0, 0]

    lax.fori_loop(0, shard_count, pack_keys, jnp.int32(0))

    def narrow_keys(b, carry):
        rows = pl.ds(b * block_keys, block_keys)
        k_b[b] = k_f[rows, :].astype(bf16)
        v_b[b] = v_f[rows, :].astype(bf16)
        dk_f[b] = jnp.zeros((block_keys, HD), f32)
        dv_f[b] = jnp.zeros((block_keys, HD), f32)
        return carry

    lax.fori_loop(0, key_blocks, narrow_keys, 0)

    shard_start = []
    total = 0
    for s in range(shard_count):
        shard_start.append(total)
        total = total + counts[s % z_count, s // z_count, 0, 0]

    def key_start(yy):
        picked = jnp.int32(0)
        for zz in range(z_count):
            picked = jnp.where(z == zz, shard_start[yy * z_count + zz], picked)
        return picked

    row_start, shift, live = [], [], []
    rows_here = 0
    for yy in range(y_count):
        row_start.append(rows_here)
        shift.append(key_start(yy) - rows_here)
        live.append(counts[z, yy, 0, 0])
        rows_here = rows_here + live[yy]

    def place_of(row):
        found = row + shift[0]
        for yy in range(1, y_count):
            found = jnp.where(row >= row_start[yy], row + shift[yy], found)
        return found

    for yy in range(y_count):
        rows = pl.ds(row_start[yy], cap)
        for h in range(GROUP):
            cols = slice(h * HD, (h + 1) * HD)
            row_f[h, rows, :] = q_in[yy, :, cols].astype(f32)
            do_f[h, rows, :] = do_in[yy, :, cols].astype(f32)
        padded = jnp.concatenate([de_in[yy], jnp.zeros((HD - GROUP, cap), f32)], axis=0)
        de_f[rows, :] = padded.T
    tail = pl.ds(rows_here, block_rows)
    for h in range(GROUP):
        row_f[h, tail, :] = jnp.zeros((block_rows, HD), f32)
        do_f[h, tail, :] = jnp.zeros((block_rows, HD), f32)
    de_f[tail, :] = jnp.zeros((block_rows, HD), f32)

    row_blocks = (rows_here + block_rows - 1) // block_rows

    def narrow_rows(b, carry):
        rows = pl.ds(pl.multiple_of(b * block_rows, block_rows), block_rows)
        across = de_f[rows, :].T
        for h in range(GROUP):
            mine = slice(h * block_rows, (h + 1) * block_rows)
            q_b[b, mine, :] = row_f[h, rows, :].astype(bf16)
            do_b[b, mine, :] = do_f[h, rows, :].astype(bf16)
            de_b[b, :, mine] = across[h : h + 1, :]
        return carry

    lax.fori_loop(0, row_blocks, narrow_rows, 0)

    nt = (((1,), (1,)), ((), ()))
    tn = (((0,), (0,)), ((), ()))

    def fold(values, combine):
        return combine(values.reshape(block_keys // 8, 8, lanes), axis=0)

    def row_block(b, carry):
        base = b * block_rows
        lane = lax.broadcasted_iota(jnp.int32, (1, lanes), 1)
        row_place = place_of(base + lane % block_rows)
        lowest = place_of(base)
        highest = place_of(jnp.minimum(base + block_rows, rows_here) - 1)
        full = (lowest + 1) // block_keys
        used = highest // block_keys + 1
        queries, douts, delta = q_b[b], do_b[b], de_b[b]

        def score(masked, kb, best):
            block = lax.dot_general(k_b[kb], queries, nt, preferred_element_type=f32)
            if masked:
                key_place = kb * block_keys + lax.broadcasted_iota(jnp.int32, (block_keys, lanes), 0)
                block = jnp.where(key_place <= row_place, block, NEGATIVE)
            scores[kb] = block
            return jnp.maximum(best, fold(block, jnp.max))

        best = jnp.full((8, lanes), NEGATIVE, f32)
        best = lax.fori_loop(0, full, functools.partial(score, False), best)
        best = lax.fori_loop(full, used, functools.partial(score, True), best)
        top = jnp.max(best, axis=0, keepdims=True) * power

        def add_up(kb, total):
            return total + fold(jnp.exp2(scores[kb] * power - top), jnp.sum)

        total = lax.fori_loop(0, used, add_up, jnp.zeros((8, lanes), f32))
        log_total = top + jnp.log2(jnp.sum(total, axis=0, keepdims=True))
        dq_f[:, :] = jnp.zeros(dq_f.shape, f32)

        def grads(kb, carry):
            prob = jnp.exp2(scores[kb] * power - log_total)
            prob_grad = lax.dot_general(v_b[kb], douts, nt, preferred_element_type=f32)
            dv_f[kb] += jnp.dot(prob.astype(bf16), douts, preferred_element_type=f32)
            score_grad = (prob * (prob_grad - delta)).astype(bf16)
            dk_f[kb] += jnp.dot(score_grad, queries, preferred_element_type=f32)
            dq_f[:, :] += lax.dot_general(score_grad, k_b[kb], tn, preferred_element_type=f32)
            return carry

        lax.fori_loop(0, used, grads, 0)
        rows = pl.ds(pl.multiple_of(base, block_rows), block_rows)
        for h in range(GROUP):
            row_f[h, rows, :] = dq_f[h * block_rows : (h + 1) * block_rows, :] * root
        return carry

    lax.fori_loop(0, row_blocks, row_block, 0)

    slot = lax.broadcasted_iota(jnp.int32, (cap, 1), 0)
    for yy in range(y_count):
        rows = pl.ds(row_start[yy], cap)
        for h in range(GROUP):
            grad = jnp.where(slot < live[yy], row_f[h, rows, :], 0.0)
            dq_out[yy, :, h * HD : (h + 1) * HD] = grad.astype(bf16)

    def widen_keys(b, carry):
        rows = pl.ds(pl.multiple_of(b * block_keys, block_keys), block_keys)
        k_f[rows, :] = dk_f[b] * root
        v_f[rows, :] = dv_f[b]
        return carry

    lax.fori_loop(0, key_blocks, widen_keys, 0)

    def unpack_keys(shard, offset):
        zz, yy = shard % z_count, shard // z_count
        count = counts[zz, yy, 0, 0]
        rows = pl.ds(offset, cap)
        dk_out[zz, yy] = jnp.where(slot < count, k_f[rows, :], 0.0).astype(bf16)
        dv_out[zz, yy] = jnp.where(slot < count, v_f[rows, :], 0.0).astype(bf16)
        return offset + count

    lax.fori_loop(0, shard_count, unpack_keys, jnp.int32(0))


def attention(y_count, z_count, counts, q_in, do_in, de_in, k_in, v_in):
    cap = q_in.shape[1]
    block_rows, block_keys = 64, 256
    lanes = GROUP * block_rows
    most = y_count * cap
    row_blocks = most // block_rows
    key_blocks = KEEP // block_keys
    vmem = pl.BlockSpec(memory_space=pltpu.VMEM)
    bf16, f32 = jnp.bfloat16, jnp.float32
    shape = jax.ShapeDtypeStruct
    return pl.pallas_call(
        functools.partial(attention_kernel, y_count, z_count, block_rows, block_keys),
        out_shape=(
            shape((y_count, cap, WIDE), bf16),
            shape((z_count, y_count, cap, HD), bf16),
            shape((z_count, y_count, cap, HD), bf16),
        ),
        in_specs=[pl.BlockSpec(memory_space=pltpu.SMEM)] + [vmem] * 5,
        out_specs=(vmem,) * 3,
        scratch_shapes=[
            pltpu.VMEM((GROUP, most + cap, HD), f32),
            pltpu.VMEM((GROUP, most + cap, HD), f32),
            pltpu.VMEM((most + cap, HD), f32),
            pltpu.VMEM((row_blocks, lanes, HD), bf16),
            pltpu.VMEM((row_blocks, lanes, HD), bf16),
            pltpu.VMEM((row_blocks, 1, lanes), f32),
            pltpu.VMEM((KEEP + cap, HD), f32),
            pltpu.VMEM((KEEP + cap, HD), f32),
            pltpu.VMEM((key_blocks, block_keys, HD), bf16),
            pltpu.VMEM((key_blocks, block_keys, HD), bf16),
            pltpu.VMEM((key_blocks, block_keys, lanes), f32),
            pltpu.VMEM((key_blocks, block_keys, HD), f32),
            pltpu.VMEM((key_blocks, block_keys, HD), f32),
            pltpu.VMEM((lanes, HD), f32),
        ],
        compiler_params=pltpu.CompilerParams(vmem_limit_bytes=48 * MIB),
        name="attention",
    )(counts, q_in, do_in, de_in, k_in, v_in)


def scatter_kernel(
    y_count, z_count, dp_count,
    dq_in, dk_in, dv_in, part,
    dq_out, dk_out, dv_out, router_out,
    held, fin, dp_held, y_held, z_held, dp_sum, y_sum,
    own_sem, q_send, q_recv, ring_send, ring_recv, fin_send, fin_recv, r_send, r_recv,
):
    y, z = place(z_count)
    dp = lax.axis_index("dp")
    f32, bf16 = jnp.float32, jnp.bfloat16

    def at(y_there, z_there):
        return {"seq": y_there * z_count + z_there}

    right, left = (z + 1) % z_count, (z + z_count - 1) % z_count
    y_peers = [(y + step) % y_count for step in range(1, y_count)]
    z_peers = [(z + step) % z_count for step in range(1, z_count)]
    dp_peers = [(dp + step) % dp_count for step in range(1, dp_count)]
    peers = [at(other, z) for other in y_peers] + [at(y, other) for other in z_peers]
    peers += [{"dp": other} for other in dp_peers]
    greet(peers)

    def wide(ref, g):
        return ref.at[:, pl.ds(pl.multiple_of(g * WIDE, WIDE), WIDE)]

    def narrow(ref, g):
        return ref.at[:, pl.ds(pl.multiple_of(g * HD, HD), HD)]

    own = [pltpu.make_async_copy(dq_in.at[y], wide(dq_out, y), own_sem.at[0])]
    own[0].start()
    pl.semaphore_wait(pltpu.get_barrier_semaphore(), len(peers))

    plan = ring_plan(z_count)
    mine = (dk_in, dv_in)

    def ring_copy(lane, step):
        array, way, steps = plan[lane]
        block = (z + way * (steps - step) + z_count) % z_count
        there = at(y, right if way == 1 else left)
        source = mine[array].at[block] if step == 0 else held.at[lane, step - 1]
        return remote(source, held.at[lane, step], ring_send.at[lane, step], ring_recv.at[lane, step], there)

    def forward(step):
        for lane, (array, way, steps) in enumerate(plan):
            if step < steps:
                if step > 0:
                    ring_copy(lane, step - 1).wait_recv()
                    block = (z + way * (steps - step) + z_count) % z_count
                    for g in range(y_count):
                        total = held[lane, step - 1, g].astype(f32) + mine[array][block, g].astype(f32)
                        held[lane, step - 1, g] = total.astype(bf16)
                ring_copy(lane, step).start()

    forward(0)
    sends = []
    for i, other in enumerate(y_peers):
        sends.append(remote(dq_in.at[other], wide(dq_out, y), q_send.at[i], q_recv.at[i], at(other, z)))
        sends[-1].start()

    def share(first, source_of, held_ref, peers_there, me):
        copies = []
        for i, there in enumerate(peers_there):
            copies.append(remote(source_of(i), held_ref.at[me], r_send.at[first + i], r_recv.at[first + i], there))
            copies[-1].start()
        return copies

    over_dp = share(0, lambda i: part.at[dp_peers[i]], dp_held, [{"dp": other} for other in dp_peers], dp)
    forward(1)
    for copy in over_dp:
        copy.wait()
    total = part[dp]
    for other in dp_peers:
        total = total + dp_held[other]
    dp_sum[...] = total
    over_y = share(dp_count - 1, lambda i: dp_sum, y_held, [at(other, z) for other in y_peers], y)
    forward(2)
    for copy in over_y:
        copy.wait()
    for other in y_peers:
        total = total + y_held[other]
    y_sum[...] = total
    over_z = share(
        dp_count + y_count - 2, lambda i: y_sum, z_held, [at(y, other) for other in z_peers], z
    )
    for step in range(3, max(p[2] for p in plan)):
        forward(step)
    for copy in over_z:
        copy.wait()
    for other in z_peers:
        total = total + z_held[other]
    router_out[...] = total

    ends = []
    for array, target in ((0, dk_out), (1, dv_out)):
        lanes = [lane for lane in range(4) if plan[lane][0] == array]
        for lane in lanes:
            ring_copy(lane, plan[lane][2] - 1).wait_recv()
        for g in range(y_count):
            total = mine[array][z, g].astype(f32)
            for lane in lanes:
                total = total + held[lane, plan[lane][2] - 1, g].astype(f32)
            fin[array, g] = total.astype(bf16)
        for i, other in enumerate(y_peers):
            ends.append(
                remote(
                    fin.at[array, other],
                    narrow(target, y),
                    fin_send.at[array, i],
                    fin_recv.at[array, i],
                    at(other, z),
                )
            )
            ends[-1].start()
        own.append(pltpu.make_async_copy(fin.at[array, y], narrow(target, y), own_sem.at[1 + array]))
        own[-1].start()
    for lane, (array, way, steps) in enumerate(plan):
        for step in range(steps):
            ring_copy(lane, step).wait_send()
    for copy in own + sends + ends:
        copy.wait()


def scatter(y_count, z_count, dp_count, dq_in, dk_in, dv_in, part):
    cap = dq_in.shape[1]
    longer = z_count // 2
    small = part.shape[1:]
    anywhere = pl.BlockSpec(memory_space=pl.ANY)
    vmem = pl.BlockSpec(memory_space=pltpu.VMEM)
    bf16, f32 = jnp.bfloat16, jnp.float32
    shape = jax.ShapeDtypeStruct
    router_copies = dp_count + y_count + z_count - 3
    return pl.pallas_call(
        functools.partial(scatter_kernel, y_count, z_count, dp_count),
        out_shape=(
            shape((cap, HEADS * HD), bf16),
            shape((cap, KV * HD), bf16),
            shape((cap, KV * HD), bf16),
            shape(small, f32),
        ),
        in_specs=[anywhere, vmem, vmem, vmem],
        out_specs=(anywhere, anywhere, anywhere, vmem),
        scratch_shapes=[
            pltpu.VMEM((4, longer, y_count, cap, HD), bf16),
            pltpu.VMEM((2, y_count, cap, HD), bf16),
            pltpu.VMEM((dp_count,) + small, f32),
            pltpu.VMEM((y_count,) + small, f32),
            pltpu.VMEM((z_count,) + small, f32),
            pltpu.VMEM(small, f32),
            pltpu.VMEM(small, f32),
            pltpu.SemaphoreType.DMA((3,)),
            pltpu.SemaphoreType.DMA((y_count - 1,)),
            pltpu.SemaphoreType.DMA((y_count - 1,)),
            pltpu.SemaphoreType.DMA((4, longer)),
            pltpu.SemaphoreType.DMA((4, longer)),
            pltpu.SemaphoreType.DMA((2, y_count - 1)),
            pltpu.SemaphoreType.DMA((2, y_count - 1)),
            pltpu.SemaphoreType.DMA((router_copies,)),
            pltpu.SemaphoreType.DMA((router_copies,)),
        ],
        compiler_params=pltpu.CompilerParams(
            collective_id=1, has_side_effects=True, vmem_limit_bytes=32 * MIB
        ),
        name="scatter",
    )(dq_in, dk_in, dv_in, part)


def on_device(tokens, router_weight, routes, counts, query, key_in, value_in, attn_out, grad_out):
    y_count = KV
    z_count = lax.axis_size("seq") // y_count
    dp_count = lax.axis_size("dp")
    width = tokens.shape[2]
    q_all, do_all, de_all, k_all, v_all, c_all, part = gather(
        y_count, z_count, dp_count, tokens[0], router_weight[None], routes, counts,
        query[0], key_in[0], value_in[0], attn_out[0], grad_out[0],
    )
    dq, dk, dv = attention(y_count, z_count, c_all, q_all, do_all, de_all, k_all, v_all)
    dq, dk, dv, router = scatter(y_count, z_count, dp_count, dq, dk, dv, part)
    share = width // (dp_count * y_count * z_count)
    router = lax.dynamic_slice(router.reshape(-1), (lax.axis_index("seq") * share,), (share,))
    return (dq[None], dk[None], dv[None], router)


def solution(mesh):
    rows = P("dp", "seq", None)
    return jax.shard_map(
        on_device,
        mesh=mesh,
        in_specs=(rows, P(), P("dp", "seq"), P("dp", "seq"), rows, rows, rows, rows, rows),
        out_specs=(rows, rows, rows, P(("dp", "seq"))),
        check_vma=False,
    )
```

```python
import functools
import math

import jax
import jax.numpy as jnp
from jax import lax
from jax.experimental import pallas as pl
from jax.experimental.pallas import tpu as pltpu
from jax.sharding import PartitionSpec as P

HEADS = 32
KV = 4
HD = 128
GROUP = HEADS // KV
WIDE = GROUP * HD
KEEP = 2048
SUB_LANES = 128
NEGATIVE = -1e30
MESH = pl.DeviceIdType.MESH
MIB = 1024 * 1024


def place(z_count):
    me = lax.axis_index("seq")
    return me // z_count, me % z_count


def remote(src, dst, send_sem, recv_sem, device):
    return pltpu.make_async_remote_copy(
        src_ref=src,
        dst_ref=dst,
        send_sem=send_sem,
        recv_sem=recv_sem,
        device_id=device,
        device_id_type=MESH,
    )


def greet(devices):
    barrier = pltpu.get_barrier_semaphore()
    for device in devices:
        pl.semaphore_signal(barrier, inc=1, device_id=device, device_id_type=MESH)


def ring_plan(z_count):
    longer = z_count // 2
    shorter = z_count - 1 - longer
    return ((0, 1, longer), (1, -1, longer), (1, 1, shorter), (0, -1, shorter))


def gather_kernel(
    y_count, z_count, chunks,
    tokens, weight, routes, counts, query, key_in, value_in, attn_out, grad_out,
    q_all, do_all, de_all, k_all, v_all, c_all, part,
    tok_v, cot_v, attn_v, dout_v, de_v, cnt_v, picked_v,
    tok_sem, in_sem, own_sem, y_send, y_recv, ring_send, ring_recv, c_send, c_recv,
):
    y, z = place(z_count)
    cap = query.shape[0]
    tok_count = tokens.shape[0]
    chunk = tokens.shape[1] // chunks

    def at(y_there, z_there):
        return {"seq": y_there * z_count + z_there}

    right, left = (z + 1) % z_count, (z + z_count - 1) % z_count
    y_peers = [(y + step) % y_count for step in range(1, y_count)]
    greet([at(other, z) for other in y_peers] + [at(y, right), at(y, left)])

    loads = []
    for c in range(chunks):
        loads.append(pltpu.make_async_copy(tokens.at[:, pl.ds(c * chunk, chunk)], tok_v.at[c], tok_sem.at[c]))
        loads[-1].start()
    rows_in = []
    for g in range(y_count):
        for a, (source, target) in enumerate(((grad_out, cot_v), (attn_out, attn_v))):
            rows_in.append(
                pltpu.make_async_copy(source.at[:, pl.ds(g * WIDE, WIDE)], target.at[g], in_sem.at[a, g])
            )
            rows_in[-1].start()
    cnt_v[...] = jnp.full(cnt_v.shape, counts[0, 0], jnp.int32)

    def wide(ref, g):
        return ref.at[:, pl.ds(pl.multiple_of(g * WIDE, WIDE), WIDE)]

    def narrow(ref, g):
        return ref.at[:, pl.ds(pl.multiple_of(g * HD, HD), HD)]

    own = [
        pltpu.make_async_copy(narrow(key_in, y), k_all.at[z, y], own_sem.at[0]),
        pltpu.make_async_copy(narrow(value_in, y), v_all.at[z, y], own_sem.at[1]),
        pltpu.make_async_copy(cnt_v, c_all.at[z, y], own_sem.at[2]),
        pltpu.make_async_copy(wide(query, y), q_all.at[y], own_sem.at[3]),
    ]
    for copy in own:
        copy.start()
    pl.semaphore_wait(pltpu.get_barrier_semaphore(), y_count + 1)

    first = []
    for i, other in enumerate(y_peers):
        there = at(other, z)
        for a, (source, target) in enumerate(
            (
                (narrow(key_in, other), k_all.at[z, y]),
                (narrow(value_in, other), v_all.at[z, y]),
                (cnt_v, c_all.at[z, y]),
            )
        ):
            first.append(remote(source, target, y_send.at[a, i], y_recv.at[a, i], there))
            first[-1].start()
    late = []
    for i, other in enumerate(y_peers):
        late.append(remote(wide(query, other), q_all.at[y], y_send.at[3, i], y_recv.at[3, i], at(other, z)))
        late[-1].start()
    for copy in own[:3]:
        copy.wait()
    for copy in first:
        copy.wait_recv()

    plan = ring_plan(z_count)
    held = (k_all, v_all)

    def ring_copy(lane, step):
        array, way, _ = plan[lane]
        block = (z - way * step + 2 * z_count) % z_count
        there = at(y, right if way == 1 else left)
        ref = held[array].at[block]
        return remote(ref, ref, ring_send.at[lane, step], ring_recv.at[lane, step], there)

    def count_copy(way, step):
        block = (z - way * step + 2 * z_count) % z_count
        there = at(y, right if way == 1 else left)
        ref = c_all.at[block]
        side = (1 - way) // 2
        return remote(ref, ref, c_send.at[side, step], c_recv.at[side, step], there)

    def forward(step):
        for lane, (array, way, steps) in enumerate(plan):
            if 0 < step <= steps:
                ring_copy(lane, step - 1).wait_recv()
            if step < steps:
                ring_copy(lane, step).start()
            if array == 0:
                if 0 < step <= steps:
                    count_copy(way, step - 1).wait_recv()
                if step < steps:
                    count_copy(way, step).start()

    forward(0)

    token_at = lax.broadcasted_iota(jnp.int32, (tok_count, cap), 0)
    hot = jnp.where(token_at == routes[...], 1.0, 0.0).T.astype(jnp.bfloat16)
    logit = jnp.zeros((cap, HD), jnp.float32)
    for c in range(chunks):
        loads[c].wait()
        picked = jnp.dot(hot, tok_v[c], preferred_element_type=jnp.float32)
        picked_v[c] = picked
        scaled = picked * weight[:, c * chunk : (c + 1) * chunk]
        for t in range(chunk // HD):
            logit = logit + scaled[:, t * HD : (t + 1) * HD]
    logit = jnp.sum(logit, axis=1, keepdims=True)
    gate = 1.0 / (1.0 + jnp.exp(-logit))
    live = lax.broadcasted_iota(jnp.int32, (cap, 1), 0) < counts[0, 0]
    kept = jnp.where(live, gate, 0.0)
    for copy in rows_in:
        copy.wait()

    lane_at = lax.broadcasted_iota(jnp.int32, (cap, HD), 1)

    def scale_group(other):
        gate_sum = jnp.zeros((cap, HD), jnp.float32)
        deltas = jnp.zeros((cap, HD), jnp.float32)
        for h in range(GROUP):
            cols = slice(h * HD, (h + 1) * HD)
            cot = cot_v[other, :, cols].astype(jnp.float32)
            out = attn_v[other, :, cols].astype(jnp.float32)
            dout = (kept * cot).astype(jnp.bfloat16)
            dout_v[other, :, cols] = dout
            gate_sum = gate_sum + cot * out
            delta = jnp.sum(dout.astype(jnp.float32) * out, axis=1, keepdims=True)
            deltas = jnp.where(lane_at == h, delta, deltas)
        de_v[other] = deltas.T[:GROUP]
        return gate_sum

    gate_sum = jnp.zeros((cap, HD), jnp.float32)
    for i, other in enumerate(y_peers):
        gate_sum = gate_sum + scale_group(other)
        for a, (source, target) in enumerate(((dout_v, do_all), (de_v, de_all))):
            late.append(
                remote(source.at[other], target.at[y], y_send.at[4 + a, i], y_recv.at[4 + a, i], at(other, z))
            )
            late[-1].start()
    forward(1)
    gate_sum = gate_sum + scale_group(y)
    mine = [
        pltpu.make_async_copy(dout_v.at[y], do_all.at[y], own_sem.at[4]),
        pltpu.make_async_copy(de_v.at[y], de_all.at[y], own_sem.at[5]),
    ]
    for copy in mine:
        copy.start()
    forward(2)
    gate_grad = jnp.sum(gate_sum, axis=1, keepdims=True)
    logit_grad = jnp.where(live, gate_grad * gate * (1.0 - gate), 0.0)
    segments = part.shape[1]
    for c in range(chunks):
        terms = jnp.sum(logit_grad * picked_v[c], axis=0, keepdims=True)
        for t in range(chunk // HD):
            n = c * (chunk // HD) + t
            part[n // segments, n % segments : n % segments + 1, :] = terms[:, t * HD : (t + 1) * HD]
    for step in range(3, max(p[2] for p in plan) + 1):
        forward(step)
    own[3].wait()
    for copy in mine:
        copy.wait()
    for copy in first:
        copy.wait_send()
    for copy in late:
        copy.wait()
    for lane, (array, way, steps) in enumerate(plan):
        for step in range(steps):
            ring_copy(lane, step).wait_send()
            if array == 0:
                count_copy(way, step).wait_send()


def gather(y_count, z_count, dp_count, tokens, weight, routes, counts, query, key_in, value_in, attn_out, grad_out):
    cap = query.shape[0]
    tok_count, width = tokens.shape
    chunks = 5
    longer = z_count // 2
    anywhere = pl.BlockSpec(memory_space=pl.ANY)
    vmem = pl.BlockSpec(memory_space=pltpu.VMEM)
    smem = pl.BlockSpec(memory_space=pltpu.SMEM)
    bf16, f32 = jnp.bfloat16, jnp.float32
    shape = jax.ShapeDtypeStruct
    return pl.pallas_call(
        functools.partial(gather_kernel, y_count, z_count, chunks),
        out_shape=(
            shape((y_count, cap, WIDE), bf16),
            shape((y_count, cap, WIDE), bf16),
            shape((y_count, GROUP, cap), f32),
            shape((z_count, y_count, cap, HD), bf16),
            shape((z_count, y_count, cap, HD), bf16),
            shape((z_count, y_count, 1, HD), jnp.int32),
            shape((dp_count, width // HD // dp_count, HD), f32),
        ),
        in_specs=[anywhere, vmem, vmem, smem] + [anywhere] * 5,
        out_specs=(anywhere,) * 6 + (vmem,),
        scratch_shapes=[
            pltpu.VMEM((chunks, tok_count, width // chunks), bf16),
            pltpu.VMEM((y_count, cap, WIDE), bf16),
            pltpu.VMEM((y_count, cap, WIDE), bf16),
            pltpu.VMEM((y_count, cap, WIDE), bf16),
            pltpu.VMEM((y_count, GROUP, cap), f32),
            pltpu.VMEM((1, HD), jnp.int32),
            pltpu.VMEM((chunks, cap, width // chunks), f32),
            pltpu.SemaphoreType.DMA((chunks,)),
            pltpu.SemaphoreType.DMA((2, y_count)),
            pltpu.SemaphoreType.DMA((6,)),
            pltpu.SemaphoreType.DMA((6, y_count - 1)),
            pltpu.SemaphoreType.DMA((6, y_count - 1)),
            pltpu.SemaphoreType.DMA((4, longer)),
            pltpu.SemaphoreType.DMA((4, longer)),
            pltpu.SemaphoreType.DMA((2, longer)),
            pltpu.SemaphoreType.DMA((2, longer)),
        ],
        compiler_params=pltpu.CompilerParams(
            collective_id=0, has_side_effects=True, vmem_limit_bytes=63 * MIB
        ),
        name="gather",
    )(tokens, weight, routes, counts, query, key_in, value_in, attn_out, grad_out)


def attention_kernel(
    y_count, z_count, block_rows, block_keys,
    counts, q_in, do_in, de_in, k_in, v_in,
    dq_out, dk_out, dv_out,
    row_f, do_f, de_f, q_b, do_b, de_b, k_f, v_f, k_b, kt_b, v_b, exps, tops, best, total, dk_f, dv_f, dq_f,
    s_even, s_odd, p_even, p_odd, ds_even, ds_odd, pair_row, pair_key, shard_start,
):
    cap = q_in.shape[1]
    z = lax.axis_index("seq") % z_count
    shard_count = y_count * z_count
    lanes = GROUP * block_rows
    key_blocks = KEEP // block_keys
    root = 1.0 / math.sqrt(HD)
    power = root * math.log2(math.e)
    f32, bf16 = jnp.float32, jnp.bfloat16
    s_b, p_b, ds_b = (s_even, s_odd), (p_even, p_odd), (ds_even, ds_odd)

    def count_of(shard):
        return counts[shard % z_count, shard // z_count, 0, 0]

    def add_counts(shard, offset):
        shard_start[shard] = offset
        return offset + count_of(shard)

    lax.fori_loop(0, shard_count, add_counts, jnp.int32(0))

    def pack_keys(step, carry):
        for more in range(4):
            shard = step * 4 + more
            zz, yy = shard % z_count, shard // z_count
            rows = pl.ds(shard_start[shard], cap)
            k_f[rows, :] = k_in[zz, yy].astype(f32)
            v_f[rows, :] = v_in[zz, yy].astype(f32)
        return carry

    lax.fori_loop(0, shard_count // 4, pack_keys, 0)

    def narrow_keys(b, carry):
        rows = pl.ds(b * block_keys, block_keys)
        k_b[b] = k_f[rows, :].astype(bf16)
        kt_b[b] = k_f[rows, :].T.astype(bf16)
        v_b[b] = v_f[rows, :].astype(bf16)
        dk_f[b] = jnp.zeros((block_keys, HD), f32)
        dv_f[b] = jnp.zeros((block_keys, HD), f32)
        return carry

    lax.fori_loop(0, key_blocks, narrow_keys, 0)

    row_start, shift, live = [], [], []
    rows_here = 0
    for yy in range(y_count):
        row_start.append(rows_here)
        shift.append(shard_start[yy * z_count + z] - rows_here)
        live.append(counts[z, yy, 0, 0])
        rows_here = rows_here + live[yy]

    def place_of(row):
        found = row + shift[0]
        for yy in range(1, y_count):
            found = jnp.where(row >= row_start[yy], row + shift[yy], found)
        return found

    for yy in range(y_count):
        rows = pl.ds(row_start[yy], cap)
        for h in range(GROUP):
            cols = slice(h * HD, (h + 1) * HD)
            row_f[h, rows, :] = q_in[yy, :, cols].astype(f32)
            do_f[h, rows, :] = do_in[yy, :, cols].astype(f32)
        padded = jnp.concatenate([de_in[yy], jnp.zeros((HD - GROUP, cap), f32)], axis=0)
        de_f[rows, :] = padded.T
    tail = pl.ds(rows_here, block_rows)
    for h in range(GROUP):
        row_f[h, tail, :] = jnp.zeros((block_rows, HD), f32)
        do_f[h, tail, :] = jnp.zeros((block_rows, HD), f32)
    de_f[tail, :] = jnp.zeros((block_rows, HD), f32)

    row_blocks = (rows_here + block_rows - 1) // block_rows

    def narrow_rows(b, carry):
        rows = pl.ds(pl.multiple_of(b * block_rows, block_rows), block_rows)
        across = de_f[rows, :].T
        for h in range(GROUP):
            mine = slice(h * block_rows, (h + 1) * block_rows)
            q_b[b, mine, :] = row_f[h, rows, :].astype(bf16)
            do_b[b, mine, :] = do_f[h, rows, :].astype(bf16)
            de_b[b, :, mine] = across[h : h + 1, :]
        return carry

    lax.fori_loop(0, row_blocks, narrow_rows, 0)

    nt = (((1,), (1,)), ((), ()))

    def list_pairs(masked, count):
        def of_rows(b, count):
            full = (place_of(b * block_rows) + 1) // block_keys
            used = place_of(jnp.minimum((b + 1) * block_rows, rows_here) - 1) // block_keys + 1

            def add(kb, count):
                pair_row[count] = b
                pair_key[count] = kb
                return count + 1

            first, last = (full, used) if masked else (0, full)
            return lax.fori_loop(first, last, add, count)

        return lax.fori_loop(0, row_blocks, of_rows, count)

    whole_pairs = list_pairs(False, jnp.int32(0))
    pairs = list_pairs(True, whole_pairs)
    for more in range(3):
        pair_row[pairs + more] = q_b.shape[0] - 1
        pair_key[pairs + more] = 0

    def start_rows(b, carry):
        best[b] = jnp.full((8, lanes), NEGATIVE, f32)
        total[b] = jnp.zeros((8, lanes), f32)
        dq_f[b] = jnp.zeros((HD, lanes), f32)
        return carry

    lax.fori_loop(0, row_blocks, start_rows, 0)

    def raw(n, slot):
        s_b[slot][:, :] = lax.dot_general(
            k_b[pair_key[n]], q_b[pair_row[n]], nt, preferred_element_type=f32
        )

    def grow(masked, n, slot):
        b, kb = pair_row[n], pair_key[n]
        for part in range(lanes // SUB_LANES):
            cols = slice(part * SUB_LANES, (part + 1) * SUB_LANES)
            block = s_b[slot][:, cols] * power
            if masked:
                lane = lax.broadcasted_iota(jnp.int32, (1, SUB_LANES), 1)
                row_place = place_of(b * block_rows + lane % block_rows) - kb * block_keys
                key_place = lax.broadcasted_iota(jnp.int32, (block_keys, SUB_LANES), 0)
                block = jnp.where(key_place <= row_place, block, NEGATIVE)
            block = block.reshape(block_keys // 8, 8, SUB_LANES)
            before = best[b, :, cols]
            after = jnp.maximum(before, jnp.max(block, axis=0))
            grown = jnp.exp2(block - after)
            exps[n, :, :, cols] = grown
            tops[n, :, cols] = after
            best[b, :, cols] = after
            total[b, :, cols] = total[b, :, cols] * jnp.exp2(before - after) + jnp.sum(grown, axis=0)

    def two_scores(masked, j, carry):
        n = 2 * j
        raw(n + 1, 1)
        grow(masked, n, 0)
        raw(n + 2, 0)
        grow(masked, n + 1, 1)
        return carry

    raw(0, 0)
    lax.fori_loop(0, whole_pairs // 2, functools.partial(two_scores, False), 0)
    lax.fori_loop(whole_pairs // 2, (pairs + 1) // 2, functools.partial(two_scores, True), 0)

    def finish_rows(b, carry):
        top = jnp.max(best[b], axis=0, keepdims=True)
        summed = jnp.sum(total[b] * jnp.exp2(best[b] - top), axis=0, keepdims=True)
        best[b] = jnp.broadcast_to(top + jnp.log2(summed), (8, lanes))
        return carry

    lax.fori_loop(0, row_blocks, finish_rows, 0)

    def terms(n, slot):
        b, kb = pair_row[n], pair_key[n]
        scale = jnp.exp2(tops[n] - best[b])
        prob = (exps[n] * scale).reshape(block_keys, lanes)
        prob_grad = lax.dot_general(v_b[kb], do_b[b], nt, preferred_element_type=f32)
        p_b[slot][:, :] = prob.astype(bf16)
        ds_b[slot][:, :] = (prob * (prob_grad - de_b[b])).astype(bf16)

    def products(n, slot):
        b, kb = pair_row[n], pair_key[n]
        score_grad = ds_b[slot][:, :]
        dv_f[kb] += jnp.dot(p_b[slot][:, :], do_b[b], preferred_element_type=f32)
        dk_f[kb] += jnp.dot(score_grad, q_b[b], preferred_element_type=f32)
        dq_f[b] += jnp.dot(kt_b[kb], score_grad, preferred_element_type=f32)

    def two_pairs(j, carry):
        n = 2 * j
        products(n, 0)
        terms(n + 1, 1)
        products(n + 1, 1)
        terms(n + 2, 0)
        return carry

    @pl.when(pairs > 0)
    def _():
        terms(0, 0)

    lax.fori_loop(0, pairs // 2, two_pairs, 0)

    @pl.when(pairs % 2 == 1)
    def _():
        products(pairs - 1, 0)

    def turn_rows(b, carry):
        rows = pl.ds(pl.multiple_of(b * block_rows, block_rows), block_rows)
        turned = dq_f[b].T * root
        for h in range(GROUP):
            row_f[h, rows, :] = turned[h * block_rows : (h + 1) * block_rows, :]
        return carry

    lax.fori_loop(0, row_blocks, turn_rows, 0)

    slot = lax.broadcasted_iota(jnp.int32, (cap, 1), 0)
    for yy in range(y_count):
        rows = pl.ds(row_start[yy], cap)
        for h in range(GROUP):
            grad = jnp.where(slot < live[yy], row_f[h, rows, :], 0.0)
            dq_out[yy, :, h * HD : (h + 1) * HD] = grad.astype(bf16)

    def widen_keys(b, carry):
        rows = pl.ds(pl.multiple_of(b * block_keys, block_keys), block_keys)
        k_f[rows, :] = dk_f[b] * root
        v_f[rows, :] = dv_f[b]
        return carry

    lax.fori_loop(0, key_blocks, widen_keys, 0)

    def unpack_keys(step, carry):
        for more in range(4):
            shard = step * 4 + more
            zz, yy = shard % z_count, shard // z_count
            rows = pl.ds(shard_start[shard], cap)
            held = slot < count_of(shard)
            dk_out[zz, yy] = jnp.where(held, k_f[rows, :], 0.0).astype(bf16)
            dv_out[zz, yy] = jnp.where(held, v_f[rows, :], 0.0).astype(bf16)
        return carry

    lax.fori_loop(0, shard_count // 4, unpack_keys, 0)


def attention(y_count, z_count, counts, q_in, do_in, de_in, k_in, v_in):
    cap = q_in.shape[1]
    block_rows, block_keys = 64, 256
    lanes = GROUP * block_rows
    most = y_count * cap
    row_blocks = most // block_rows
    key_blocks = KEEP // block_keys
    vmem = pl.BlockSpec(memory_space=pltpu.VMEM)
    bf16, f32 = jnp.bfloat16, jnp.float32
    shape = jax.ShapeDtypeStruct
    return pl.pallas_call(
        functools.partial(attention_kernel, y_count, z_count, block_rows, block_keys),
        out_shape=(
            shape((y_count, cap, WIDE), bf16),
            shape((z_count, y_count, cap, HD), bf16),
            shape((z_count, y_count, cap, HD), bf16),
        ),
        in_specs=[pl.BlockSpec(memory_space=pltpu.SMEM)] + [vmem] * 5,
        out_specs=(vmem,) * 3,
        scratch_shapes=[
            pltpu.VMEM((GROUP, most + cap, HD), f32),
            pltpu.VMEM((GROUP, most + cap, HD), f32),
            pltpu.VMEM((most + cap, HD), f32),
            pltpu.VMEM((row_blocks + 1, lanes, HD), bf16),
            pltpu.VMEM((row_blocks + 1, lanes, HD), bf16),
            pltpu.VMEM((row_blocks + 1, 1, lanes), f32),
            pltpu.VMEM((KEEP + cap, HD), f32),
            pltpu.VMEM((KEEP + cap, HD), f32),
            pltpu.VMEM((key_blocks, block_keys, HD), bf16),
            pltpu.VMEM((key_blocks, HD, block_keys), bf16),
            pltpu.VMEM((key_blocks, block_keys, HD), bf16),
            pltpu.VMEM((row_blocks * key_blocks + 1, block_keys // 8, 8, lanes), f32),
            pltpu.VMEM((row_blocks * key_blocks + 1, 8, lanes), f32),
            pltpu.VMEM((row_blocks + 1, 8, lanes), f32),
            pltpu.VMEM((row_blocks + 1, 8, lanes), f32),
            pltpu.VMEM((key_blocks, block_keys, HD), f32),
            pltpu.VMEM((key_blocks, block_keys, HD), f32),
            pltpu.VMEM((row_blocks, HD, lanes), f32),
            pltpu.VMEM((block_keys, lanes), f32),
            pltpu.VMEM((block_keys, lanes), f32),
            pltpu.VMEM((block_keys, lanes), bf16),
            pltpu.VMEM((block_keys, lanes), bf16),
            pltpu.VMEM((block_keys, lanes), bf16),
            pltpu.VMEM((block_keys, lanes), bf16),
            pltpu.SMEM((row_blocks * key_blocks + 3,), jnp.int32),
            pltpu.SMEM((row_blocks * key_blocks + 3,), jnp.int32),
            pltpu.SMEM((y_count * z_count,), jnp.int32),
        ],
        compiler_params=pltpu.CompilerParams(vmem_limit_bytes=62 * MIB),
        name="attention",
    )(counts, q_in, do_in, de_in, k_in, v_in)


def scatter_kernel(
    y_count, z_count, dp_count,
    dq_in, dk_in, dv_in, part,
    dq_out, dk_out, dv_out, router_out,
    held, fin, dp_held, y_held, z_held, dp_sum, y_sum,
    own_sem, q_send, q_recv, ring_send, ring_recv, fin_send, fin_recv, r_send, r_recv,
):
    y, z = place(z_count)
    dp = lax.axis_index("dp")
    f32, bf16 = jnp.float32, jnp.bfloat16

    def at(y_there, z_there):
        return {"seq": y_there * z_count + z_there}

    right, left = (z + 1) % z_count, (z + z_count - 1) % z_count
    y_peers = [(y + step) % y_count for step in range(1, y_count)]
    z_peers = [(z + step) % z_count for step in range(1, z_count)]
    dp_peers = [(dp + step) % dp_count for step in range(1, dp_count)]
    peers = [at(other, z) for other in y_peers] + [at(y, other) for other in z_peers]
    peers += [{"dp": other} for other in dp_peers]
    greet(peers)

    def wide(ref, g):
        return ref.at[:, pl.ds(pl.multiple_of(g * WIDE, WIDE), WIDE)]

    def narrow(ref, g):
        return ref.at[:, pl.ds(pl.multiple_of(g * HD, HD), HD)]

    own = [pltpu.make_async_copy(dq_in.at[y], wide(dq_out, y), own_sem.at[0])]
    own[0].start()
    pl.semaphore_wait(pltpu.get_barrier_semaphore(), len(peers))

    plan = ring_plan(z_count)
    mine = (dk_in, dv_in)

    def ring_copy(lane, step):
        array, way, steps = plan[lane]
        block = (z + way * (steps - step) + z_count) % z_count
        there = at(y, right if way == 1 else left)
        source = mine[array].at[block] if step == 0 else held.at[lane, step - 1]
        return remote(source, held.at[lane, step], ring_send.at[lane, step], ring_recv.at[lane, step], there)

    def forward(step):
        for lane, (array, way, steps) in enumerate(plan):
            if step < steps:
                if step > 0:
                    ring_copy(lane, step - 1).wait_recv()
                    block = (z + way * (steps - step) + z_count) % z_count
                    for g in range(y_count):
                        total = held[lane, step - 1, g].astype(f32) + mine[array][block, g].astype(f32)
                        held[lane, step - 1, g] = total.astype(bf16)
                ring_copy(lane, step).start()

    forward(0)
    sends = []
    for i, other in enumerate(y_peers):
        sends.append(remote(dq_in.at[other], wide(dq_out, y), q_send.at[i], q_recv.at[i], at(other, z)))
        sends[-1].start()

    def share(first, source_of, held_ref, peers_there, me):
        copies = []
        for i, there in enumerate(peers_there):
            copies.append(remote(source_of(i), held_ref.at[me], r_send.at[first + i], r_recv.at[first + i], there))
            copies[-1].start()
        return copies

    over_dp = share(0, lambda i: part.at[dp_peers[i]], dp_held, [{"dp": other} for other in dp_peers], dp)
    forward(1)
    for copy in over_dp:
        copy.wait()
    total = part[dp]
    for other in dp_peers:
        total = total + dp_held[other]
    dp_sum[...] = total
    over_y = share(dp_count - 1, lambda i: dp_sum, y_held, [at(other, z) for other in y_peers], y)
    forward(2)
    for copy in over_y:
        copy.wait()
    for other in y_peers:
        total = total + y_held[other]
    y_sum[...] = total
    over_z = share(
        dp_count + y_count - 2, lambda i: y_sum, z_held, [at(y, other) for other in z_peers], z
    )
    for step in range(3, max(p[2] for p in plan)):
        forward(step)
    for copy in over_z:
        copy.wait()
    for other in z_peers:
        total = total + z_held[other]
    router_out[...] = total

    ends = []
    for array, target in ((0, dk_out), (1, dv_out)):
        lanes = [lane for lane in range(4) if plan[lane][0] == array]
        for lane in lanes:
            ring_copy(lane, plan[lane][2] - 1).wait_recv()
        for g in range(y_count):
            total = mine[array][z, g].astype(f32)
            for lane in lanes:
                total = total + held[lane, plan[lane][2] - 1, g].astype(f32)
            fin[array, g] = total.astype(bf16)
        for i, other in enumerate(y_peers):
            ends.append(
                remote(
                    fin.at[array, other],
                    narrow(target, y),
                    fin_send.at[array, i],
                    fin_recv.at[array, i],
                    at(other, z),
                )
            )
            ends[-1].start()
        own.append(pltpu.make_async_copy(fin.at[array, y], narrow(target, y), own_sem.at[1 + array]))
        own[-1].start()
    for lane, (array, way, steps) in enumerate(plan):
        for step in range(steps):
            ring_copy(lane, step).wait_send()
    for copy in own + sends + ends:
        copy.wait()


def scatter(y_count, z_count, dp_count, dq_in, dk_in, dv_in, part):
    cap = dq_in.shape[1]
    longer = z_count // 2
    small = part.shape[1:]
    anywhere = pl.BlockSpec(memory_space=pl.ANY)
    vmem = pl.BlockSpec(memory_space=pltpu.VMEM)
    bf16, f32 = jnp.bfloat16, jnp.float32
    shape = jax.ShapeDtypeStruct
    router_copies = dp_count + y_count + z_count - 3
    return pl.pallas_call(
        functools.partial(scatter_kernel, y_count, z_count, dp_count),
        out_shape=(
            shape((cap, HEADS * HD), bf16),
            shape((cap, KV * HD), bf16),
            shape((cap, KV * HD), bf16),
            shape(small, f32),
        ),
        in_specs=[anywhere, vmem, vmem, vmem],
        out_specs=(anywhere, anywhere, anywhere, vmem),
        scratch_shapes=[
            pltpu.VMEM((4, longer, y_count, cap, HD), bf16),
            pltpu.VMEM((2, y_count, cap, HD), bf16),
            pltpu.VMEM((dp_count,) + small, f32),
            pltpu.VMEM((y_count,) + small, f32),
            pltpu.VMEM((z_count,) + small, f32),
            pltpu.VMEM(small, f32),
            pltpu.VMEM(small, f32),
            pltpu.SemaphoreType.DMA((3,)),
            pltpu.SemaphoreType.DMA((y_count - 1,)),
            pltpu.SemaphoreType.DMA((y_count - 1,)),
            pltpu.SemaphoreType.DMA((4, longer)),
            pltpu.SemaphoreType.DMA((4, longer)),
            pltpu.SemaphoreType.DMA((2, y_count - 1)),
            pltpu.SemaphoreType.DMA((2, y_count - 1)),
            pltpu.SemaphoreType.DMA((router_copies,)),
            pltpu.SemaphoreType.DMA((router_copies,)),
        ],
        compiler_params=pltpu.CompilerParams(
            collective_id=1, has_side_effects=True, vmem_limit_bytes=32 * MIB
        ),
        name="scatter",
    )(dq_in, dk_in, dv_in, part)


def on_device(tokens, router_weight, routes, counts, query, key_in, value_in, attn_out, grad_out):
    y_count = KV
    z_count = lax.axis_size("seq") // y_count
    dp_count = lax.axis_size("dp")
    width = tokens.shape[2]
    q_all, do_all, de_all, k_all, v_all, c_all, part = gather(
        y_count, z_count, dp_count, tokens[0], router_weight[None], routes, counts,
        query[0], key_in[0], value_in[0], attn_out[0], grad_out[0],
    )
    dq, dk, dv = attention(y_count, z_count, c_all, q_all, do_all, de_all, k_all, v_all)
    dq, dk, dv, router = scatter(y_count, z_count, dp_count, dq, dk, dv, part)
    share = width // (dp_count * y_count * z_count)
    router = lax.dynamic_slice(router.reshape(-1), (lax.axis_index("seq") * share,), (share,))
    return (dq[None], dk[None], dv[None], router)


def solution(mesh):
    rows = P("dp", "seq", None)
    return jax.shard_map(
        on_device,
        mesh=mesh,
        in_specs=(rows, P(), P("dp", "seq"), P("dp", "seq"), rows, rows, rows, rows, rows),
        out_specs=(rows, rows, rows, P(("dp", "seq"))),
        check_vma=False,
    )
```

```python
import functools
import math

import jax
import jax.numpy as jnp
from jax import lax
from jax.experimental import pallas as pl
from jax.experimental.pallas import tpu as pltpu
from jax.sharding import PartitionSpec as P

HEADS = 32
KV = 4
HD = 128
GROUP = HEADS // KV
WIDE = GROUP * HD
KEEP = 2048
SUB_LANES = 128
DEEP = 4
NEGATIVE = -1e30
MESH = pl.DeviceIdType.MESH
MIB = 1024 * 1024


def place(z_count):
    me = lax.axis_index("seq")
    return me // z_count, me % z_count


def remote(src, dst, send_sem, recv_sem, device):
    return pltpu.make_async_remote_copy(
        src_ref=src,
        dst_ref=dst,
        send_sem=send_sem,
        recv_sem=recv_sem,
        device_id=device,
        device_id_type=MESH,
    )


def greet(devices):
    barrier = pltpu.get_barrier_semaphore()
    for device in devices:
        pl.semaphore_signal(barrier, inc=1, device_id=device, device_id_type=MESH)


def ring_plan(z_count):
    longer = z_count // 2
    shorter = z_count - 1 - longer
    return ((0, 1, longer), (1, -1, longer), (1, 1, shorter), (0, -1, shorter))


def gather_kernel(
    y_count, z_count, chunks,
    tokens, weight, routes, counts, query, key_in, value_in, attn_out, grad_out,
    q_all, do_all, de_all, k_all, v_all, c_all, part,
    tok_v, cot_v, attn_v, dout_v, de_v, cnt_v, picked_v, q_own, k_own, v_own,
    tok_sem, in_sem, own_sem, y_send, y_recv, ring_send, ring_recv, c_send, c_recv,
):
    y, z = place(z_count)
    cap = query.shape[0]
    tok_count = tokens.shape[0]
    chunk = tokens.shape[1] // chunks

    def at(y_there, z_there):
        return {"seq": y_there * z_count + z_there}

    right, left = (z + 1) % z_count, (z + z_count - 1) % z_count
    y_peers = [(y + step) % y_count for step in range(1, y_count)]
    greet([at(other, z) for other in y_peers] + [at(y, right), at(y, left)])

    cnt_v[...] = jnp.full(cnt_v.shape, counts[0, 0], jnp.int32)

    def wide(ref, g):
        return ref.at[:, pl.ds(pl.multiple_of(g * WIDE, WIDE), WIDE)]

    def narrow(ref, g):
        return ref.at[:, pl.ds(pl.multiple_of(g * HD, HD), HD)]

    own_in = [
        pltpu.make_async_copy(narrow(key_in, y), k_own, own_sem.at[0]),
        pltpu.make_async_copy(narrow(value_in, y), v_own, own_sem.at[1]),
        pltpu.make_async_copy(wide(query, y), q_own, own_sem.at[2]),
    ]
    for copy in own_in:
        copy.start()
    loads = []
    for c in range(chunks):
        loads.append(pltpu.make_async_copy(tokens.at[:, pl.ds(c * chunk, chunk)], tok_v.at[c], tok_sem.at[c]))
        loads[-1].start()
    rows_in = []
    for g in range(y_count):
        for a, (source, target) in enumerate(((grad_out, cot_v), (attn_out, attn_v))):
            rows_in.append(
                pltpu.make_async_copy(source.at[:, pl.ds(g * WIDE, WIDE)], target.at[g], in_sem.at[a, g])
            )
            rows_in[-1].start()
    for copy in own_in:
        copy.wait()
    own = [
        pltpu.make_async_copy(k_own, k_all.at[z, y], own_sem.at[0]),
        pltpu.make_async_copy(v_own, v_all.at[z, y], own_sem.at[1]),
        pltpu.make_async_copy(cnt_v, c_all.at[z, y], own_sem.at[3]),
        pltpu.make_async_copy(q_own, q_all.at[y], own_sem.at[2]),
    ]
    for copy in own:
        copy.start()
    pl.semaphore_wait(pltpu.get_barrier_semaphore(), y_count + 1)

    first = []
    for i, other in enumerate(y_peers):
        there = at(other, z)
        for a, (source, target) in enumerate(
            (
                (narrow(key_in, other), k_all.at[z, y]),
                (narrow(value_in, other), v_all.at[z, y]),
                (cnt_v, c_all.at[z, y]),
            )
        ):
            first.append(remote(source, target, y_send.at[a, i], y_recv.at[a, i], there))
            first[-1].start()
    late = []
    for i, other in enumerate(y_peers):
        late.append(remote(wide(query, other), q_all.at[y], y_send.at[3, i], y_recv.at[3, i], at(other, z)))
        late[-1].start()
    for copy in own[:3]:
        copy.wait()
    for copy in first:
        copy.wait_recv()

    plan = ring_plan(z_count)
    held = (k_all, v_all)

    def ring_copy(lane, step):
        array, way, _ = plan[lane]
        block = (z - way * step + 2 * z_count) % z_count
        there = at(y, right if way == 1 else left)
        ref = held[array].at[block]
        return remote(ref, ref, ring_send.at[lane, step], ring_recv.at[lane, step], there)

    def count_copy(way, step):
        block = (z - way * step + 2 * z_count) % z_count
        there = at(y, right if way == 1 else left)
        ref = c_all.at[block]
        side = (1 - way) // 2
        return remote(ref, ref, c_send.at[side, step], c_recv.at[side, step], there)

    def forward(step):
        for lane, (array, way, steps) in enumerate(plan):
            if 0 < step <= steps:
                ring_copy(lane, step - 1).wait_recv()
            if step < steps:
                ring_copy(lane, step).start()
            if array == 0:
                if 0 < step <= steps:
                    count_copy(way, step - 1).wait_recv()
                if step < steps:
                    count_copy(way, step).start()

    forward(0)

    token_at = lax.broadcasted_iota(jnp.int32, (tok_count, cap), 0)
    hot = jnp.where(token_at == routes[...], 1.0, 0.0).T.astype(jnp.bfloat16)
    logit = jnp.zeros((cap, HD), jnp.float32)
    for c in range(chunks):
        loads[c].wait()
        picked = jnp.dot(hot, tok_v[c], preferred_element_type=jnp.float32)
        picked_v[c] = picked
        scaled = picked * weight[:, c * chunk : (c + 1) * chunk]
        for t in range(chunk // HD):
            logit = logit + scaled[:, t * HD : (t + 1) * HD]
    logit = jnp.sum(logit, axis=1, keepdims=True)
    gate = 1.0 / (1.0 + jnp.exp(-logit))
    live = lax.broadcasted_iota(jnp.int32, (cap, 1), 0) < counts[0, 0]
    kept = jnp.where(live, gate, 0.0)
    for copy in rows_in:
        copy.wait()

    lane_at = lax.broadcasted_iota(jnp.int32, (cap, HD), 1)

    def scale_group(other):
        gate_sum = jnp.zeros((cap, HD), jnp.float32)
        deltas = jnp.zeros((cap, HD), jnp.float32)
        for h in range(GROUP):
            cols = slice(h * HD, (h + 1) * HD)
            cot = cot_v[other, :, cols].astype(jnp.float32)
            out = attn_v[other, :, cols].astype(jnp.float32)
            dout = (kept * cot).astype(jnp.bfloat16)
            dout_v[other, :, cols] = dout
            gate_sum = gate_sum + cot * out
            delta = jnp.sum(dout.astype(jnp.float32) * out, axis=1, keepdims=True)
            deltas = jnp.where(lane_at == h, delta, deltas)
        de_v[other] = deltas.T[:GROUP]
        return gate_sum

    gate_sum = jnp.zeros((cap, HD), jnp.float32)
    for i, other in enumerate(y_peers):
        gate_sum = gate_sum + scale_group(other)
        for a, (source, target) in enumerate(((dout_v, do_all), (de_v, de_all))):
            late.append(
                remote(source.at[other], target.at[y], y_send.at[4 + a, i], y_recv.at[4 + a, i], at(other, z))
            )
            late[-1].start()
    forward(1)
    gate_sum = gate_sum + scale_group(y)
    mine = [
        pltpu.make_async_copy(dout_v.at[y], do_all.at[y], own_sem.at[4]),
        pltpu.make_async_copy(de_v.at[y], de_all.at[y], own_sem.at[5]),
    ]
    for copy in mine:
        copy.start()
    forward(2)
    gate_grad = jnp.sum(gate_sum, axis=1, keepdims=True)
    logit_grad = jnp.where(live, gate_grad * gate * (1.0 - gate), 0.0)
    segments = part.shape[1]
    for c in range(chunks):
        terms = jnp.sum(logit_grad * picked_v[c], axis=0, keepdims=True)
        for t in range(chunk // HD):
            n = c * (chunk // HD) + t
            part[n // segments, n % segments : n % segments + 1, :] = terms[:, t * HD : (t + 1) * HD]
    for step in range(3, max(p[2] for p in plan) + 1):
        forward(step)
    own[3].wait()
    for copy in mine:
        copy.wait()
    for copy in first:
        copy.wait_send()
    for copy in late:
        copy.wait()
    for lane, (array, way, steps) in enumerate(plan):
        for step in range(steps):
            ring_copy(lane, step).wait_send()
            if array == 0:
                count_copy(way, step).wait_send()


def gather(y_count, z_count, dp_count, tokens, weight, routes, counts, query, key_in, value_in, attn_out, grad_out):
    cap = query.shape[0]
    tok_count, width = tokens.shape
    chunks = 5
    longer = z_count // 2
    anywhere = pl.BlockSpec(memory_space=pl.ANY)
    vmem = pl.BlockSpec(memory_space=pltpu.VMEM)
    smem = pl.BlockSpec(memory_space=pltpu.SMEM)
    bf16, f32 = jnp.bfloat16, jnp.float32
    shape = jax.ShapeDtypeStruct
    return pl.pallas_call(
        functools.partial(gather_kernel, y_count, z_count, chunks),
        out_shape=(
            shape((y_count, cap, WIDE), bf16),
            shape((y_count, cap, WIDE), bf16),
            shape((y_count, GROUP, cap), f32),
            shape((z_count, y_count, cap, HD), bf16),
            shape((z_count, y_count, cap, HD), bf16),
            shape((z_count, y_count, 1, HD), jnp.int32),
            shape((dp_count, width // HD // dp_count, HD), f32),
        ),
        in_specs=[anywhere, vmem, vmem, smem] + [anywhere] * 5,
        out_specs=(anywhere,) * 6 + (vmem,),
        scratch_shapes=[
            pltpu.VMEM((chunks, tok_count, width // chunks), bf16),
            pltpu.VMEM((y_count, cap, WIDE), bf16),
            pltpu.VMEM((y_count, cap, WIDE), bf16),
            pltpu.VMEM((y_count, cap, WIDE), bf16),
            pltpu.VMEM((y_count, GROUP, cap), f32),
            pltpu.VMEM((1, HD), jnp.int32),
            pltpu.VMEM((chunks, cap, width // chunks), f32),
            pltpu.VMEM((cap, WIDE), bf16),
            pltpu.VMEM((cap, HD), bf16),
            pltpu.VMEM((cap, HD), bf16),
            pltpu.SemaphoreType.DMA((chunks,)),
            pltpu.SemaphoreType.DMA((2, y_count)),
            pltpu.SemaphoreType.DMA((6,)),
            pltpu.SemaphoreType.DMA((6, y_count - 1)),
            pltpu.SemaphoreType.DMA((6, y_count - 1)),
            pltpu.SemaphoreType.DMA((4, longer)),
            pltpu.SemaphoreType.DMA((4, longer)),
            pltpu.SemaphoreType.DMA((2, longer)),
            pltpu.SemaphoreType.DMA((2, longer)),
        ],
        compiler_params=pltpu.CompilerParams(
            collective_id=0, has_side_effects=True, vmem_limit_bytes=63 * MIB
        ),
        name="gather",
    )(tokens, weight, routes, counts, query, key_in, value_in, attn_out, grad_out)


def attention_kernel(
    y_count, z_count, block_rows, block_keys,
    counts, q_hbm, do_hbm, de_hbm, k_hbm, v_hbm,
    dq_hbm, dk_hbm, dv_hbm,
    q_in, do_in, de_in, k_in, v_in, dq_out, dk_out, dv_out, in_sem, out_sem,
    row_f, do_f, de_f, q_b, do_b, de_b, k_f, v_f, k_b, kt_b, v_b, exps, tops, best, total, dk_f, dv_f, dq_f,
    s_even, s_odd, p_even, p_odd, ds_even, ds_odd, pair_row, pair_key, shard_start,
):
    loads = []
    for i, (source, target) in enumerate(
        ((k_hbm, k_in), (v_hbm, v_in), (q_hbm, q_in), (do_hbm, do_in), (de_hbm, de_in))
    ):
        loads.append(pltpu.make_async_copy(source, target, in_sem.at[i]))
        loads[-1].start()
    cap = q_in.shape[1]
    z = lax.axis_index("seq") % z_count
    shard_count = y_count * z_count
    lanes = GROUP * block_rows
    key_blocks = KEEP // block_keys
    root = 1.0 / math.sqrt(HD)
    power = root * math.log2(math.e)
    f32, bf16 = jnp.float32, jnp.bfloat16
    s_b, p_b, ds_b = (s_even, s_odd), (p_even, p_odd), (ds_even, ds_odd)

    def count_of(shard):
        return counts[shard % z_count, shard // z_count, 0, 0]

    def add_counts(shard, offset):
        shard_start[shard] = offset
        return offset + count_of(shard)

    lax.fori_loop(0, shard_count, add_counts, jnp.int32(0))

    loads[0].wait()
    loads[1].wait()

    def pack_keys(step, carry):
        for more in range(4):
            shard = step * 4 + more
            zz, yy = shard % z_count, shard // z_count
            rows = pl.ds(shard_start[shard], cap)
            k_f[rows, :] = k_in[zz, yy].astype(f32)
            v_f[rows, :] = v_in[zz, yy].astype(f32)
        return carry

    lax.fori_loop(0, shard_count // 4, pack_keys, 0)

    def narrow_keys(b, carry):
        rows = pl.ds(b * block_keys, block_keys)
        k_b[b] = k_f[rows, :].astype(bf16)
        kt_b[b] = k_f[rows, :].T.astype(bf16)
        v_b[b] = v_f[rows, :].astype(bf16)
        dk_f[b] = jnp.zeros((block_keys, HD), f32)
        dv_f[b] = jnp.zeros((block_keys, HD), f32)
        return carry

    lax.fori_loop(0, key_blocks, narrow_keys, 0)

    row_start, shift, live = [], [], []
    rows_here = 0
    for yy in range(y_count):
        row_start.append(rows_here)
        shift.append(shard_start[yy * z_count + z] - rows_here)
        live.append(counts[z, yy, 0, 0])
        rows_here = rows_here + live[yy]

    def place_of(row):
        found = row + shift[0]
        for yy in range(1, y_count):
            found = jnp.where(row >= row_start[yy], row + shift[yy], found)
        return found

    for load in loads[2:]:
        load.wait()
    for yy in range(y_count):
        rows = pl.ds(row_start[yy], cap)
        for h in range(GROUP):
            cols = slice(h * HD, (h + 1) * HD)
            row_f[h, rows, :] = q_in[yy, :, cols].astype(f32)
            do_f[h, rows, :] = do_in[yy, :, cols].astype(f32)
        padded = jnp.concatenate([de_in[yy], jnp.zeros((HD - GROUP, cap), f32)], axis=0)
        de_f[rows, :] = padded.T
    tail = pl.ds(rows_here, block_rows)
    for h in range(GROUP):
        row_f[h, tail, :] = jnp.zeros((block_rows, HD), f32)
        do_f[h, tail, :] = jnp.zeros((block_rows, HD), f32)
    de_f[tail, :] = jnp.zeros((block_rows, HD), f32)

    row_blocks = (rows_here + block_rows - 1) // block_rows

    def narrow_rows(b, carry):
        rows = pl.ds(pl.multiple_of(b * block_rows, block_rows), block_rows)
        across = de_f[rows, :].T
        for h in range(GROUP):
            mine = slice(h * block_rows, (h + 1) * block_rows)
            q_b[b, mine, :] = row_f[h, rows, :].astype(bf16)
            do_b[b, mine, :] = do_f[h, rows, :].astype(bf16)
            de_b[b, :, mine] = across[h : h + 1, :]
        return carry

    lax.fori_loop(0, row_blocks, narrow_rows, 0)

    nt = (((1,), (1,)), ((), ()))

    def list_pairs(masked, count):
        def of_rows(b, count):
            full = (place_of(b * block_rows) + 1) // block_keys
            used = place_of(jnp.minimum((b + 1) * block_rows, rows_here) - 1) // block_keys + 1

            def add(kb, count):
                pair_row[count] = b
                pair_key[count] = kb
                return count + 1

            first, last = (full, used) if masked else (0, full)
            return lax.fori_loop(first, last, add, count)

        return lax.fori_loop(0, row_blocks, of_rows, count)

    whole_pairs = list_pairs(False, jnp.int32(0))
    pairs = list_pairs(True, whole_pairs)
    for more in range(3):
        pair_row[pairs + more] = q_b.shape[0] - 1
        pair_key[pairs + more] = 0

    def start_rows(b, carry):
        best[b] = jnp.full((8, lanes), NEGATIVE, f32)
        total[b] = jnp.zeros((8, lanes), f32)
        dq_f[b] = jnp.zeros((HD, lanes), f32)
        return carry

    lax.fori_loop(0, row_blocks, start_rows, 0)

    def raw(n, slot):
        s_b[slot][:, :] = lax.dot_general(
            k_b[pair_key[n]], q_b[pair_row[n]], nt, preferred_element_type=f32
        )

    def grow(masked, n, slot):
        b, kb = pair_row[n], pair_key[n]
        for part in range(lanes // SUB_LANES):
            cols = slice(part * SUB_LANES, (part + 1) * SUB_LANES)
            block = s_b[slot][:, cols] * power
            if masked:
                lane = lax.broadcasted_iota(jnp.int32, (1, SUB_LANES), 1)
                row_place = place_of(b * block_rows + lane % block_rows) - kb * block_keys
                key_place = lax.broadcasted_iota(jnp.int32, (block_keys, SUB_LANES), 0)
                block = jnp.where(key_place <= row_place, block, NEGATIVE)
            block = block.reshape(block_keys // 8, 8, SUB_LANES)
            before = best[b, :, cols]
            after = jnp.maximum(before, jnp.max(block, axis=0))
            grown = jnp.exp2(block - after)
            exps[n, :, :, cols] = grown
            tops[n, :, cols] = after
            best[b, :, cols] = after
            total[b, :, cols] = total[b, :, cols] * jnp.exp2(before - after) + jnp.sum(grown, axis=0)

    def some_scores(masked, many, j, carry):
        for more in range(many):
            n = many * j + more
            raw(n + 1, (more + 1) % 2)
            grow(masked, n, more % 2)
        return carry

    raw(0, 0)
    whole_steps = whole_pairs // DEEP
    lax.fori_loop(0, whole_steps, functools.partial(some_scores, False, DEEP), 0)
    lax.fori_loop(whole_steps * (DEEP // 2), (pairs + 1) // 2, functools.partial(some_scores, True, 2), 0)

    def finish_rows(b, carry):
        top = jnp.max(best[b], axis=0, keepdims=True)
        summed = jnp.sum(total[b] * jnp.exp2(best[b] - top), axis=0, keepdims=True)
        best[b] = jnp.broadcast_to(top + jnp.log2(summed), (8, lanes))
        return carry

    lax.fori_loop(0, row_blocks, finish_rows, 0)

    def terms(n, slot):
        b, kb = pair_row[n], pair_key[n]
        scale = jnp.exp2(tops[n] - best[b])
        prob = (exps[n] * scale).reshape(block_keys, lanes)
        prob_grad = lax.dot_general(v_b[kb], do_b[b], nt, preferred_element_type=f32)
        p_b[slot][:, :] = prob.astype(bf16)
        ds_b[slot][:, :] = (prob * (prob_grad - de_b[b])).astype(bf16)

    def products(n, slot):
        b, kb = pair_row[n], pair_key[n]
        score_grad = ds_b[slot][:, :]
        dv_f[kb] += jnp.dot(p_b[slot][:, :], do_b[b], preferred_element_type=f32)
        dk_f[kb] += jnp.dot(score_grad, q_b[b], preferred_element_type=f32)
        dq_f[b] += jnp.dot(kt_b[kb], score_grad, preferred_element_type=f32)

    def some_pairs(many, j, carry):
        for more in range(many):
            n = many * j + more
            products(n, more % 2)
            terms(n + 1, (more + 1) % 2)
        return carry

    @pl.when(pairs > 0)
    def _():
        terms(0, 0)

    steps = pairs // DEEP
    lax.fori_loop(0, steps, functools.partial(some_pairs, DEEP), 0)
    lax.fori_loop(steps * (DEEP // 2), pairs // 2, functools.partial(some_pairs, 2), 0)

    @pl.when(pairs % 2 == 1)
    def _():
        products(pairs - 1, 0)

    slot = lax.broadcasted_iota(jnp.int32, (cap, 1), 0)

    def widen_keys(b, carry):
        rows = pl.ds(pl.multiple_of(b * block_keys, block_keys), block_keys)
        k_f[rows, :] = dk_f[b] * root
        v_f[rows, :] = dv_f[b]
        return carry

    lax.fori_loop(0, key_blocks, widen_keys, 0)

    def unpack_keys(step, carry):
        for more in range(4):
            shard = step * 4 + more
            zz, yy = shard % z_count, shard // z_count
            rows = pl.ds(shard_start[shard], cap)
            held = slot < count_of(shard)
            dk_out[zz, yy] = jnp.where(held, k_f[rows, :], 0.0).astype(bf16)
            dv_out[zz, yy] = jnp.where(held, v_f[rows, :], 0.0).astype(bf16)
        return carry

    lax.fori_loop(0, shard_count // 4, unpack_keys, 0)
    stores = [
        pltpu.make_async_copy(dk_out, dk_hbm, out_sem.at[0]),
        pltpu.make_async_copy(dv_out, dv_hbm, out_sem.at[1]),
        pltpu.make_async_copy(dq_out, dq_hbm, out_sem.at[2]),
    ]
    stores[0].start()
    stores[1].start()

    def turn_rows(b, carry):
        rows = pl.ds(pl.multiple_of(b * block_rows, block_rows), block_rows)
        turned = dq_f[b].T * root
        for h in range(GROUP):
            row_f[h, rows, :] = turned[h * block_rows : (h + 1) * block_rows, :]
        return carry

    lax.fori_loop(0, row_blocks, turn_rows, 0)

    for yy in range(y_count):
        rows = pl.ds(row_start[yy], cap)
        for h in range(GROUP):
            grad = jnp.where(slot < live[yy], row_f[h, rows, :], 0.0)
            dq_out[yy, :, h * HD : (h + 1) * HD] = grad.astype(bf16)

    stores[2].start()
    for store in stores:
        store.wait()


def attention(y_count, z_count, counts, q_in, do_in, de_in, k_in, v_in):
    cap = q_in.shape[1]
    block_rows, block_keys = 64, 256
    lanes = GROUP * block_rows
    most = y_count * cap
    row_blocks = most // block_rows
    key_blocks = KEEP // block_keys
    anywhere = pl.BlockSpec(memory_space=pl.ANY)
    bf16, f32 = jnp.bfloat16, jnp.float32
    shape = jax.ShapeDtypeStruct
    return pl.pallas_call(
        functools.partial(attention_kernel, y_count, z_count, block_rows, block_keys),
        out_shape=(
            shape((y_count, cap, WIDE), bf16),
            shape((z_count, y_count, cap, HD), bf16),
            shape((z_count, y_count, cap, HD), bf16),
        ),
        in_specs=[pl.BlockSpec(memory_space=pltpu.SMEM)] + [anywhere] * 5,
        out_specs=(anywhere,) * 3,
        scratch_shapes=[
            pltpu.VMEM((y_count, cap, WIDE), bf16),
            pltpu.VMEM((y_count, cap, WIDE), bf16),
            pltpu.VMEM((y_count, GROUP, cap), f32),
            pltpu.VMEM((z_count, y_count, cap, HD), bf16),
            pltpu.VMEM((z_count, y_count, cap, HD), bf16),
            pltpu.VMEM((y_count, cap, WIDE), bf16),
            pltpu.VMEM((z_count, y_count, cap, HD), bf16),
            pltpu.VMEM((z_count, y_count, cap, HD), bf16),
            pltpu.SemaphoreType.DMA((5,)),
            pltpu.SemaphoreType.DMA((3,)),
            pltpu.VMEM((GROUP, most + cap, HD), f32),
            pltpu.VMEM((GROUP, most + cap, HD), f32),
            pltpu.VMEM((most + cap, HD), f32),
            pltpu.VMEM((row_blocks + 1, lanes, HD), bf16),
            pltpu.VMEM((row_blocks + 1, lanes, HD), bf16),
            pltpu.VMEM((row_blocks + 1, 1, lanes), f32),
            pltpu.VMEM((KEEP + cap, HD), f32),
            pltpu.VMEM((KEEP + cap, HD), f32),
            pltpu.VMEM((key_blocks, block_keys, HD), bf16),
            pltpu.VMEM((key_blocks, HD, block_keys), bf16),
            pltpu.VMEM((key_blocks, block_keys, HD), bf16),
            pltpu.VMEM((row_blocks * key_blocks + 1, block_keys // 8, 8, lanes), f32),
            pltpu.VMEM((row_blocks * key_blocks + 1, 8, lanes), f32),
            pltpu.VMEM((row_blocks + 1, 8, lanes), f32),
            pltpu.VMEM((row_blocks + 1, 8, lanes), f32),
            pltpu.VMEM((key_blocks, block_keys, HD), f32),
            pltpu.VMEM((key_blocks, block_keys, HD), f32),
            pltpu.VMEM((row_blocks, HD, lanes), f32),
            pltpu.VMEM((block_keys, lanes), f32),
            pltpu.VMEM((block_keys, lanes), f32),
            pltpu.VMEM((block_keys, lanes), bf16),
            pltpu.VMEM((block_keys, lanes), bf16),
            pltpu.VMEM((block_keys, lanes), bf16),
            pltpu.VMEM((block_keys, lanes), bf16),
            pltpu.SMEM((row_blocks * key_blocks + 3,), jnp.int32),
            pltpu.SMEM((row_blocks * key_blocks + 3,), jnp.int32),
            pltpu.SMEM((y_count * z_count,), jnp.int32),
        ],
        compiler_params=pltpu.CompilerParams(vmem_limit_bytes=62 * MIB),
        name="attention",
    )(counts, q_in, do_in, de_in, k_in, v_in)


def scatter_kernel(
    y_count, z_count, dp_count,
    dq_in, dk_hbm, dv_hbm, part,
    dq_out, dk_out, dv_out, router_out, dk_in, dv_in,
    held, fin, dp_held, y_held, z_held, dp_sum, y_sum, dq_own,
    own_sem, q_send, q_recv, ring_send, ring_recv, fin_send, fin_recv, r_send, r_recv,
):
    y, z = place(z_count)
    dp = lax.axis_index("dp")
    f32, bf16 = jnp.float32, jnp.bfloat16

    def at(y_there, z_there):
        return {"seq": y_there * z_count + z_there}

    right, left = (z + 1) % z_count, (z + z_count - 1) % z_count
    y_peers = [(y + step) % y_count for step in range(1, y_count)]
    z_peers = [(z + step) % z_count for step in range(1, z_count)]
    dp_peers = [(dp + step) % dp_count for step in range(1, dp_count)]
    peers = [at(other, z) for other in y_peers] + [at(y, other) for other in z_peers]
    peers += [{"dp": other} for other in dp_peers]
    greet(peers)

    def wide(ref, g):
        return ref.at[:, pl.ds(pl.multiple_of(g * WIDE, WIDE), WIDE)]

    def narrow(ref, g):
        return ref.at[:, pl.ds(pl.multiple_of(g * HD, HD), HD)]

    own_in = [
        pltpu.make_async_copy(dk_hbm, dk_in, own_sem.at[1]),
        pltpu.make_async_copy(dv_hbm, dv_in, own_sem.at[2]),
        pltpu.make_async_copy(dq_in.at[y], dq_own, own_sem.at[0]),
    ]
    for copy in own_in:
        copy.start()
    for copy in own_in:
        copy.wait()
    own = [pltpu.make_async_copy(dq_own, wide(dq_out, y), own_sem.at[0])]
    own[0].start()
    pl.semaphore_wait(pltpu.get_barrier_semaphore(), len(peers))

    plan = ring_plan(z_count)
    mine = (dk_in, dv_in)

    def ring_copy(lane, step):
        array, way, steps = plan[lane]
        block = (z + way * (steps - step) + z_count) % z_count
        there = at(y, right if way == 1 else left)
        source = mine[array].at[block] if step == 0 else held.at[lane, step - 1]
        return remote(source, held.at[lane, step], ring_send.at[lane, step], ring_recv.at[lane, step], there)

    def forward(step):
        for lane, (array, way, steps) in enumerate(plan):
            if step < steps:
                if step > 0:
                    ring_copy(lane, step - 1).wait_recv()
                    block = (z + way * (steps - step) + z_count) % z_count
                    for g in range(y_count):
                        total = held[lane, step - 1, g].astype(f32) + mine[array][block, g].astype(f32)
                        held[lane, step - 1, g] = total.astype(bf16)
                ring_copy(lane, step).start()

    forward(0)
    sends = []
    for i, other in enumerate(y_peers):
        sends.append(remote(dq_in.at[other], wide(dq_out, y), q_send.at[i], q_recv.at[i], at(other, z)))
        sends[-1].start()

    def share(first, source_of, held_ref, peers_there, me):
        copies = []
        for i, there in enumerate(peers_there):
            copies.append(remote(source_of(i), held_ref.at[me], r_send.at[first + i], r_recv.at[first + i], there))
            copies[-1].start()
        return copies

    over_dp = share(0, lambda i: part.at[dp_peers[i]], dp_held, [{"dp": other} for other in dp_peers], dp)
    forward(1)
    for copy in over_dp:
        copy.wait()
    total = part[dp]
    for other in dp_peers:
        total = total + dp_held[other]
    dp_sum[...] = total
    over_y = share(dp_count - 1, lambda i: dp_sum, y_held, [at(other, z) for other in y_peers], y)
    forward(2)
    for copy in over_y:
        copy.wait()
    for other in y_peers:
        total = total + y_held[other]
    y_sum[...] = total
    over_z = share(
        dp_count + y_count - 2, lambda i: y_sum, z_held, [at(y, other) for other in z_peers], z
    )
    for step in range(3, max(p[2] for p in plan)):
        forward(step)
    for copy in over_z:
        copy.wait()
    for other in z_peers:
        total = total + z_held[other]
    router_out[...] = total

    ends = []
    for array, target in ((0, dk_out), (1, dv_out)):
        lanes = [lane for lane in range(4) if plan[lane][0] == array]
        for lane in lanes:
            ring_copy(lane, plan[lane][2] - 1).wait_recv()
        for g in range(y_count):
            total = mine[array][z, g].astype(f32)
            for lane in lanes:
                total = total + held[lane, plan[lane][2] - 1, g].astype(f32)
            fin[array, g] = total.astype(bf16)
        for i, other in enumerate(y_peers):
            ends.append(
                remote(
                    fin.at[array, other],
                    narrow(target, y),
                    fin_send.at[array, i],
                    fin_recv.at[array, i],
                    at(other, z),
                )
            )
            ends[-1].start()
        own.append(pltpu.make_async_copy(fin.at[array, y], narrow(target, y), own_sem.at[1 + array]))
        own[-1].start()
    for lane, (array, way, steps) in enumerate(plan):
        for step in range(steps):
            ring_copy(lane, step).wait_send()
    for copy in own + sends + ends:
        copy.wait()


def scatter(y_count, z_count, dp_count, dq_in, dk_in, dv_in, part):
    cap = dq_in.shape[1]
    longer = z_count // 2
    small = part.shape[1:]
    anywhere = pl.BlockSpec(memory_space=pl.ANY)
    vmem = pl.BlockSpec(memory_space=pltpu.VMEM)
    bf16, f32 = jnp.bfloat16, jnp.float32
    shape = jax.ShapeDtypeStruct
    router_copies = dp_count + y_count + z_count - 3
    return pl.pallas_call(
        functools.partial(scatter_kernel, y_count, z_count, dp_count),
        out_shape=(
            shape((cap, HEADS * HD), bf16),
            shape((cap, KV * HD), bf16),
            shape((cap, KV * HD), bf16),
            shape(small, f32),
        ),
        in_specs=[anywhere, anywhere, anywhere, vmem],
        out_specs=(anywhere, anywhere, anywhere, vmem),
        scratch_shapes=[
            pltpu.VMEM((z_count, y_count, cap, HD), bf16),
            pltpu.VMEM((z_count, y_count, cap, HD), bf16),
            pltpu.VMEM((4, longer, y_count, cap, HD), bf16),
            pltpu.VMEM((2, y_count, cap, HD), bf16),
            pltpu.VMEM((dp_count,) + small, f32),
            pltpu.VMEM((y_count,) + small, f32),
            pltpu.VMEM((z_count,) + small, f32),
            pltpu.VMEM(small, f32),
            pltpu.VMEM(small, f32),
            pltpu.VMEM((cap, WIDE), bf16),
            pltpu.SemaphoreType.DMA((3,)),
            pltpu.SemaphoreType.DMA((y_count - 1,)),
            pltpu.SemaphoreType.DMA((y_count - 1,)),
            pltpu.SemaphoreType.DMA((4, longer)),
            pltpu.SemaphoreType.DMA((4, longer)),
            pltpu.SemaphoreType.DMA((2, y_count - 1)),
            pltpu.SemaphoreType.DMA((2, y_count - 1)),
            pltpu.SemaphoreType.DMA((router_copies,)),
            pltpu.SemaphoreType.DMA((router_copies,)),
        ],
        compiler_params=pltpu.CompilerParams(
            collective_id=1, has_side_effects=True, vmem_limit_bytes=63 * MIB
        ),
        name="scatter",
    )(dq_in, dk_in, dv_in, part)


def result_kernel(dq_in, dk_in, dv_in, dq_out, dk_out, dv_out, dq_v, dk_v, dv_v, in_sem, out_sem):
    moves = []
    rows = dq_v.shape[1]
    for i in range(dq_v.shape[0]):
        part = pl.ds(i * rows, rows)
        moves.append((dq_in.at[part], dq_v.at[i], dq_out.at[part]))
    moves += [(dk_in, dk_v, dk_out), (dv_in, dv_v, dv_out)]
    loads = [pltpu.make_async_copy(a, b, in_sem.at[i]) for i, (a, b, _) in enumerate(moves)]
    stores = [pltpu.make_async_copy(b, c, out_sem.at[i]) for i, (_, b, c) in enumerate(moves)]
    for load in loads:
        load.start()
    for load, store in zip(loads, stores):
        load.wait()
        store.start()
    for store in stores:
        store.wait()


def results(dq, dk, dv):
    anywhere = pl.BlockSpec(memory_space=pl.ANY)
    pieces = 4
    shape = jax.ShapeDtypeStruct
    return pl.pallas_call(
        result_kernel,
        out_shape=tuple(shape(x.shape, x.dtype) for x in (dq, dk, dv)),
        in_specs=[anywhere] * 3,
        out_specs=(anywhere,) * 3,
        scratch_shapes=[
            pltpu.VMEM((pieces, dq.shape[0] // pieces, dq.shape[1]), dq.dtype),
            pltpu.VMEM(dk.shape, dk.dtype),
            pltpu.VMEM(dv.shape, dv.dtype),
            pltpu.SemaphoreType.DMA((pieces + 2,)),
            pltpu.SemaphoreType.DMA((pieces + 2,)),
        ],
        compiler_params=pltpu.CompilerParams(vmem_limit_bytes=63 * MIB),
        name="results",
    )(dq, dk, dv)


def on_device(tokens, router_weight, routes, counts, query, key_in, value_in, attn_out, grad_out):
    y_count = KV
    z_count = lax.axis_size("seq") // y_count
    dp_count = lax.axis_size("dp")
    width = tokens.shape[2]
    q_all, do_all, de_all, k_all, v_all, c_all, part = gather(
        y_count, z_count, dp_count, tokens[0], router_weight[None], routes, counts,
        query[0], key_in[0], value_in[0], attn_out[0], grad_out[0],
    )
    dq, dk, dv = attention(y_count, z_count, c_all, q_all, do_all, de_all, k_all, v_all)
    dq, dk, dv, router = scatter(y_count, z_count, dp_count, dq, dk, dv, part)
    dq, dk, dv = results(dq, dk, dv)
    share = width // (dp_count * y_count * z_count)
    router = lax.dynamic_slice(router.reshape(-1), (lax.axis_index("seq") * share,), (share,))
    return (dq[None], dk[None], dv[None], router)


def solution(mesh):
    rows = P("dp", "seq", None)
    return jax.shard_map(
        on_device,
        mesh=mesh,
        in_specs=(rows, P(), P("dp", "seq"), P("dp", "seq"), rows, rows, rows, rows, rows),
        out_specs=(rows, rows, rows, P(("dp", "seq"))),
        check_vma=False,
    )
```

```python
import functools
import math

import jax
import jax.numpy as jnp
from jax import lax
from jax.experimental import pallas as pl
from jax.experimental.pallas import tpu as pltpu
from jax.sharding import PartitionSpec as P

HEADS = 32
KV = 4
HD = 128
GROUP = HEADS // KV
WIDE = GROUP * HD
KEEP = 2048
SUB_LANES = 128
DEEP = (8, 4, 2)
NEGATIVE = -1e30
MESH = pl.DeviceIdType.MESH
MIB = 1024 * 1024


def place(z_count):
    me = lax.axis_index("seq")
    return me // z_count, me % z_count


def remote(src, dst, send_sem, recv_sem, device):
    return pltpu.make_async_remote_copy(
        src_ref=src,
        dst_ref=dst,
        send_sem=send_sem,
        recv_sem=recv_sem,
        device_id=device,
        device_id_type=MESH,
    )


def greet(devices):
    barrier = pltpu.get_barrier_semaphore()
    for device in devices:
        pl.semaphore_signal(barrier, inc=1, device_id=device, device_id_type=MESH)


def ring_plan(z_count):
    longer = z_count // 2
    shorter = z_count - 1 - longer
    return ((0, 1, longer), (1, -1, longer), (1, 1, shorter), (0, -1, shorter))


def gather_kernel(
    y_count, z_count, chunks,
    tokens, weight, routes, counts, query, key_in, value_in, attn_out, grad_out,
    q_all, do_all, de_all, k_all, v_all, c_all, part,
    tok_v, cot_v, attn_v, dout_v, de_v, cnt_v, picked_v, q_own, k_own, v_own,
    tok_sem, in_sem, own_sem, y_send, y_recv, ring_send, ring_recv, c_send, c_recv,
):
    y, z = place(z_count)
    cap = query.shape[0]
    tok_count = tokens.shape[0]
    chunk = tokens.shape[1] // chunks

    def at(y_there, z_there):
        return {"seq": y_there * z_count + z_there}

    right, left = (z + 1) % z_count, (z + z_count - 1) % z_count
    y_peers = [(y + step) % y_count for step in range(1, y_count)]
    greet([at(other, z) for other in y_peers] + [at(y, right), at(y, left)])

    cnt_v[...] = jnp.full(cnt_v.shape, counts[0, 0], jnp.int32)

    def wide(ref, g):
        return ref.at[:, pl.ds(pl.multiple_of(g * WIDE, WIDE), WIDE)]

    def narrow(ref, g):
        return ref.at[:, pl.ds(pl.multiple_of(g * HD, HD), HD)]

    own_in = [
        pltpu.make_async_copy(narrow(key_in, y), k_own, own_sem.at[0]),
        pltpu.make_async_copy(narrow(value_in, y), v_own, own_sem.at[1]),
        pltpu.make_async_copy(wide(query, y), q_own, own_sem.at[2]),
    ]
    for copy in own_in:
        copy.start()
    loads = []
    for c in range(chunks):
        loads.append(pltpu.make_async_copy(tokens.at[:, pl.ds(c * chunk, chunk)], tok_v.at[c], tok_sem.at[c]))
        loads[-1].start()
    rows_in = []
    for g in range(y_count):
        for a, (source, target) in enumerate(((grad_out, cot_v), (attn_out, attn_v))):
            rows_in.append(
                pltpu.make_async_copy(source.at[:, pl.ds(g * WIDE, WIDE)], target.at[g], in_sem.at[a, g])
            )
            rows_in[-1].start()
    pl.semaphore_wait(pltpu.get_barrier_semaphore(), y_count + 1)

    first = []
    for i, other in enumerate(y_peers):
        there = at(other, z)
        for a, (source, target) in enumerate(
            (
                (narrow(key_in, other), k_all.at[z, y]),
                (narrow(value_in, other), v_all.at[z, y]),
                (cnt_v, c_all.at[z, y]),
            )
        ):
            first.append(remote(source, target, y_send.at[a, i], y_recv.at[a, i], there))
            first[-1].start()
    late = []
    for i, other in enumerate(y_peers):
        late.append(remote(wide(query, other), q_all.at[y], y_send.at[3, i], y_recv.at[3, i], at(other, z)))
        late[-1].start()
    own = [
        pltpu.make_async_copy(k_own, k_all.at[z, y], own_sem.at[0]),
        pltpu.make_async_copy(v_own, v_all.at[z, y], own_sem.at[1]),
        pltpu.make_async_copy(cnt_v, c_all.at[z, y], own_sem.at[3]),
        pltpu.make_async_copy(q_own, q_all.at[y], own_sem.at[2]),
    ]
    for copy in own_in:
        copy.wait()
    for copy in own:
        copy.start()
    for copy in own[:3]:
        copy.wait()
    for copy in first:
        copy.wait_recv()

    plan = ring_plan(z_count)
    held = (k_all, v_all)

    def ring_copy(lane, step):
        array, way, _ = plan[lane]
        block = (z - way * step + 2 * z_count) % z_count
        there = at(y, right if way == 1 else left)
        ref = held[array].at[block]
        return remote(ref, ref, ring_send.at[lane, step], ring_recv.at[lane, step], there)

    def count_copy(way, step):
        block = (z - way * step + 2 * z_count) % z_count
        there = at(y, right if way == 1 else left)
        ref = c_all.at[block]
        side = (1 - way) // 2
        return remote(ref, ref, c_send.at[side, step], c_recv.at[side, step], there)

    def forward(step):
        for lane, (array, way, steps) in enumerate(plan):
            if 0 < step <= steps:
                ring_copy(lane, step - 1).wait_recv()
            if step < steps:
                ring_copy(lane, step).start()
            if array == 0:
                if 0 < step <= steps:
                    count_copy(way, step - 1).wait_recv()
                if step < steps:
                    count_copy(way, step).start()

    forward(0)

    token_at = lax.broadcasted_iota(jnp.int32, (tok_count, cap), 0)
    hot = jnp.where(token_at == routes[...], 1.0, 0.0).T.astype(jnp.bfloat16)
    logit = jnp.zeros((cap, HD), jnp.float32)
    for c in range(chunks):
        loads[c].wait()
        picked = jnp.dot(hot, tok_v[c], preferred_element_type=jnp.float32)
        picked_v[c] = picked
        scaled = picked * weight[:, c * chunk : (c + 1) * chunk]
        for t in range(chunk // HD):
            logit = logit + scaled[:, t * HD : (t + 1) * HD]
    logit = jnp.sum(logit, axis=1, keepdims=True)
    gate = 1.0 / (1.0 + jnp.exp(-logit))
    live = lax.broadcasted_iota(jnp.int32, (cap, 1), 0) < counts[0, 0]
    kept = jnp.where(live, gate, 0.0)
    for copy in rows_in:
        copy.wait()

    lane_at = lax.broadcasted_iota(jnp.int32, (cap, HD), 1)

    def scale_group(other):
        gate_sum = jnp.zeros((cap, HD), jnp.float32)
        deltas = jnp.zeros((cap, HD), jnp.float32)
        for h in range(GROUP):
            cols = slice(h * HD, (h + 1) * HD)
            cot = cot_v[other, :, cols].astype(jnp.float32)
            out = attn_v[other, :, cols].astype(jnp.float32)
            dout = (kept * cot).astype(jnp.bfloat16)
            dout_v[other, :, cols] = dout
            gate_sum = gate_sum + cot * out
            delta = jnp.sum(dout.astype(jnp.float32) * out, axis=1, keepdims=True)
            deltas = jnp.where(lane_at == h, delta, deltas)
        de_v[other] = deltas.T[:GROUP]
        return gate_sum

    gate_sum = jnp.zeros((cap, HD), jnp.float32)
    for i, other in enumerate(y_peers):
        gate_sum = gate_sum + scale_group(other)
        for a, (source, target) in enumerate(((dout_v, do_all), (de_v, de_all))):
            late.append(
                remote(source.at[other], target.at[y], y_send.at[4 + a, i], y_recv.at[4 + a, i], at(other, z))
            )
            late[-1].start()
    forward(1)
    gate_sum = gate_sum + scale_group(y)
    mine = [
        pltpu.make_async_copy(dout_v.at[y], do_all.at[y], own_sem.at[4]),
        pltpu.make_async_copy(de_v.at[y], de_all.at[y], own_sem.at[5]),
    ]
    for copy in mine:
        copy.start()
    forward(2)
    gate_grad = jnp.sum(gate_sum, axis=1, keepdims=True)
    logit_grad = jnp.where(live, gate_grad * gate * (1.0 - gate), 0.0)
    segments = part.shape[1]
    for c in range(chunks):
        terms = jnp.sum(logit_grad * picked_v[c], axis=0, keepdims=True)
        for t in range(chunk // HD):
            n = c * (chunk // HD) + t
            part[n // segments, n % segments : n % segments + 1, :] = terms[:, t * HD : (t + 1) * HD]
    for step in range(3, max(p[2] for p in plan) + 1):
        forward(step)
    own[3].wait()
    for copy in mine:
        copy.wait()
    for copy in first:
        copy.wait_send()
    for copy in late:
        copy.wait()
    for lane, (array, way, steps) in enumerate(plan):
        for step in range(steps):
            ring_copy(lane, step).wait_send()
            if array == 0:
                count_copy(way, step).wait_send()


def gather(y_count, z_count, dp_count, tokens, weight, routes, counts, query, key_in, value_in, attn_out, grad_out):
    cap = query.shape[0]
    tok_count, width = tokens.shape
    chunks = 5
    longer = z_count // 2
    anywhere = pl.BlockSpec(memory_space=pl.ANY)
    vmem = pl.BlockSpec(memory_space=pltpu.VMEM)
    smem = pl.BlockSpec(memory_space=pltpu.SMEM)
    bf16, f32 = jnp.bfloat16, jnp.float32
    shape = jax.ShapeDtypeStruct
    return pl.pallas_call(
        functools.partial(gather_kernel, y_count, z_count, chunks),
        out_shape=(
            shape((y_count, cap, WIDE), bf16),
            shape((y_count, cap, WIDE), bf16),
            shape((y_count, GROUP, cap), f32),
            shape((z_count, y_count, cap, HD), bf16),
            shape((z_count, y_count, cap, HD), bf16),
            shape((z_count, y_count, 1, HD), jnp.int32),
            shape((dp_count, width // HD // dp_count, HD), f32),
        ),
        in_specs=[anywhere, vmem, vmem, smem] + [anywhere] * 5,
        out_specs=(anywhere,) * 6 + (vmem,),
        scratch_shapes=[
            pltpu.VMEM((chunks, tok_count, width // chunks), bf16),
            pltpu.VMEM((y_count, cap, WIDE), bf16),
            pltpu.VMEM((y_count, cap, WIDE), bf16),
            pltpu.VMEM((y_count, cap, WIDE), bf16),
            pltpu.VMEM((y_count, GROUP, cap), f32),
            pltpu.VMEM((1, HD), jnp.int32),
            pltpu.VMEM((chunks, cap, width // chunks), f32),
            pltpu.VMEM((cap, WIDE), bf16),
            pltpu.VMEM((cap, HD), bf16),
            pltpu.VMEM((cap, HD), bf16),
            pltpu.SemaphoreType.DMA((chunks,)),
            pltpu.SemaphoreType.DMA((2, y_count)),
            pltpu.SemaphoreType.DMA((6,)),
            pltpu.SemaphoreType.DMA((6, y_count - 1)),
            pltpu.SemaphoreType.DMA((6, y_count - 1)),
            pltpu.SemaphoreType.DMA((4, longer)),
            pltpu.SemaphoreType.DMA((4, longer)),
            pltpu.SemaphoreType.DMA((2, longer)),
            pltpu.SemaphoreType.DMA((2, longer)),
        ],
        compiler_params=pltpu.CompilerParams(
            collective_id=0, has_side_effects=True, vmem_limit_bytes=63 * MIB
        ),
        name="gather",
    )(tokens, weight, routes, counts, query, key_in, value_in, attn_out, grad_out)


def attention_kernel(
    y_count, z_count, block_rows, block_keys,
    counts, q_hbm, do_hbm, de_hbm, k_hbm, v_hbm,
    dq_hbm, dk_hbm, dv_hbm,
    q_in, do_in, de_in, k_in, v_in, dq_out, dk_out, dv_out, in_sem, out_sem,
    row_f, do_f, de_f, q_b, do_b, de_b, k_f, v_f, k_b, kt_b, v_b, exps, tops, best, total, dk_f, dv_f, dq_f,
    s_even, s_odd, p_even, p_odd, ds_even, ds_odd, pair_row, pair_key, shard_start,
):
    loads = []
    for i, (source, target) in enumerate(
        ((k_hbm, k_in), (v_hbm, v_in), (q_hbm, q_in), (do_hbm, do_in), (de_hbm, de_in))
    ):
        loads.append(pltpu.make_async_copy(source, target, in_sem.at[i]))
        loads[-1].start()
    cap = q_in.shape[1]
    z = lax.axis_index("seq") % z_count
    shard_count = y_count * z_count
    lanes = GROUP * block_rows
    key_blocks = KEEP // block_keys
    root = 1.0 / math.sqrt(HD)
    power = root * math.log2(math.e)
    f32, bf16 = jnp.float32, jnp.bfloat16
    s_b, p_b, ds_b = (s_even, s_odd), (p_even, p_odd), (ds_even, ds_odd)

    def count_of(shard):
        return counts[shard % z_count, shard // z_count, 0, 0]

    keys_before = jnp.int32(0)
    for shard in range(shard_count):
        shard_start[shard] = keys_before
        keys_before = keys_before + count_of(shard)

    loads[0].wait()
    loads[1].wait()

    def pack_keys(step, carry):
        for more in range(4):
            shard = step * 4 + more
            zz, yy = shard % z_count, shard // z_count
            rows = pl.ds(shard_start[shard], cap)
            k_f[rows, :] = k_in[zz, yy].astype(f32)
            v_f[rows, :] = v_in[zz, yy].astype(f32)
        return carry

    lax.fori_loop(0, shard_count // 4, pack_keys, 0)

    def narrow_keys(b, carry):
        rows = pl.ds(b * block_keys, block_keys)
        k_b[b] = k_f[rows, :].astype(bf16)
        kt_b[b] = k_f[rows, :].T.astype(bf16)
        v_b[b] = v_f[rows, :].astype(bf16)
        dk_f[b] = jnp.zeros((block_keys, HD), f32)
        dv_f[b] = jnp.zeros((block_keys, HD), f32)
        return carry

    lax.fori_loop(0, key_blocks, narrow_keys, 0)

    row_start, shift, live = [], [], []
    rows_here = 0
    for yy in range(y_count):
        row_start.append(rows_here)
        shift.append(shard_start[yy * z_count + z] - rows_here)
        live.append(counts[z, yy, 0, 0])
        rows_here = rows_here + live[yy]

    def place_of(row):
        found = row + shift[0]
        for yy in range(1, y_count):
            found = jnp.where(row >= row_start[yy], row + shift[yy], found)
        return found

    for load in loads[2:]:
        load.wait()
    for yy in range(y_count):
        rows = pl.ds(row_start[yy], cap)
        for h in range(GROUP):
            cols = slice(h * HD, (h + 1) * HD)
            row_f[h, rows, :] = q_in[yy, :, cols].astype(f32)
            do_f[h, rows, :] = do_in[yy, :, cols].astype(f32)
        padded = jnp.concatenate([de_in[yy], jnp.zeros((HD - GROUP, cap), f32)], axis=0)
        de_f[rows, :] = padded.T
    tail = pl.ds(rows_here, block_rows)
    for h in range(GROUP):
        row_f[h, tail, :] = jnp.zeros((block_rows, HD), f32)
        do_f[h, tail, :] = jnp.zeros((block_rows, HD), f32)
    de_f[tail, :] = jnp.zeros((block_rows, HD), f32)

    row_blocks = (rows_here + block_rows - 1) // block_rows

    def narrow_rows(b, carry):
        rows = pl.ds(pl.multiple_of(b * block_rows, block_rows), block_rows)
        across = de_f[rows, :].T
        for h in range(GROUP):
            mine = slice(h * block_rows, (h + 1) * block_rows)
            q_b[b, mine, :] = row_f[h, rows, :].astype(bf16)
            do_b[b, mine, :] = do_f[h, rows, :].astype(bf16)
            de_b[b, :, mine] = across[h : h + 1, :]
        return carry

    lax.fori_loop(0, row_blocks, narrow_rows, 0)

    nt = (((1,), (1,)), ((), ()))

    def list_pairs(masked, count):
        def of_rows(b, count):
            full = (place_of(b * block_rows) + 1) // block_keys
            used = place_of(jnp.minimum((b + 1) * block_rows, rows_here) - 1) // block_keys + 1

            def add(kb, count):
                pair_row[count] = b
                pair_key[count] = kb
                return count + 1

            first, last = (full, used) if masked else (0, full)
            return lax.fori_loop(first, last, add, count)

        return lax.fori_loop(0, row_blocks, of_rows, count)

    whole_pairs = list_pairs(False, jnp.int32(0))
    pairs = list_pairs(True, whole_pairs)
    for more in range(3):
        pair_row[pairs + more] = q_b.shape[0] - 1
        pair_key[pairs + more] = 0

    def start_rows(b, carry):
        best[b] = jnp.full((8, lanes), NEGATIVE, f32)
        total[b] = jnp.zeros((8, lanes), f32)
        dq_f[b] = jnp.zeros((HD, lanes), f32)
        return carry

    lax.fori_loop(0, row_blocks, start_rows, 0)

    def raw(n, slot):
        s_b[slot][:, :] = lax.dot_general(
            k_b[pair_key[n]], q_b[pair_row[n]], nt, preferred_element_type=f32
        )

    def grow(masked, n, slot):
        b, kb = pair_row[n], pair_key[n]
        for part in range(lanes // SUB_LANES):
            cols = slice(part * SUB_LANES, (part + 1) * SUB_LANES)
            block = s_b[slot][:, cols] * power
            if masked:
                lane = lax.broadcasted_iota(jnp.int32, (1, SUB_LANES), 1)
                row_place = place_of(b * block_rows + lane % block_rows) - kb * block_keys
                key_place = lax.broadcasted_iota(jnp.int32, (block_keys, SUB_LANES), 0)
                block = jnp.where(key_place <= row_place, block, NEGATIVE)
            block = block.reshape(block_keys // 8, 8, SUB_LANES)
            before = best[b, :, cols]
            after = jnp.maximum(before, jnp.max(block, axis=0))
            grown = jnp.exp2(block - after)
            exps[n, :, :, cols] = grown
            tops[n, :, cols] = after
            best[b, :, cols] = after
            total[b, :, cols] = total[b, :, cols] * jnp.exp2(before - after) + jnp.sum(grown, axis=0)

    def some_scores(masked, many, j, carry):
        for more in range(many):
            n = many * j + more
            raw(n + 1, (more + 1) % 2)
            grow(masked, n, more % 2)
        return carry

    raw(0, 0)
    done = jnp.int32(0)
    for many in DEEP:
        lax.fori_loop(done // many, whole_pairs // many, functools.partial(some_scores, False, many), 0)
        done = whole_pairs // many * many
    lax.fori_loop(done // 2, (pairs + 1) // 2, functools.partial(some_scores, True, 2), 0)

    def finish_rows(b, carry):
        top = jnp.max(best[b], axis=0, keepdims=True)
        summed = jnp.sum(total[b] * jnp.exp2(best[b] - top), axis=0, keepdims=True)
        best[b] = jnp.broadcast_to(top + jnp.log2(summed), (8, lanes))
        return carry

    lax.fori_loop(0, row_blocks, finish_rows, 0)

    def terms(n, slot):
        b, kb = pair_row[n], pair_key[n]
        scale = jnp.exp2(tops[n] - best[b])
        prob = (exps[n] * scale).reshape(block_keys, lanes)
        prob_grad = lax.dot_general(v_b[kb], do_b[b], nt, preferred_element_type=f32)
        p_b[slot][:, :] = prob.astype(bf16)
        ds_b[slot][:, :] = (prob * (prob_grad - de_b[b])).astype(bf16)

    def products(n, slot):
        b, kb = pair_row[n], pair_key[n]
        score_grad = ds_b[slot][:, :]
        dv_f[kb] += jnp.dot(p_b[slot][:, :], do_b[b], preferred_element_type=f32)
        dk_f[kb] += jnp.dot(score_grad, q_b[b], preferred_element_type=f32)
        dq_f[b] += jnp.dot(kt_b[kb], score_grad, preferred_element_type=f32)

    def some_pairs(many, j, carry):
        for more in range(many):
            n = many * j + more
            products(n, more % 2)
            terms(n + 1, (more + 1) % 2)
        return carry

    @pl.when(pairs > 0)
    def _():
        terms(0, 0)

    done = jnp.int32(0)
    for many in DEEP:
        lax.fori_loop(done // many, pairs // many, functools.partial(some_pairs, many), 0)
        done = pairs // many * many

    @pl.when(pairs % 2 == 1)
    def _():
        products(pairs - 1, 0)

    slot = lax.broadcasted_iota(jnp.int32, (cap, 1), 0)

    def widen_keys(b, carry):
        rows = pl.ds(pl.multiple_of(b * block_keys, block_keys), block_keys)
        k_f[rows, :] = dk_f[b] * root
        v_f[rows, :] = dv_f[b]
        return carry

    lax.fori_loop(0, key_blocks, widen_keys, 0)

    def unpack_keys(step, carry):
        for more in range(4):
            shard = step * 4 + more
            zz, yy = shard % z_count, shard // z_count
            rows = pl.ds(shard_start[shard], cap)
            held = slot < count_of(shard)
            dk_out[zz, yy] = jnp.where(held, k_f[rows, :], 0.0).astype(bf16)
            dv_out[zz, yy] = jnp.where(held, v_f[rows, :], 0.0).astype(bf16)
        return carry

    lax.fori_loop(0, shard_count // 4, unpack_keys, 0)
    stores = [
        pltpu.make_async_copy(dk_out, dk_hbm, out_sem.at[0]),
        pltpu.make_async_copy(dv_out, dv_hbm, out_sem.at[1]),
        pltpu.make_async_copy(dq_out, dq_hbm, out_sem.at[2]),
    ]
    stores[0].start()
    stores[1].start()

    def turn_rows(b, carry):
        rows = pl.ds(pl.multiple_of(b * block_rows, block_rows), block_rows)
        turned = dq_f[b].T * root
        for h in range(GROUP):
            row_f[h, rows, :] = turned[h * block_rows : (h + 1) * block_rows, :]
        return carry

    lax.fori_loop(0, row_blocks, turn_rows, 0)

    for yy in range(y_count):
        rows = pl.ds(row_start[yy], cap)
        for h in range(GROUP):
            grad = jnp.where(slot < live[yy], row_f[h, rows, :], 0.0)
            dq_out[yy, :, h * HD : (h + 1) * HD] = grad.astype(bf16)

    stores[2].start()
    for store in stores:
        store.wait()


def attention(y_count, z_count, counts, q_in, do_in, de_in, k_in, v_in):
    cap = q_in.shape[1]
    block_rows, block_keys = 64, 256
    lanes = GROUP * block_rows
    most = y_count * cap
    row_blocks = most // block_rows
    key_blocks = KEEP // block_keys
    anywhere = pl.BlockSpec(memory_space=pl.ANY)
    bf16, f32 = jnp.bfloat16, jnp.float32
    shape = jax.ShapeDtypeStruct
    return pl.pallas_call(
        functools.partial(attention_kernel, y_count, z_count, block_rows, block_keys),
        out_shape=(
            shape((y_count, cap, WIDE), bf16),
            shape((z_count, y_count, cap, HD), bf16),
            shape((z_count, y_count, cap, HD), bf16),
        ),
        in_specs=[pl.BlockSpec(memory_space=pltpu.SMEM)] + [anywhere] * 5,
        out_specs=(anywhere,) * 3,
        scratch_shapes=[
            pltpu.VMEM((y_count, cap, WIDE), bf16),
            pltpu.VMEM((y_count, cap, WIDE), bf16),
            pltpu.VMEM((y_count, GROUP, cap), f32),
            pltpu.VMEM((z_count, y_count, cap, HD), bf16),
            pltpu.VMEM((z_count, y_count, cap, HD), bf16),
            pltpu.VMEM((y_count, cap, WIDE), bf16),
            pltpu.VMEM((z_count, y_count, cap, HD), bf16),
            pltpu.VMEM((z_count, y_count, cap, HD), bf16),
            pltpu.SemaphoreType.DMA((5,)),
            pltpu.SemaphoreType.DMA((3,)),
            pltpu.VMEM((GROUP, most + cap, HD), f32),
            pltpu.VMEM((GROUP, most + cap, HD), f32),
            pltpu.VMEM((most + cap, HD), f32),
            pltpu.VMEM((row_blocks + 1, lanes, HD), bf16),
            pltpu.VMEM((row_blocks + 1, lanes, HD), bf16),
            pltpu.VMEM((row_blocks + 1, 1, lanes), f32),
            pltpu.VMEM((KEEP + cap, HD), f32),
            pltpu.VMEM((KEEP + cap, HD), f32),
            pltpu.VMEM((key_blocks, block_keys, HD), bf16),
            pltpu.VMEM((key_blocks, HD, block_keys), bf16),
            pltpu.VMEM((key_blocks, block_keys, HD), bf16),
            pltpu.VMEM((row_blocks * key_blocks + 1, block_keys // 8, 8, lanes), f32),
            pltpu.VMEM((row_blocks * key_blocks + 1, 8, lanes), f32),
            pltpu.VMEM((row_blocks + 1, 8, lanes), f32),
            pltpu.VMEM((row_blocks + 1, 8, lanes), f32),
            pltpu.VMEM((key_blocks, block_keys, HD), f32),
            pltpu.VMEM((key_blocks, block_keys, HD), f32),
            pltpu.VMEM((row_blocks, HD, lanes), f32),
            pltpu.VMEM((block_keys, lanes), f32),
            pltpu.VMEM((block_keys, lanes), f32),
            pltpu.VMEM((block_keys, lanes), bf16),
            pltpu.VMEM((block_keys, lanes), bf16),
            pltpu.VMEM((block_keys, lanes), bf16),
            pltpu.VMEM((block_keys, lanes), bf16),
            pltpu.SMEM((row_blocks * key_blocks + 3,), jnp.int32),
            pltpu.SMEM((row_blocks * key_blocks + 3,), jnp.int32),
            pltpu.SMEM((y_count * z_count,), jnp.int32),
        ],
        compiler_params=pltpu.CompilerParams(vmem_limit_bytes=62 * MIB),
        name="attention",
    )(counts, q_in, do_in, de_in, k_in, v_in)


def scatter_kernel(
    y_count, z_count, dp_count,
    dq_in, dk_hbm, dv_hbm, part,
    dq_out, dk_out, dv_out, router_out, dk_in, dv_in,
    held, fin, dp_held, y_held, z_held, dp_sum, y_sum, dq_own,
    own_sem, q_send, q_recv, ring_send, ring_recv, fin_send, fin_recv, r_send, r_recv,
):
    y, z = place(z_count)
    dp = lax.axis_index("dp")
    f32, bf16 = jnp.float32, jnp.bfloat16

    def at(y_there, z_there):
        return {"seq": y_there * z_count + z_there}

    right, left = (z + 1) % z_count, (z + z_count - 1) % z_count
    y_peers = [(y + step) % y_count for step in range(1, y_count)]
    z_peers = [(z + step) % z_count for step in range(1, z_count)]
    dp_peers = [(dp + step) % dp_count for step in range(1, dp_count)]
    peers = [at(other, z) for other in y_peers] + [at(y, other) for other in z_peers]
    peers += [{"dp": other} for other in dp_peers]
    greet(peers)

    def wide(ref, g):
        return ref.at[:, pl.ds(pl.multiple_of(g * WIDE, WIDE), WIDE)]

    def narrow(ref, g):
        return ref.at[:, pl.ds(pl.multiple_of(g * HD, HD), HD)]

    own_in = [
        pltpu.make_async_copy(dk_hbm, dk_in, own_sem.at[1]),
        pltpu.make_async_copy(dv_hbm, dv_in, own_sem.at[2]),
        pltpu.make_async_copy(dq_in.at[y], dq_own, own_sem.at[0]),
    ]
    for copy in own_in:
        copy.start()
    pl.semaphore_wait(pltpu.get_barrier_semaphore(), len(peers))

    plan = ring_plan(z_count)
    mine = (dk_in, dv_in)
    apart = (dk_hbm, dv_hbm)

    def ring_copy(lane, step):
        array, way, steps = plan[lane]
        block = (z + way * (steps - step) + z_count) % z_count
        there = at(y, right if way == 1 else left)
        source = apart[array].at[block] if step == 0 else held.at[lane, step - 1]
        return remote(source, held.at[lane, step], ring_send.at[lane, step], ring_recv.at[lane, step], there)

    def forward(step):
        for lane, (array, way, steps) in enumerate(plan):
            if step < steps:
                if step > 0:
                    ring_copy(lane, step - 1).wait_recv()
                    block = (z + way * (steps - step) + z_count) % z_count
                    for g in range(y_count):
                        total = held[lane, step - 1, g].astype(f32) + mine[array][block, g].astype(f32)
                        held[lane, step - 1, g] = total.astype(bf16)
                ring_copy(lane, step).start()

    forward(0)
    sends = []
    for i, other in enumerate(y_peers):
        sends.append(remote(dq_in.at[other], wide(dq_out, y), q_send.at[i], q_recv.at[i], at(other, z)))
        sends[-1].start()
    for copy in own_in:
        copy.wait()
    own = [pltpu.make_async_copy(dq_own, wide(dq_out, y), own_sem.at[0])]
    own[0].start()

    def share(first, source_of, held_ref, peers_there, me):
        copies = []
        for i, there in enumerate(peers_there):
            copies.append(remote(source_of(i), held_ref.at[me], r_send.at[first + i], r_recv.at[first + i], there))
            copies[-1].start()
        return copies

    over_dp = share(0, lambda i: part.at[dp_peers[i]], dp_held, [{"dp": other} for other in dp_peers], dp)
    forward(1)
    for copy in over_dp:
        copy.wait()
    total = part[dp]
    for other in dp_peers:
        total = total + dp_held[other]
    dp_sum[...] = total
    over_y = share(dp_count - 1, lambda i: dp_sum, y_held, [at(other, z) for other in y_peers], y)
    forward(2)
    for copy in over_y:
        copy.wait()
    for other in y_peers:
        total = total + y_held[other]
    y_sum[...] = total
    over_z = share(
        dp_count + y_count - 2, lambda i: y_sum, z_held, [at(y, other) for other in z_peers], z
    )
    for step in range(3, max(p[2] for p in plan)):
        forward(step)
    for copy in over_z:
        copy.wait()
    for other in z_peers:
        total = total + z_held[other]
    router_out[...] = total

    ends = []
    for array, target in ((0, dk_out), (1, dv_out)):
        lanes = [lane for lane in range(4) if plan[lane][0] == array]
        for lane in lanes:
            ring_copy(lane, plan[lane][2] - 1).wait_recv()
        for g in range(y_count):
            total = mine[array][z, g].astype(f32)
            for lane in lanes:
                total = total + held[lane, plan[lane][2] - 1, g].astype(f32)
            fin[array, g] = total.astype(bf16)
        for i, other in enumerate(y_peers):
            ends.append(
                remote(
                    fin.at[array, other],
                    narrow(target, y),
                    fin_send.at[array, i],
                    fin_recv.at[array, i],
                    at(other, z),
                )
            )
            ends[-1].start()
        own.append(pltpu.make_async_copy(fin.at[array, y], narrow(target, y), own_sem.at[1 + array]))
        own[-1].start()
    for lane, (array, way, steps) in enumerate(plan):
        for step in range(steps):
            ring_copy(lane, step).wait_send()
    for copy in own + sends + ends:
        copy.wait()


def scatter(y_count, z_count, dp_count, dq_in, dk_in, dv_in, part):
    cap = dq_in.shape[1]
    longer = z_count // 2
    small = part.shape[1:]
    anywhere = pl.BlockSpec(memory_space=pl.ANY)
    vmem = pl.BlockSpec(memory_space=pltpu.VMEM)
    bf16, f32 = jnp.bfloat16, jnp.float32
    shape = jax.ShapeDtypeStruct
    router_copies = dp_count + y_count + z_count - 3
    return pl.pallas_call(
        functools.partial(scatter_kernel, y_count, z_count, dp_count),
        out_shape=(
            shape((cap, HEADS * HD), bf16),
            shape((cap, KV * HD), bf16),
            shape((cap, KV * HD), bf16),
            shape(small, f32),
        ),
        in_specs=[anywhere, anywhere, anywhere, vmem],
        out_specs=(anywhere, anywhere, anywhere, vmem),
        scratch_shapes=[
            pltpu.VMEM((z_count, y_count, cap, HD), bf16),
            pltpu.VMEM((z_count, y_count, cap, HD), bf16),
            pltpu.VMEM((4, longer, y_count, cap, HD), bf16),
            pltpu.VMEM((2, y_count, cap, HD), bf16),
            pltpu.VMEM((dp_count,) + small, f32),
            pltpu.VMEM((y_count,) + small, f32),
            pltpu.VMEM((z_count,) + small, f32),
            pltpu.VMEM(small, f32),
            pltpu.VMEM(small, f32),
            pltpu.VMEM((cap, WIDE), bf16),
            pltpu.SemaphoreType.DMA((3,)),
            pltpu.SemaphoreType.DMA((y_count - 1,)),
            pltpu.SemaphoreType.DMA((y_count - 1,)),
            pltpu.SemaphoreType.DMA((4, longer)),
            pltpu.SemaphoreType.DMA((4, longer)),
            pltpu.SemaphoreType.DMA((2, y_count - 1)),
            pltpu.SemaphoreType.DMA((2, y_count - 1)),
            pltpu.SemaphoreType.DMA((router_copies,)),
            pltpu.SemaphoreType.DMA((router_copies,)),
        ],
        compiler_params=pltpu.CompilerParams(
            collective_id=1, has_side_effects=True, vmem_limit_bytes=63 * MIB
        ),
        name="scatter",
    )(dq_in, dk_in, dv_in, part)


def result_kernel(
    dq_in, dk_in, dv_in, router, dq_out, dk_out, dv_out, share, dq_v, dk_v, dv_v, in_sem, out_sem
):
    moves = []
    rows = dq_v.shape[1]
    for i in range(dq_v.shape[0]):
        part = pl.ds(i * rows, rows)
        moves.append((dq_in.at[part], dq_v.at[i], dq_out.at[part]))
    moves += [(dk_in, dk_v, dk_out), (dv_in, dv_v, dv_out)]
    loads = [pltpu.make_async_copy(a, b, in_sem.at[i]) for i, (a, b, _) in enumerate(moves)]
    stores = [pltpu.make_async_copy(b, c, out_sem.at[i]) for i, (_, b, c) in enumerate(moves)]
    for load in loads:
        load.start()
    first = lax.axis_index("seq") * share.shape[1]
    lane = lax.broadcasted_iota(jnp.int32, (1, HD), 1)
    here = jnp.zeros((1, HD), jnp.float32)
    for row in range(router.shape[0]):
        turned = pltpu.roll(router[row : row + 1, :], (HD - first % HD) % HD, 1)
        here = jnp.where((first + lane) // HD == row, turned, here)
    share[...] = here[:, : share.shape[1]]
    for load, store in zip(loads, stores):
        load.wait()
        store.start()
    for store in stores:
        store.wait()


def results(share, dq, dk, dv, router):
    vmem = pl.BlockSpec(memory_space=pltpu.VMEM)
    anywhere = pl.BlockSpec(memory_space=pl.ANY)
    pieces = 4
    shape = jax.ShapeDtypeStruct
    return pl.pallas_call(
        result_kernel,
        out_shape=tuple(shape(x.shape, x.dtype) for x in (dq, dk, dv)) + (shape((1, share), jnp.float32),),
        in_specs=[anywhere] * 3 + [vmem],
        out_specs=(anywhere,) * 3 + (vmem,),
        scratch_shapes=[
            pltpu.VMEM((pieces, dq.shape[0] // pieces, dq.shape[1]), dq.dtype),
            pltpu.VMEM(dk.shape, dk.dtype),
            pltpu.VMEM(dv.shape, dv.dtype),
            pltpu.SemaphoreType.DMA((pieces + 2,)),
            pltpu.SemaphoreType.DMA((pieces + 2,)),
        ],
        compiler_params=pltpu.CompilerParams(vmem_limit_bytes=63 * MIB),
        name="results",
    )(dq, dk, dv, router)


def on_device(tokens, router_weight, routes, counts, query, key_in, value_in, attn_out, grad_out):
    y_count = KV
    z_count = lax.axis_size("seq") // y_count
    dp_count = lax.axis_size("dp")
    width = tokens.shape[2]
    q_all, do_all, de_all, k_all, v_all, c_all, part = gather(
        y_count, z_count, dp_count, tokens[0], router_weight[None], routes, counts,
        query[0], key_in[0], value_in[0], attn_out[0], grad_out[0],
    )
    dq, dk, dv = attention(y_count, z_count, c_all, q_all, do_all, de_all, k_all, v_all)
    dq, dk, dv, router = scatter(y_count, z_count, dp_count, dq, dk, dv, part)
    share = width // (dp_count * y_count * z_count)
    dq, dk, dv, router = results(share, dq, dk, dv, router)
    return (dq[None], dk[None], dv[None], router[0])


def solution(mesh):
    rows = P("dp", "seq", None)
    return jax.shard_map(
        on_device,
        mesh=mesh,
        in_specs=(rows, P(), P("dp", "seq"), P("dp", "seq"), rows, rows, rows, rows, rows),
        out_specs=(rows, rows, rows, P(("dp", "seq"))),
        check_vma=False,
    )
```

```python
import functools
import math

import jax
import jax.numpy as jnp
from jax import lax
from jax.experimental import pallas as pl
from jax.experimental.pallas import tpu as pltpu
from jax.sharding import PartitionSpec as P

HEADS = 32
KV = 4
HD = 128
GROUP = HEADS // KV
WIDE = GROUP * HD
KEEP = 2048
SUB_LANES = 128
DEEP = (8, 4, 2)
NEGATIVE = -1e30
MESH = pl.DeviceIdType.MESH
MIB = 1024 * 1024


def place(z_count):
    me = lax.axis_index("seq")
    return me // z_count, me % z_count


def remote(src, dst, send_sem, recv_sem, device):
    return pltpu.make_async_remote_copy(
        src_ref=src,
        dst_ref=dst,
        send_sem=send_sem,
        recv_sem=recv_sem,
        device_id=device,
        device_id_type=MESH,
    )


def greet(devices):
    barrier = pltpu.get_barrier_semaphore()
    for device in devices:
        pl.semaphore_signal(barrier, inc=1, device_id=device, device_id_type=MESH)


def ring_plan(z_count):
    longer = z_count // 2
    shorter = z_count - 1 - longer
    return ((0, 1, longer), (1, -1, longer), (1, 1, shorter), (0, -1, shorter))


def gather_kernel(
    y_count, z_count, chunks,
    tokens, weight, routes, counts, query, key_in, value_in, attn_out, grad_out,
    q_all, do_all, de_all, k_all, v_all, c_all, part,
    tok_v, cot_v, attn_v, dout_v, de_v, cnt_v, picked_v, q_own, k_own, v_own,
    tok_sem, in_sem, own_sem, y_send, y_recv, ring_send, ring_recv, c_send, c_recv,
):
    y, z = place(z_count)
    cap = query.shape[0]
    tok_count = tokens.shape[0]
    chunk = tokens.shape[1] // chunks

    def at(y_there, z_there):
        return {"seq": y_there * z_count + z_there}

    right, left = (z + 1) % z_count, (z + z_count - 1) % z_count
    y_peers = [(y + step) % y_count for step in range(1, y_count)]
    greet([at(other, z) for other in y_peers] + [at(y, right), at(y, left)])

    cnt_v[...] = jnp.full(cnt_v.shape, counts[0, 0], jnp.int32)

    def wide(ref, g):
        return ref.at[:, pl.ds(pl.multiple_of(g * WIDE, WIDE), WIDE)]

    def narrow(ref, g):
        return ref.at[:, pl.ds(pl.multiple_of(g * HD, HD), HD)]

    own_in = [
        pltpu.make_async_copy(narrow(key_in, y), k_own, own_sem.at[0]),
        pltpu.make_async_copy(narrow(value_in, y), v_own, own_sem.at[1]),
        pltpu.make_async_copy(wide(query, y), q_own, own_sem.at[2]),
    ]
    for copy in own_in:
        copy.start()
    loads = []
    for c in range(chunks):
        loads.append(pltpu.make_async_copy(tokens.at[:, pl.ds(c * chunk, chunk)], tok_v.at[c], tok_sem.at[c]))
        loads[-1].start()
    rows_in = []
    for g in range(y_count):
        for a, (source, target) in enumerate(((grad_out, cot_v), (attn_out, attn_v))):
            rows_in.append(
                pltpu.make_async_copy(source.at[:, pl.ds(g * WIDE, WIDE)], target.at[g], in_sem.at[a, g])
            )
            rows_in[-1].start()
    pl.semaphore_wait(pltpu.get_barrier_semaphore(), y_count + 1)

    first = []
    for i, other in enumerate(y_peers):
        there = at(other, z)
        for a, (source, target) in enumerate(
            (
                (narrow(key_in, other), k_all.at[z, y]),
                (narrow(value_in, other), v_all.at[z, y]),
                (cnt_v, c_all.at[z, y]),
            )
        ):
            first.append(remote(source, target, y_send.at[a, i], y_recv.at[a, i], there))
            first[-1].start()
    late = []
    for i, other in enumerate(y_peers):
        late.append(remote(wide(query, other), q_all.at[y], y_send.at[3, i], y_recv.at[3, i], at(other, z)))
        late[-1].start()
    own = [
        pltpu.make_async_copy(k_own, k_all.at[z, y], own_sem.at[0]),
        pltpu.make_async_copy(v_own, v_all.at[z, y], own_sem.at[1]),
        pltpu.make_async_copy(cnt_v, c_all.at[z, y], own_sem.at[3]),
        pltpu.make_async_copy(q_own, q_all.at[y], own_sem.at[2]),
    ]
    for copy in own_in:
        copy.wait()
    for copy in own:
        copy.start()
    for copy in own[:3]:
        copy.wait()
    for copy in first:
        copy.wait_recv()

    plan = ring_plan(z_count)
    held = (k_all, v_all)

    def ring_copy(lane, step):
        array, way, _ = plan[lane]
        block = (z - way * step + 2 * z_count) % z_count
        there = at(y, right if way == 1 else left)
        ref = held[array].at[block]
        return remote(ref, ref, ring_send.at[lane, step], ring_recv.at[lane, step], there)

    def count_copy(way, step):
        block = (z - way * step + 2 * z_count) % z_count
        there = at(y, right if way == 1 else left)
        ref = c_all.at[block]
        side = (1 - way) // 2
        return remote(ref, ref, c_send.at[side, step], c_recv.at[side, step], there)

    def forward(step):
        for lane, (array, way, steps) in enumerate(plan):
            if 0 < step <= steps:
                ring_copy(lane, step - 1).wait_recv()
            if step < steps:
                ring_copy(lane, step).start()
            if array == 0:
                if 0 < step <= steps:
                    count_copy(way, step - 1).wait_recv()
                if step < steps:
                    count_copy(way, step).start()

    forward(0)

    token_at = lax.broadcasted_iota(jnp.int32, (tok_count, cap), 0)
    hot = jnp.where(token_at == routes[...], 1.0, 0.0).T.astype(jnp.bfloat16)
    logit = jnp.zeros((cap, HD), jnp.float32)
    for c in range(chunks):
        loads[c].wait()
        picked = jnp.dot(hot, tok_v[c], preferred_element_type=jnp.float32)
        picked_v[c] = picked
        scaled = picked * weight[:, c * chunk : (c + 1) * chunk]
        for t in range(chunk // HD):
            logit = logit + scaled[:, t * HD : (t + 1) * HD]
    logit = jnp.sum(logit, axis=1, keepdims=True)
    gate = 1.0 / (1.0 + jnp.exp(-logit))
    live = lax.broadcasted_iota(jnp.int32, (cap, 1), 0) < counts[0, 0]
    kept = jnp.where(live, gate, 0.0)
    for copy in rows_in:
        copy.wait()

    lane_at = lax.broadcasted_iota(jnp.int32, (cap, HD), 1)

    def scale_group(other):
        gate_sum = jnp.zeros((cap, HD), jnp.float32)
        deltas = jnp.zeros((cap, HD), jnp.float32)
        for h in range(GROUP):
            cols = slice(h * HD, (h + 1) * HD)
            cot = cot_v[other, :, cols].astype(jnp.float32)
            out = attn_v[other, :, cols].astype(jnp.float32)
            dout = (kept * cot).astype(jnp.bfloat16)
            dout_v[other, :, cols] = dout
            gate_sum = gate_sum + cot * out
            delta = jnp.sum(dout.astype(jnp.float32) * out, axis=1, keepdims=True)
            deltas = jnp.where(lane_at == h, delta, deltas)
        de_v[other] = deltas.T[:GROUP]
        return gate_sum

    gate_sum = jnp.zeros((cap, HD), jnp.float32)
    for i, other in enumerate(y_peers):
        gate_sum = gate_sum + scale_group(other)
        for a, (source, target) in enumerate(((dout_v, do_all), (de_v, de_all))):
            late.append(
                remote(source.at[other], target.at[y], y_send.at[4 + a, i], y_recv.at[4 + a, i], at(other, z))
            )
            late[-1].start()
    forward(1)
    gate_sum = gate_sum + scale_group(y)
    mine = [
        pltpu.make_async_copy(dout_v.at[y], do_all.at[y], own_sem.at[4]),
        pltpu.make_async_copy(de_v.at[y], de_all.at[y], own_sem.at[5]),
    ]
    for copy in mine:
        copy.start()
    forward(2)
    gate_grad = jnp.sum(gate_sum, axis=1, keepdims=True)
    logit_grad = jnp.where(live, gate_grad * gate * (1.0 - gate), 0.0)
    segments = part.shape[1]
    for c in range(chunks):
        terms = jnp.sum(logit_grad * picked_v[c], axis=0, keepdims=True)
        for t in range(chunk // HD):
            n = c * (chunk // HD) + t
            part[n // segments, n % segments : n % segments + 1, :] = terms[:, t * HD : (t + 1) * HD]
    for step in range(3, max(p[2] for p in plan) + 1):
        forward(step)
    own[3].wait()
    for copy in mine:
        copy.wait()
    for copy in first:
        copy.wait_send()
    for copy in late:
        copy.wait()
    for lane, (array, way, steps) in enumerate(plan):
        for step in range(steps):
            ring_copy(lane, step).wait_send()
            if array == 0:
                count_copy(way, step).wait_send()


def gather(y_count, z_count, dp_count, tokens, weight, routes, counts, query, key_in, value_in, attn_out, grad_out):
    cap = query.shape[0]
    tok_count, width = tokens.shape
    chunks = 5
    longer = z_count // 2
    anywhere = pl.BlockSpec(memory_space=pl.ANY)
    vmem = pl.BlockSpec(memory_space=pltpu.VMEM)
    smem = pl.BlockSpec(memory_space=pltpu.SMEM)
    bf16, f32 = jnp.bfloat16, jnp.float32
    shape = jax.ShapeDtypeStruct
    return pl.pallas_call(
        functools.partial(gather_kernel, y_count, z_count, chunks),
        out_shape=(
            shape((y_count, cap, WIDE), bf16),
            shape((y_count, cap, WIDE), bf16),
            shape((y_count, GROUP, cap), f32),
            shape((z_count, y_count, cap, HD), bf16),
            shape((z_count, y_count, cap, HD), bf16),
            shape((z_count, y_count, 1, HD), jnp.int32),
            shape((dp_count, width // HD // dp_count, HD), f32),
        ),
        in_specs=[anywhere, vmem, vmem, smem] + [anywhere] * 5,
        out_specs=(anywhere,) * 6 + (vmem,),
        scratch_shapes=[
            pltpu.VMEM((chunks, tok_count, width // chunks), bf16),
            pltpu.VMEM((y_count, cap, WIDE), bf16),
            pltpu.VMEM((y_count, cap, WIDE), bf16),
            pltpu.VMEM((y_count, cap, WIDE), bf16),
            pltpu.VMEM((y_count, GROUP, cap), f32),
            pltpu.VMEM((1, HD), jnp.int32),
            pltpu.VMEM((chunks, cap, width // chunks), f32),
            pltpu.VMEM((cap, WIDE), bf16),
            pltpu.VMEM((cap, HD), bf16),
            pltpu.VMEM((cap, HD), bf16),
            pltpu.SemaphoreType.DMA((chunks,)),
            pltpu.SemaphoreType.DMA((2, y_count)),
            pltpu.SemaphoreType.DMA((6,)),
            pltpu.SemaphoreType.DMA((6, y_count - 1)),
            pltpu.SemaphoreType.DMA((6, y_count - 1)),
            pltpu.SemaphoreType.DMA((4, longer)),
            pltpu.SemaphoreType.DMA((4, longer)),
            pltpu.SemaphoreType.DMA((2, longer)),
            pltpu.SemaphoreType.DMA((2, longer)),
        ],
        compiler_params=pltpu.CompilerParams(
            collective_id=0, has_side_effects=True, vmem_limit_bytes=63 * MIB
        ),
        name="gather",
    )(tokens, weight, routes, counts, query, key_in, value_in, attn_out, grad_out)


def attention_kernel(
    y_count, z_count, block_rows, block_keys,
    counts, q_hbm, do_hbm, de_hbm, k_hbm, v_hbm,
    dq_hbm, dk_hbm, dv_hbm,
    q_in, do_in, de_in, k_in, v_in, dk_out, dv_out, in_sem, out_sem,
    q_b, do_b, de_b, k_f, v_f, k_b, kt_b, v_b, exps, tops, best, total, dk_f, dv_f, dq_f,
    s_even, s_odd, p_even, p_odd, ds_even, ds_odd, pair_row, pair_key, shard_start,
):
    loads = []
    for i, (source, target) in enumerate(
        ((k_hbm, k_in), (v_hbm, v_in), (q_hbm, q_in), (do_hbm, do_in), (de_hbm, de_in))
    ):
        loads.append(pltpu.make_async_copy(source, target, in_sem.at[i]))
        loads[-1].start()
    cap = q_in.shape[1]
    z = lax.axis_index("seq") % z_count
    shard_count = y_count * z_count
    lanes = GROUP * block_rows
    key_blocks = KEEP // block_keys
    root = 1.0 / math.sqrt(HD)
    power = root * math.log2(math.e)
    f32, bf16 = jnp.float32, jnp.bfloat16
    s_b, p_b, ds_b = (s_even, s_odd), (p_even, p_odd), (ds_even, ds_odd)

    def count_of(shard):
        return counts[shard % z_count, shard // z_count, 0, 0]

    keys_before = jnp.int32(0)
    for shard in range(shard_count):
        shard_start[shard] = keys_before
        keys_before = keys_before + count_of(shard)

    def pack(source, target, step, carry):
        for more in range(4):
            shard = step * 4 + more
            rows = pl.ds(shard_start[shard], cap)
            target[rows, :] = source[shard % z_count, shard // z_count].astype(f32)
        return carry

    loads[0].wait()
    lax.fori_loop(0, shard_count // 4, functools.partial(pack, k_in, k_f), 0)
    loads[1].wait()
    lax.fori_loop(0, shard_count // 4, functools.partial(pack, v_in, v_f), 0)

    def narrow_keys(b, carry):
        rows = pl.ds(b * block_keys, block_keys)
        k_b[b] = k_f[rows, :].astype(bf16)
        kt_b[b] = k_f[rows, :].T.astype(bf16)
        v_b[b] = v_f[rows, :].astype(bf16)
        dk_f[b] = jnp.zeros((block_keys, HD), f32)
        dv_f[b] = jnp.zeros((block_keys, HD), f32)
        return carry

    lax.fori_loop(0, key_blocks, narrow_keys, 0)

    halves = cap // block_rows
    row_blocks = y_count * halves

    def first_place(b):
        return shard_start[b // halves * z_count + z] + b % halves * block_rows

    def live_rows(b):
        return jnp.clip(counts[z, b // halves, 0, 0] - b % halves * block_rows, 0, block_rows)

    for load in loads[2:]:
        load.wait()
    for b in range(row_blocks):
        here = slice(b % halves * block_rows, (b % halves + 1) * block_rows)
        for h in range(GROUP):
            mine, cols = slice(h * block_rows, (h + 1) * block_rows), slice(h * HD, (h + 1) * HD)
            q_b[b, mine, :] = q_in[b // halves, here, cols]
            do_b[b, mine, :] = do_in[b // halves, here, cols]
            de_b[b, :, mine] = de_in[b // halves, h : h + 1, here]

    nt = (((1,), (1,)), ((), ()))

    def list_pairs(masked, count):
        def of_rows(b, count):
            full = (first_place(b) + 1) // block_keys
            used = (first_place(b) + live_rows(b) - 1) // block_keys + 1
            used = jnp.where(live_rows(b) > 0, used, 0)
            full = jnp.minimum(full, used)

            def add(kb, count):
                pair_row[count] = b
                pair_key[count] = kb
                return count + 1

            first, last = (full, used) if masked else (0, full)
            return lax.fori_loop(first, last, add, count)

        return lax.fori_loop(0, row_blocks, of_rows, count)

    whole_pairs = list_pairs(False, jnp.int32(0))
    pairs = list_pairs(True, whole_pairs)
    for more in range(3):
        pair_row[pairs + more] = q_b.shape[0] - 1
        pair_key[pairs + more] = 0

    def start_rows(b, carry):
        best[b] = jnp.full((8, lanes), NEGATIVE, f32)
        total[b] = jnp.zeros((8, lanes), f32)
        dq_f[b] = jnp.zeros((HD, lanes), f32)
        return carry

    lax.fori_loop(0, row_blocks, start_rows, 0)

    def raw(n, slot):
        s_b[slot][:, :] = lax.dot_general(
            k_b[pair_key[n]], q_b[pair_row[n]], nt, preferred_element_type=f32
        )

    def grow(masked, n, slot):
        b, kb = pair_row[n], pair_key[n]
        for part in range(lanes // SUB_LANES):
            cols = slice(part * SUB_LANES, (part + 1) * SUB_LANES)
            block = s_b[slot][:, cols] * power
            if masked:
                lane = lax.broadcasted_iota(jnp.int32, (1, SUB_LANES), 1)
                row_place = first_place(b) + lane % block_rows - kb * block_keys
                key_place = lax.broadcasted_iota(jnp.int32, (block_keys, SUB_LANES), 0)
                block = jnp.where(key_place <= row_place, block, NEGATIVE)
            block = block.reshape(block_keys // 8, 8, SUB_LANES)
            before = best[b, :, cols]
            after = jnp.maximum(before, jnp.max(block, axis=0))
            grown = jnp.exp2(block - after)
            exps[n, :, :, cols] = grown
            tops[n, :, cols] = after
            best[b, :, cols] = after
            total[b, :, cols] = total[b, :, cols] * jnp.exp2(before - after) + jnp.sum(grown, axis=0)

    def some_scores(masked, many, j, carry):
        for more in range(many):
            n = many * j + more
            raw(n + 1, (more + 1) % 2)
            grow(masked, n, more % 2)
        return carry

    raw(0, 0)
    done = jnp.int32(0)
    for many in DEEP:
        lax.fori_loop(done // many, whole_pairs // many, functools.partial(some_scores, False, many), 0)
        done = whole_pairs // many * many
    lax.fori_loop(done // 2, (pairs + 1) // 2, functools.partial(some_scores, True, 2), 0)

    def finish_rows(b, carry):
        top = jnp.max(best[b], axis=0, keepdims=True)
        summed = jnp.sum(total[b] * jnp.exp2(best[b] - top), axis=0, keepdims=True)
        best[b] = jnp.broadcast_to(top + jnp.log2(summed), (8, lanes))
        return carry

    lax.fori_loop(0, row_blocks, finish_rows, 0)

    def terms(n, slot):
        b, kb = pair_row[n], pair_key[n]
        scale = jnp.exp2(tops[n] - best[b])
        prob = (exps[n] * scale).reshape(block_keys, lanes)
        prob_grad = lax.dot_general(v_b[kb], do_b[b], nt, preferred_element_type=f32)
        p_b[slot][:, :] = prob.astype(bf16)
        ds_b[slot][:, :] = (prob * (prob_grad - de_b[b])).astype(bf16)

    def products(n, slot):
        b, kb = pair_row[n], pair_key[n]
        score_grad = ds_b[slot][:, :]
        dv_f[kb] += jnp.dot(p_b[slot][:, :], do_b[b], preferred_element_type=f32)
        dk_f[kb] += jnp.dot(score_grad, q_b[b], preferred_element_type=f32)
        dq_f[b] += jnp.dot(kt_b[kb], score_grad, preferred_element_type=f32)

    def some_pairs(many, j, carry):
        for more in range(many):
            n = many * j + more
            products(n, more % 2)
            terms(n + 1, (more + 1) % 2)
        return carry

    @pl.when(pairs > 0)
    def _():
        terms(0, 0)

    done = jnp.int32(0)
    for many in DEEP:
        lax.fori_loop(done // many, pairs // many, functools.partial(some_pairs, many), 0)
        done = pairs // many * many

    @pl.when(pairs % 2 == 1)
    def _():
        products(pairs - 1, 0)

    stores = [
        pltpu.make_async_copy(dq_f, dq_hbm, out_sem.at[0]),
        pltpu.make_async_copy(dk_out, dk_hbm, out_sem.at[1]),
        pltpu.make_async_copy(dv_out, dv_hbm, out_sem.at[2]),
    ]
    stores[0].start()
    slot = lax.broadcasted_iota(jnp.int32, (cap, 1), 0)

    def widen_keys(b, carry):
        rows = pl.ds(pl.multiple_of(b * block_keys, block_keys), block_keys)
        k_f[rows, :] = dk_f[b] * root
        v_f[rows, :] = dv_f[b]
        return carry

    lax.fori_loop(0, key_blocks, widen_keys, 0)

    def unpack_keys(step, carry):
        for more in range(4):
            shard = step * 4 + more
            zz, yy = shard % z_count, shard // z_count
            rows = pl.ds(shard_start[shard], cap)
            held = slot < count_of(shard)
            dk_out[zz, yy] = jnp.where(held, k_f[rows, :], 0.0).astype(bf16)
            dv_out[zz, yy] = jnp.where(held, v_f[rows, :], 0.0).astype(bf16)
        return carry

    lax.fori_loop(0, shard_count // 4, unpack_keys, 0)
    for store in stores[1:]:
        store.start()
    for store in stores:
        store.wait()


def attention(y_count, z_count, counts, q_in, do_in, de_in, k_in, v_in):
    cap = q_in.shape[1]
    block_rows, block_keys = 64, 256
    lanes = GROUP * block_rows
    most = y_count * cap
    row_blocks = most // block_rows
    key_blocks = KEEP // block_keys
    anywhere = pl.BlockSpec(memory_space=pl.ANY)
    bf16, f32 = jnp.bfloat16, jnp.float32
    shape = jax.ShapeDtypeStruct
    return pl.pallas_call(
        functools.partial(attention_kernel, y_count, z_count, block_rows, block_keys),
        out_shape=(
            shape((row_blocks, HD, lanes), f32),
            shape((z_count, y_count, cap, HD), bf16),
            shape((z_count, y_count, cap, HD), bf16),
        ),
        in_specs=[pl.BlockSpec(memory_space=pltpu.SMEM)] + [anywhere] * 5,
        out_specs=(anywhere,) * 3,
        scratch_shapes=[
            pltpu.VMEM((y_count, cap, WIDE), bf16),
            pltpu.VMEM((y_count, cap, WIDE), bf16),
            pltpu.VMEM((y_count, GROUP, cap), f32),
            pltpu.VMEM((z_count, y_count, cap, HD), bf16),
            pltpu.VMEM((z_count, y_count, cap, HD), bf16),
            pltpu.VMEM((z_count, y_count, cap, HD), bf16),
            pltpu.VMEM((z_count, y_count, cap, HD), bf16),
            pltpu.SemaphoreType.DMA((5,)),
            pltpu.SemaphoreType.DMA((3,)),
            pltpu.VMEM((row_blocks + 1, lanes, HD), bf16),
            pltpu.VMEM((row_blocks + 1, lanes, HD), bf16),
            pltpu.VMEM((row_blocks + 1, 1, lanes), f32),
            pltpu.VMEM((KEEP + cap, HD), f32),
            pltpu.VMEM((KEEP + cap, HD), f32),
            pltpu.VMEM((key_blocks, block_keys, HD), bf16),
            pltpu.VMEM((key_blocks, HD, block_keys), bf16),
            pltpu.VMEM((key_blocks, block_keys, HD), bf16),
            pltpu.VMEM((row_blocks * key_blocks + 1, block_keys // 8, 8, lanes), f32),
            pltpu.VMEM((row_blocks * key_blocks + 1, 8, lanes), f32),
            pltpu.VMEM((row_blocks + 1, 8, lanes), f32),
            pltpu.VMEM((row_blocks + 1, 8, lanes), f32),
            pltpu.VMEM((key_blocks, block_keys, HD), f32),
            pltpu.VMEM((key_blocks, block_keys, HD), f32),
            pltpu.VMEM((row_blocks, HD, lanes), f32),
            pltpu.VMEM((block_keys, lanes), f32),
            pltpu.VMEM((block_keys, lanes), f32),
            pltpu.VMEM((block_keys, lanes), bf16),
            pltpu.VMEM((block_keys, lanes), bf16),
            pltpu.VMEM((block_keys, lanes), bf16),
            pltpu.VMEM((block_keys, lanes), bf16),
            pltpu.SMEM((row_blocks * key_blocks + 3,), jnp.int32),
            pltpu.SMEM((row_blocks * key_blocks + 3,), jnp.int32),
            pltpu.SMEM((y_count * z_count,), jnp.int32),
        ],
        compiler_params=pltpu.CompilerParams(vmem_limit_bytes=62 * MIB),
        name="attention",
    )(counts, q_in, do_in, de_in, k_in, v_in)


def scatter_kernel(
    y_count, z_count, dp_count,
    dq_hbm, dk_hbm, dv_hbm, part,
    dq_out, dk_out, dv_out, router_out, dq_in, dk_in, dv_in,
    held, fin, dp_held, y_held, z_held, dp_sum, y_sum, dq_v,
    own_sem, q_send, q_recv, ring_send, ring_recv, fin_send, fin_recv, r_send, r_recv,
):
    y, z = place(z_count)
    dp = lax.axis_index("dp")
    f32, bf16 = jnp.float32, jnp.bfloat16

    def at(y_there, z_there):
        return {"seq": y_there * z_count + z_there}

    right, left = (z + 1) % z_count, (z + z_count - 1) % z_count
    y_peers = [(y + step) % y_count for step in range(1, y_count)]
    z_peers = [(z + step) % z_count for step in range(1, z_count)]
    dp_peers = [(dp + step) % dp_count for step in range(1, dp_count)]
    peers = [at(other, z) for other in y_peers] + [at(y, other) for other in z_peers]
    peers += [{"dp": other} for other in dp_peers]
    greet(peers)

    def wide(ref, g):
        return ref.at[:, pl.ds(pl.multiple_of(g * WIDE, WIDE), WIDE)]

    def narrow(ref, g):
        return ref.at[:, pl.ds(pl.multiple_of(g * HD, HD), HD)]

    own_in = [
        pltpu.make_async_copy(dk_hbm, dk_in, own_sem.at[1]),
        pltpu.make_async_copy(dv_hbm, dv_in, own_sem.at[2]),
        pltpu.make_async_copy(dq_hbm, dq_in, own_sem.at[0]),
    ]
    for copy in own_in:
        copy.start()
    for copy in own_in[:2]:
        copy.wait()
    pl.semaphore_wait(pltpu.get_barrier_semaphore(), len(peers))

    plan = ring_plan(z_count)
    mine = (dk_in, dv_in)

    def ring_copy(lane, step):
        array, way, steps = plan[lane]
        block = (z + way * (steps - step) + z_count) % z_count
        there = at(y, right if way == 1 else left)
        source = mine[array].at[block] if step == 0 else held.at[lane, step - 1]
        return remote(source, held.at[lane, step], ring_send.at[lane, step], ring_recv.at[lane, step], there)

    def forward(step):
        for lane, (array, way, steps) in enumerate(plan):
            if step < steps:
                if step > 0:
                    ring_copy(lane, step - 1).wait_recv()
                    block = (z + way * (steps - step) + z_count) % z_count
                    for g in range(y_count):
                        total = held[lane, step - 1, g].astype(f32) + mine[array][block, g].astype(f32)
                        held[lane, step - 1, g] = total.astype(bf16)
                ring_copy(lane, step).start()

    forward(0)
    own_in[2].wait()
    block_rows = dq_in.shape[2] // GROUP
    halves = dq_v.shape[1] // block_rows

    def turn_rows(b, carry):
        rows = pl.ds(pl.multiple_of(b % halves * block_rows, block_rows), block_rows)
        turned = (dq_in[b].T * (1.0 / math.sqrt(HD))).astype(bf16)
        for h in range(GROUP):
            dq_v[b // halves, rows, h * HD : (h + 1) * HD] = turned[h * block_rows : (h + 1) * block_rows, :]
        return carry

    lax.fori_loop(0, dq_in.shape[0], turn_rows, 0)
    sends = []
    for i, other in enumerate(y_peers):
        sends.append(remote(dq_v.at[other], wide(dq_out, y), q_send.at[i], q_recv.at[i], at(other, z)))
        sends[-1].start()
    own = [pltpu.make_async_copy(dq_v.at[y], wide(dq_out, y), own_sem.at[0])]
    own[0].start()

    def share(first, source_of, held_ref, peers_there, me):
        copies = []
        for i, there in enumerate(peers_there):
            copies.append(remote(source_of(i), held_ref.at[me], r_send.at[first + i], r_recv.at[first + i], there))
            copies[-1].start()
        return copies

    over_dp = share(0, lambda i: part.at[dp_peers[i]], dp_held, [{"dp": other} for other in dp_peers], dp)
    forward(1)
    for copy in over_dp:
        copy.wait()
    total = part[dp]
    for other in dp_peers:
        total = total + dp_held[other]
    dp_sum[...] = total
    over_y = share(dp_count - 1, lambda i: dp_sum, y_held, [at(other, z) for other in y_peers], y)
    forward(2)
    for copy in over_y:
        copy.wait()
    for other in y_peers:
        total = total + y_held[other]
    y_sum[...] = total
    over_z = share(
        dp_count + y_count - 2, lambda i: y_sum, z_held, [at(y, other) for other in z_peers], z
    )
    for step in range(3, max(p[2] for p in plan)):
        forward(step)
    for copy in over_z:
        copy.wait()
    for other in z_peers:
        total = total + z_held[other]
    first = lax.axis_index("seq") * router_out.shape[1]
    lane = lax.broadcasted_iota(jnp.int32, (1, HD), 1)
    here = jnp.zeros((1, HD), f32)
    for row in range(total.shape[0]):
        turned = pltpu.roll(total[row : row + 1, :], (HD - first % HD) % HD, 1)
        here = jnp.where((first + lane) // HD == row, turned, here)
    router_out[...] = here[:, : router_out.shape[1]]

    ends = []
    for array, target in ((0, dk_out), (1, dv_out)):
        lanes = [lane for lane in range(4) if plan[lane][0] == array]
        for lane in lanes:
            ring_copy(lane, plan[lane][2] - 1).wait_recv()
        for g in range(y_count):
            total = mine[array][z, g].astype(f32)
            for lane in lanes:
                total = total + held[lane, plan[lane][2] - 1, g].astype(f32)
            fin[array, g] = total.astype(bf16)
        for i, other in enumerate(y_peers):
            ends.append(
                remote(
                    fin.at[array, other],
                    narrow(target, y),
                    fin_send.at[array, i],
                    fin_recv.at[array, i],
                    at(other, z),
                )
            )
            ends[-1].start()
        own.append(pltpu.make_async_copy(fin.at[array, y], narrow(target, y), own_sem.at[1 + array]))
        own[-1].start()
    for lane, (array, way, steps) in enumerate(plan):
        for step in range(steps):
            ring_copy(lane, step).wait_send()
    for copy in own + sends + ends:
        copy.wait()


def scatter(y_count, z_count, dp_count, dq_in, dk_in, dv_in, part):
    share = part.shape[1] * HD // (y_count * z_count)
    cap = dk_in.shape[2]
    longer = z_count // 2
    small = part.shape[1:]
    anywhere = pl.BlockSpec(memory_space=pl.ANY)
    vmem = pl.BlockSpec(memory_space=pltpu.VMEM)
    bf16, f32 = jnp.bfloat16, jnp.float32
    shape = jax.ShapeDtypeStruct
    router_copies = dp_count + y_count + z_count - 3
    return pl.pallas_call(
        functools.partial(scatter_kernel, y_count, z_count, dp_count),
        out_shape=(
            shape((cap, HEADS * HD), bf16),
            shape((cap, KV * HD), bf16),
            shape((cap, KV * HD), bf16),
            shape((1, share), f32),
        ),
        in_specs=[anywhere, anywhere, anywhere, vmem],
        out_specs=(anywhere, anywhere, anywhere, vmem),
        scratch_shapes=[
            pltpu.VMEM(dq_in.shape, f32),
            pltpu.VMEM((z_count, y_count, cap, HD), bf16),
            pltpu.VMEM((z_count, y_count, cap, HD), bf16),
            pltpu.VMEM((4, longer, y_count, cap, HD), bf16),
            pltpu.VMEM((2, y_count, cap, HD), bf16),
            pltpu.VMEM((dp_count,) + small, f32),
            pltpu.VMEM((y_count,) + small, f32),
            pltpu.VMEM((z_count,) + small, f32),
            pltpu.VMEM(small, f32),
            pltpu.VMEM(small, f32),
            pltpu.VMEM((y_count, cap, WIDE), bf16),
            pltpu.SemaphoreType.DMA((3,)),
            pltpu.SemaphoreType.DMA((y_count - 1,)),
            pltpu.SemaphoreType.DMA((y_count - 1,)),
            pltpu.SemaphoreType.DMA((4, longer)),
            pltpu.SemaphoreType.DMA((4, longer)),
            pltpu.SemaphoreType.DMA((2, y_count - 1)),
            pltpu.SemaphoreType.DMA((2, y_count - 1)),
            pltpu.SemaphoreType.DMA((router_copies,)),
            pltpu.SemaphoreType.DMA((router_copies,)),
        ],
        compiler_params=pltpu.CompilerParams(
            collective_id=1, has_side_effects=True, vmem_limit_bytes=63 * MIB
        ),
        name="scatter",
    )(dq_in, dk_in, dv_in, part)


def result_kernel(
    dq_in, dk_in, dv_in, share_in, dq_out, dk_out, dv_out, share_out, dq_v, dk_v, dv_v, share_v, in_sem, out_sem
):
    moves = []
    rows = dq_v.shape[1]
    for i in range(dq_v.shape[0]):
        part = pl.ds(i * rows, rows)
        moves.append((dq_in.at[part], dq_v.at[i], dq_out.at[part]))
    moves += [(dk_in, dk_v, dk_out), (dv_in, dv_v, dv_out), (share_in, share_v, share_out)]
    loads = [pltpu.make_async_copy(a, b, in_sem.at[i]) for i, (a, b, _) in enumerate(moves)]
    stores = [pltpu.make_async_copy(b, c, out_sem.at[i]) for i, (_, b, c) in enumerate(moves)]
    for load in loads:
        load.start()
    for load, store in zip(loads, stores):
        load.wait()
        store.start()
    for store in stores:
        store.wait()


def results(dq, dk, dv, share):
    anywhere = pl.BlockSpec(memory_space=pl.ANY)
    pieces = 4
    shape = jax.ShapeDtypeStruct
    return pl.pallas_call(
        result_kernel,
        out_shape=tuple(shape(x.shape, x.dtype) for x in (dq, dk, dv, share)),
        in_specs=[anywhere] * 4,
        out_specs=(anywhere,) * 4,
        scratch_shapes=[
            pltpu.VMEM((pieces, dq.shape[0] // pieces, dq.shape[1]), dq.dtype),
            pltpu.VMEM(dk.shape, dk.dtype),
            pltpu.VMEM(dv.shape, dv.dtype),
            pltpu.VMEM(share.shape, share.dtype),
            pltpu.SemaphoreType.DMA((pieces + 3,)),
            pltpu.SemaphoreType.DMA((pieces + 3,)),
        ],
        compiler_params=pltpu.CompilerParams(vmem_limit_bytes=63 * MIB),
        name="results",
    )(dq, dk, dv, share)


def on_device(tokens, router_weight, routes, counts, query, key_in, value_in, attn_out, grad_out):
    y_count = KV
    z_count = lax.axis_size("seq") // y_count
    dp_count = lax.axis_size("dp")
    q_all, do_all, de_all, k_all, v_all, c_all, part = gather(
        y_count, z_count, dp_count, tokens[0], router_weight[None], routes, counts,
        query[0], key_in[0], value_in[0], attn_out[0], grad_out[0],
    )
    dq, dk, dv = attention(y_count, z_count, c_all, q_all, do_all, de_all, k_all, v_all)
    dq, dk, dv, router = scatter(y_count, z_count, dp_count, dq, dk, dv, part)
    dq, dk, dv, router = results(dq, dk, dv, router)
    return (dq[None], dk[None], dv[None], router[0])


def solution(mesh):
    rows = P("dp", "seq", None)
    return jax.shard_map(
        on_device,
        mesh=mesh,
        in_specs=(rows, P(), P("dp", "seq"), P("dp", "seq"), rows, rows, rows, rows, rows),
        out_specs=(rows, rows, rows, P(("dp", "seq"))),
        check_vma=False,
    )
```

```python
import functools
import math

import jax
import jax.numpy as jnp
from jax import lax
from jax.experimental import pallas as pl
from jax.experimental.pallas import tpu as pltpu
from jax.sharding import PartitionSpec as P

HEADS = 32
KV = 4
HD = 128
GROUP = HEADS // KV
WIDE = GROUP * HD
KEEP = 2048
SUB_LANES = 128
DEEP = (8, 4, 2)
NEGATIVE = -1e30
MESH = pl.DeviceIdType.MESH
MIB = 1024 * 1024


def place(z_count):
    me = lax.axis_index("seq")
    return me // z_count, me % z_count


def remote(src, dst, send_sem, recv_sem, device):
    return pltpu.make_async_remote_copy(
        src_ref=src,
        dst_ref=dst,
        send_sem=send_sem,
        recv_sem=recv_sem,
        device_id=device,
        device_id_type=MESH,
    )


def greet(devices):
    barrier = pltpu.get_barrier_semaphore()
    for device in devices:
        pl.semaphore_signal(barrier, inc=1, device_id=device, device_id_type=MESH)


def ring_plan(z_count):
    longer = z_count // 2
    shorter = z_count - 1 - longer
    return ((0, 1, longer), (1, -1, longer), (1, 1, shorter), (0, -1, shorter))


def gather_kernel(
    y_count, z_count, chunks,
    tokens, weight, routes, counts, query, key_in, value_in, attn_out, grad_out,
    q_all, do_all, de_all, k_all, v_all, c_all, part,
    tok_v, cot_v, attn_v, dout_v, de_v, cnt_v, picked_v, q_own, k_own, v_own,
    tok_sem, in_sem, own_sem, y_send, y_recv, ring_send, ring_recv, c_send, c_recv,
):
    y, z = place(z_count)
    cap = query.shape[0]
    tok_count = tokens.shape[0]
    chunk = tokens.shape[1] // chunks

    def at(y_there, z_there):
        return {"seq": y_there * z_count + z_there}

    right, left = (z + 1) % z_count, (z + z_count - 1) % z_count
    y_peers = [(y + step) % y_count for step in range(1, y_count)]
    greet([at(other, z) for other in y_peers] + [at(y, right), at(y, left)])

    cnt_v[...] = jnp.full(cnt_v.shape, counts[0, 0], jnp.int32)

    def wide(ref, g):
        return ref.at[:, pl.ds(pl.multiple_of(g * WIDE, WIDE), WIDE)]

    def narrow(ref, g):
        return ref.at[:, pl.ds(pl.multiple_of(g * HD, HD), HD)]

    own_in = [
        pltpu.make_async_copy(narrow(key_in, y), k_own, own_sem.at[0]),
        pltpu.make_async_copy(narrow(value_in, y), v_own, own_sem.at[1]),
        pltpu.make_async_copy(wide(query, y), q_own, own_sem.at[2]),
    ]
    for copy in own_in:
        copy.start()
    loads = []
    for c in range(chunks):
        loads.append(pltpu.make_async_copy(tokens.at[:, pl.ds(c * chunk, chunk)], tok_v.at[c], tok_sem.at[c]))
        loads[-1].start()
    rows_in = []
    for g in range(y_count):
        for a, (source, target) in enumerate(((grad_out, cot_v), (attn_out, attn_v))):
            rows_in.append(
                pltpu.make_async_copy(source.at[:, pl.ds(g * WIDE, WIDE)], target.at[g], in_sem.at[a, g])
            )
            rows_in[-1].start()
    pl.semaphore_wait(pltpu.get_barrier_semaphore(), y_count + 1)

    first = []
    for i, other in enumerate(y_peers):
        there = at(other, z)
        for a, (source, target) in enumerate(
            (
                (narrow(key_in, other), k_all.at[z, y]),
                (narrow(value_in, other), v_all.at[z, y]),
                (cnt_v, c_all.at[z, y]),
            )
        ):
            first.append(remote(source, target, y_send.at[a, i], y_recv.at[a, i], there))
            first[-1].start()
    late = []
    for i, other in enumerate(y_peers):
        late.append(remote(wide(query, other), q_all.at[y], y_send.at[3, i], y_recv.at[3, i], at(other, z)))
        late[-1].start()
    own = [
        pltpu.make_async_copy(k_own, k_all.at[z, y], own_sem.at[0]),
        pltpu.make_async_copy(v_own, v_all.at[z, y], own_sem.at[1]),
        pltpu.make_async_copy(cnt_v, c_all.at[z, y], own_sem.at[3]),
        pltpu.make_async_copy(q_own, q_all.at[y], own_sem.at[2]),
    ]
    for copy in own_in:
        copy.wait()
    for copy in own:
        copy.start()
    for copy in own[:3]:
        copy.wait()
    for copy in first:
        copy.wait_recv()

    plan = ring_plan(z_count)
    held = (k_all, v_all)

    def ring_copy(lane, step):
        array, way, _ = plan[lane]
        block = (z - way * step + 2 * z_count) % z_count
        there = at(y, right if way == 1 else left)
        ref = held[array].at[block]
        return remote(ref, ref, ring_send.at[lane, step], ring_recv.at[lane, step], there)

    def count_copy(way, step):
        block = (z - way * step + 2 * z_count) % z_count
        there = at(y, right if way == 1 else left)
        ref = c_all.at[block]
        side = (1 - way) // 2
        return remote(ref, ref, c_send.at[side, step], c_recv.at[side, step], there)

    def forward(step):
        for lane, (array, way, steps) in enumerate(plan):
            if 0 < step <= steps:
                ring_copy(lane, step - 1).wait_recv()
            if step < steps:
                ring_copy(lane, step).start()
            if array == 0:
                if 0 < step <= steps:
                    count_copy(way, step - 1).wait_recv()
                if step < steps:
                    count_copy(way, step).start()

    forward(0)

    token_at = lax.broadcasted_iota(jnp.int32, (tok_count, cap), 0)
    hot = jnp.where(token_at == routes[...], 1.0, 0.0).T.astype(jnp.bfloat16)
    logit = jnp.zeros((cap, HD), jnp.float32)
    for c in range(chunks):
        loads[c].wait()
        picked = jnp.dot(hot, tok_v[c], preferred_element_type=jnp.float32)
        picked_v[c] = picked
        scaled = picked * weight[:, c * chunk : (c + 1) * chunk]
        for t in range(chunk // HD):
            logit = logit + scaled[:, t * HD : (t + 1) * HD]
    logit = jnp.sum(logit, axis=1, keepdims=True)
    gate = 1.0 / (1.0 + jnp.exp(-logit))
    live = lax.broadcasted_iota(jnp.int32, (cap, 1), 0) < counts[0, 0]
    kept = jnp.where(live, gate, 0.0)
    for copy in rows_in:
        copy.wait()

    lane_at = lax.broadcasted_iota(jnp.int32, (cap, HD), 1)

    def scale_group(other):
        gate_sum = jnp.zeros((cap, HD), jnp.float32)
        deltas = jnp.zeros((cap, HD), jnp.float32)
        for h in range(GROUP):
            cols = slice(h * HD, (h + 1) * HD)
            cot = cot_v[other, :, cols].astype(jnp.float32)
            out = attn_v[other, :, cols].astype(jnp.float32)
            dout = (kept * cot).astype(jnp.bfloat16)
            dout_v[other, :, cols] = dout
            gate_sum = gate_sum + cot * out
            delta = jnp.sum(dout.astype(jnp.float32) * out, axis=1, keepdims=True)
            deltas = jnp.where(lane_at == h, delta, deltas)
        de_v[other] = deltas.T[:GROUP]
        return gate_sum

    gate_sum = jnp.zeros((cap, HD), jnp.float32)
    for i, other in enumerate(y_peers):
        gate_sum = gate_sum + scale_group(other)
        for a, (source, target) in enumerate(((dout_v, do_all), (de_v, de_all))):
            late.append(
                remote(source.at[other], target.at[y], y_send.at[4 + a, i], y_recv.at[4 + a, i], at(other, z))
            )
            late[-1].start()
    forward(1)
    gate_sum = gate_sum + scale_group(y)
    mine = [
        pltpu.make_async_copy(dout_v.at[y], do_all.at[y], own_sem.at[4]),
        pltpu.make_async_copy(de_v.at[y], de_all.at[y], own_sem.at[5]),
    ]
    for copy in mine:
        copy.start()
    forward(2)
    gate_grad = jnp.sum(gate_sum, axis=1, keepdims=True)
    logit_grad = jnp.where(live, gate_grad * gate * (1.0 - gate), 0.0)
    segments = part.shape[1]
    for c in range(chunks):
        terms = jnp.sum(logit_grad * picked_v[c], axis=0, keepdims=True)
        for t in range(chunk // HD):
            n = c * (chunk // HD) + t
            part[n // segments, n % segments : n % segments + 1, :] = terms[:, t * HD : (t + 1) * HD]
    for step in range(3, max(p[2] for p in plan) + 1):
        forward(step)
    own[3].wait()
    for copy in mine:
        copy.wait()
    for copy in first:
        copy.wait_send()
    for copy in late:
        copy.wait()
    for lane, (array, way, steps) in enumerate(plan):
        for step in range(steps):
            ring_copy(lane, step).wait_send()
            if array == 0:
                count_copy(way, step).wait_send()


def gather(y_count, z_count, dp_count, tokens, weight, routes, counts, query, key_in, value_in, attn_out, grad_out):
    cap = query.shape[0]
    tok_count, width = tokens.shape
    chunks = 5
    longer = z_count // 2
    anywhere = pl.BlockSpec(memory_space=pl.ANY)
    vmem = pl.BlockSpec(memory_space=pltpu.VMEM)
    smem = pl.BlockSpec(memory_space=pltpu.SMEM)
    bf16, f32 = jnp.bfloat16, jnp.float32
    shape = jax.ShapeDtypeStruct
    return pl.pallas_call(
        functools.partial(gather_kernel, y_count, z_count, chunks),
        out_shape=(
            shape((y_count, cap, WIDE), bf16),
            shape((y_count, cap, WIDE), bf16),
            shape((y_count, GROUP, cap), f32),
            shape((z_count, y_count, cap, HD), bf16),
            shape((z_count, y_count, cap, HD), bf16),
            shape((z_count, y_count, 1, HD), jnp.int32),
            shape((dp_count, width // HD // dp_count, HD), f32),
        ),
        in_specs=[anywhere, vmem, vmem, smem] + [anywhere] * 5,
        out_specs=(anywhere,) * 6 + (vmem,),
        scratch_shapes=[
            pltpu.VMEM((chunks, tok_count, width // chunks), bf16),
            pltpu.VMEM((y_count, cap, WIDE), bf16),
            pltpu.VMEM((y_count, cap, WIDE), bf16),
            pltpu.VMEM((y_count, cap, WIDE), bf16),
            pltpu.VMEM((y_count, GROUP, cap), f32),
            pltpu.VMEM((1, HD), jnp.int32),
            pltpu.VMEM((chunks, cap, width // chunks), f32),
            pltpu.VMEM((cap, WIDE), bf16),
            pltpu.VMEM((cap, HD), bf16),
            pltpu.VMEM((cap, HD), bf16),
            pltpu.SemaphoreType.DMA((chunks,)),
            pltpu.SemaphoreType.DMA((2, y_count)),
            pltpu.SemaphoreType.DMA((6,)),
            pltpu.SemaphoreType.DMA((6, y_count - 1)),
            pltpu.SemaphoreType.DMA((6, y_count - 1)),
            pltpu.SemaphoreType.DMA((4, longer)),
            pltpu.SemaphoreType.DMA((4, longer)),
            pltpu.SemaphoreType.DMA((2, longer)),
            pltpu.SemaphoreType.DMA((2, longer)),
        ],
        compiler_params=pltpu.CompilerParams(
            collective_id=0, has_side_effects=True, vmem_limit_bytes=63 * MIB
        ),
        name="gather",
    )(tokens, weight, routes, counts, query, key_in, value_in, attn_out, grad_out)


def attention_kernel(
    y_count, z_count, block_rows, block_keys,
    counts, q_hbm, do_hbm, de_hbm, k_hbm, v_hbm,
    dq_hbm, dk_hbm, dv_hbm,
    q_in, do_in, de_in, k_in, v_in, dk_out, dv_out, in_sem, out_sem,
    q_b, do_b, de_b, k_f, v_f, k_b, kt_b, v_b, exps, tops, best, total, dk_f, dv_f, dq_f,
    s_even, s_odd, p_even, p_odd, ds_even, ds_odd, pair_row, pair_key, shard_start,
):
    loads = []
    for i, (source, target) in enumerate(
        ((k_hbm, k_in), (v_hbm, v_in), (q_hbm, q_in), (do_hbm, do_in), (de_hbm, de_in))
    ):
        loads.append(pltpu.make_async_copy(source, target, in_sem.at[i]))
        loads[-1].start()
    cap = q_in.shape[1]
    z = lax.axis_index("seq") % z_count
    shard_count = y_count * z_count
    lanes = GROUP * block_rows
    key_blocks = KEEP // block_keys
    root = 1.0 / math.sqrt(HD)
    power = root * math.log2(math.e)
    f32, bf16 = jnp.float32, jnp.bfloat16
    s_b, p_b, ds_b = (s_even, s_odd), (p_even, p_odd), (ds_even, ds_odd)

    def count_of(shard):
        return counts[shard % z_count, shard // z_count, 0, 0]

    keys_before = jnp.int32(0)
    for shard in range(shard_count):
        shard_start[shard] = keys_before
        keys_before = keys_before + count_of(shard)

    def pack(source, target, step, carry):
        for more in range(4):
            shard = step * 4 + more
            rows = pl.ds(shard_start[shard], cap)
            target[rows, :] = source[shard % z_count, shard // z_count].astype(f32)
        return carry

    loads[0].wait()
    lax.fori_loop(0, shard_count // 4, functools.partial(pack, k_in, k_f), 0)
    loads[1].wait()
    lax.fori_loop(0, shard_count // 4, functools.partial(pack, v_in, v_f), 0)

    def narrow_keys(b, carry):
        rows = pl.ds(b * block_keys, block_keys)
        k_b[b] = k_f[rows, :].astype(bf16)
        kt_b[b] = k_f[rows, :].T.astype(bf16)
        v_b[b] = v_f[rows, :].astype(bf16)
        dk_f[b] = jnp.zeros((block_keys, HD), f32)
        dv_f[b] = jnp.zeros((block_keys, HD), f32)
        return carry

    lax.fori_loop(0, key_blocks, narrow_keys, 0)

    halves = cap // block_rows
    row_blocks = y_count * halves

    def first_place(b):
        return shard_start[b // halves * z_count + z] + b % halves * block_rows

    def live_rows(b):
        return jnp.clip(counts[z, b // halves, 0, 0] - b % halves * block_rows, 0, block_rows)

    for load in loads[2:]:
        load.wait()
    for b in range(row_blocks):
        here = slice(b % halves * block_rows, (b % halves + 1) * block_rows)
        for h in range(GROUP):
            mine, cols = slice(h * block_rows, (h + 1) * block_rows), slice(h * HD, (h + 1) * HD)
            q_b[b, mine, :] = q_in[b // halves, here, cols]
            do_b[b, mine, :] = do_in[b // halves, here, cols]
            de_b[b, :, mine] = de_in[b // halves, h : h + 1, here]

    nt = (((1,), (1,)), ((), ()))

    def list_pairs(masked, count):
        def of_rows(b, count):
            full = (first_place(b) + 1) // block_keys
            used = (first_place(b) + live_rows(b) - 1) // block_keys + 1
            used = jnp.where(live_rows(b) > 0, used, 0)
            full = jnp.minimum(full, used)

            def add(kb, count):
                pair_row[count] = b
                pair_key[count] = kb
                return count + 1

            first, last = (full, used) if masked else (0, full)
            return lax.fori_loop(first, last, add, count)

        return lax.fori_loop(0, row_blocks, of_rows, count)

    whole_pairs = list_pairs(False, jnp.int32(0))
    pairs = list_pairs(True, whole_pairs)
    for more in range(3):
        pair_row[pairs + more] = q_b.shape[0] - 1
        pair_key[pairs + more] = 0

    def start_rows(b, carry):
        best[b] = jnp.full((8, lanes), NEGATIVE, f32)
        total[b] = jnp.zeros((8, lanes), f32)
        dq_f[b] = jnp.zeros((HD, lanes), f32)
        return carry

    lax.fori_loop(0, row_blocks, start_rows, 0)

    def raw(n, slot):
        s_b[slot][:, :] = lax.dot_general(
            k_b[pair_key[n]], q_b[pair_row[n]], nt, preferred_element_type=f32
        )

    def grow(masked, n, slot):
        b, kb = pair_row[n], pair_key[n]
        if masked:
            lane = lax.broadcasted_iota(jnp.int32, (8, SUB_LANES), 1)
            sublane = lax.broadcasted_iota(jnp.int32, (8, SUB_LANES), 0)
            ahead = first_place(b) - kb * block_keys + lane % block_rows - sublane
        for part in range(lanes // SUB_LANES):
            cols = slice(part * SUB_LANES, (part + 1) * SUB_LANES)
            block = s_b[slot][:, cols] * power
            if masked:
                allowed = ahead[None] >= 8 * lax.broadcasted_iota(jnp.int32, (block_keys // 8, 8, SUB_LANES), 0)
                block = jnp.where(allowed, block.reshape(block_keys // 8, 8, SUB_LANES), NEGATIVE)
            block = block.reshape(block_keys // 8, 8, SUB_LANES)
            before = best[b, :, cols]
            after = jnp.maximum(before, jnp.max(block, axis=0))
            grown = jnp.exp2(block - after)
            exps[n, :, :, cols] = grown
            tops[n, :, cols] = after
            best[b, :, cols] = after
            total[b, :, cols] = total[b, :, cols] * jnp.exp2(before - after) + jnp.sum(grown, axis=0)

    def some_scores(masked, many, j, carry):
        for more in range(many):
            n = many * j + more
            raw(n + 1, (more + 1) % 2)
            grow(masked, n, more % 2)
        return carry

    raw(0, 0)
    done = jnp.int32(0)
    for many in DEEP:
        lax.fori_loop(done // many, whole_pairs // many, functools.partial(some_scores, False, many), 0)
        done = whole_pairs // many * many
    fours = jnp.maximum(pairs - done, 0) // 4

    def four_scores(j, carry):
        for more in range(4):
            n = done + 4 * j + more
            raw(n + 1, (more + 1) % 2)
            grow(True, n, more % 2)
        return carry

    lax.fori_loop(0, fours, four_scores, 0)
    done = done + 4 * fours
    lax.fori_loop(done // 2, (pairs + 1) // 2, functools.partial(some_scores, True, 2), 0)

    def finish_rows(b, carry):
        top = jnp.max(best[b], axis=0, keepdims=True)
        summed = jnp.sum(total[b] * jnp.exp2(best[b] - top), axis=0, keepdims=True)
        best[b] = jnp.broadcast_to(top + jnp.log2(summed), (8, lanes))
        return carry

    lax.fori_loop(0, row_blocks, finish_rows, 0)

    def terms(n, slot):
        b, kb = pair_row[n], pair_key[n]
        scale = jnp.exp2(tops[n] - best[b])
        prob = (exps[n] * scale).reshape(block_keys, lanes)
        prob_grad = lax.dot_general(v_b[kb], do_b[b], nt, preferred_element_type=f32)
        p_b[slot][:, :] = prob.astype(bf16)
        ds_b[slot][:, :] = (prob * (prob_grad - de_b[b])).astype(bf16)

    def products(n, slot):
        b, kb = pair_row[n], pair_key[n]
        score_grad = ds_b[slot][:, :]
        dv_f[kb] += jnp.dot(p_b[slot][:, :], do_b[b], preferred_element_type=f32)
        dk_f[kb] += jnp.dot(score_grad, q_b[b], preferred_element_type=f32)
        dq_f[b] += jnp.dot(kt_b[kb], score_grad, preferred_element_type=f32)

    def some_pairs(many, j, carry):
        for more in range(many):
            n = many * j + more
            products(n, more % 2)
            terms(n + 1, (more + 1) % 2)
        return carry

    @pl.when(pairs > 0)
    def _():
        terms(0, 0)

    done = jnp.int32(0)
    for many in DEEP:
        lax.fori_loop(done // many, pairs // many, functools.partial(some_pairs, many), 0)
        done = pairs // many * many

    @pl.when(pairs % 2 == 1)
    def _():
        products(pairs - 1, 0)

    stores = [
        pltpu.make_async_copy(dq_f, dq_hbm, out_sem.at[0]),
        pltpu.make_async_copy(dk_out, dk_hbm, out_sem.at[1]),
        pltpu.make_async_copy(dv_out, dv_hbm, out_sem.at[2]),
    ]
    stores[0].start()
    slot = lax.broadcasted_iota(jnp.int32, (cap, 1), 0)

    def unpack(total, scale, packed, target, store):
        def widen(b, carry):
            rows = pl.ds(pl.multiple_of(b * block_keys, block_keys), block_keys)
            packed[rows, :] = total[b] * scale
            return carry

        def place_shards(step, carry):
            for more in range(4):
                shard = step * 4 + more
                rows = packed[pl.ds(shard_start[shard], cap), :]
                rows = jnp.where(slot < count_of(shard), rows, 0.0)
                target[shard % z_count, shard // z_count] = rows.astype(bf16)
            return carry

        lax.fori_loop(0, key_blocks, widen, 0)
        lax.fori_loop(0, shard_count // 4, place_shards, 0)
        store.start()

    unpack(dk_f, root, k_f, dk_out, stores[1])
    unpack(dv_f, 1.0, v_f, dv_out, stores[2])
    for store in stores:
        store.wait()


def attention(y_count, z_count, counts, q_in, do_in, de_in, k_in, v_in):
    cap = q_in.shape[1]
    block_rows, block_keys = 64, 256
    lanes = GROUP * block_rows
    most = y_count * cap
    row_blocks = most // block_rows
    key_blocks = KEEP // block_keys
    anywhere = pl.BlockSpec(memory_space=pl.ANY)
    bf16, f32 = jnp.bfloat16, jnp.float32
    shape = jax.ShapeDtypeStruct
    return pl.pallas_call(
        functools.partial(attention_kernel, y_count, z_count, block_rows, block_keys),
        out_shape=(
            shape((row_blocks, HD, lanes), f32),
            shape((z_count, y_count, cap, HD), bf16),
            shape((z_count, y_count, cap, HD), bf16),
        ),
        in_specs=[pl.BlockSpec(memory_space=pltpu.SMEM)] + [anywhere] * 5,
        out_specs=(anywhere,) * 3,
        scratch_shapes=[
            pltpu.VMEM((y_count, cap, WIDE), bf16),
            pltpu.VMEM((y_count, cap, WIDE), bf16),
            pltpu.VMEM((y_count, GROUP, cap), f32),
            pltpu.VMEM((z_count, y_count, cap, HD), bf16),
            pltpu.VMEM((z_count, y_count, cap, HD), bf16),
            pltpu.VMEM((z_count, y_count, cap, HD), bf16),
            pltpu.VMEM((z_count, y_count, cap, HD), bf16),
            pltpu.SemaphoreType.DMA((5,)),
            pltpu.SemaphoreType.DMA((3,)),
            pltpu.VMEM((row_blocks + 1, lanes, HD), bf16),
            pltpu.VMEM((row_blocks + 1, lanes, HD), bf16),
            pltpu.VMEM((row_blocks + 1, 1, lanes), f32),
            pltpu.VMEM((KEEP + cap, HD), f32),
            pltpu.VMEM((KEEP + cap, HD), f32),
            pltpu.VMEM((key_blocks, block_keys, HD), bf16),
            pltpu.VMEM((key_blocks, HD, block_keys), bf16),
            pltpu.VMEM((key_blocks, block_keys, HD), bf16),
            pltpu.VMEM((row_blocks * key_blocks + 1, block_keys // 8, 8, lanes), f32),
            pltpu.VMEM((row_blocks * key_blocks + 1, 8, lanes), f32),
            pltpu.VMEM((row_blocks + 1, 8, lanes), f32),
            pltpu.VMEM((row_blocks + 1, 8, lanes), f32),
            pltpu.VMEM((key_blocks, block_keys, HD), f32),
            pltpu.VMEM((key_blocks, block_keys, HD), f32),
            pltpu.VMEM((row_blocks, HD, lanes), f32),
            pltpu.VMEM((block_keys, lanes), f32),
            pltpu.VMEM((block_keys, lanes), f32),
            pltpu.VMEM((block_keys, lanes), bf16),
            pltpu.VMEM((block_keys, lanes), bf16),
            pltpu.VMEM((block_keys, lanes), bf16),
            pltpu.VMEM((block_keys, lanes), bf16),
            pltpu.SMEM((row_blocks * key_blocks + 3,), jnp.int32),
            pltpu.SMEM((row_blocks * key_blocks + 3,), jnp.int32),
            pltpu.SMEM((y_count * z_count,), jnp.int32),
        ],
        compiler_params=pltpu.CompilerParams(vmem_limit_bytes=62 * MIB),
        name="attention",
    )(counts, q_in, do_in, de_in, k_in, v_in)


def scatter_kernel(
    y_count, z_count, dp_count,
    dq_hbm, dk_hbm, dv_hbm, part,
    dq_out, dk_out, dv_out, router_out, dq_in, dk_in, dv_in,
    held, fin, dp_held, y_held, z_held, dp_sum, y_sum, dq_v,
    own_sem, q_send, q_recv, ring_send, ring_recv, fin_send, fin_recv, r_send, r_recv,
):
    y, z = place(z_count)
    dp = lax.axis_index("dp")
    f32, bf16 = jnp.float32, jnp.bfloat16

    def at(y_there, z_there):
        return {"seq": y_there * z_count + z_there}

    right, left = (z + 1) % z_count, (z + z_count - 1) % z_count
    y_peers = [(y + step) % y_count for step in range(1, y_count)]
    z_peers = [(z + step) % z_count for step in range(1, z_count)]
    dp_peers = [(dp + step) % dp_count for step in range(1, dp_count)]
    peers = [at(other, z) for other in y_peers] + [at(y, other) for other in z_peers]
    peers += [{"dp": other} for other in dp_peers]
    greet(peers)

    def wide(ref, g):
        return ref.at[:, pl.ds(pl.multiple_of(g * WIDE, WIDE), WIDE)]

    def narrow(ref, g):
        return ref.at[:, pl.ds(pl.multiple_of(g * HD, HD), HD)]

    own_in = [
        pltpu.make_async_copy(dk_hbm, dk_in, own_sem.at[1]),
        pltpu.make_async_copy(dv_hbm, dv_in, own_sem.at[2]),
        pltpu.make_async_copy(dq_hbm, dq_in, own_sem.at[0]),
    ]
    for copy in own_in[:2]:
        copy.start()
    for copy in own_in[:2]:
        copy.wait()
    pl.semaphore_wait(pltpu.get_barrier_semaphore(), len(peers))

    plan = ring_plan(z_count)
    mine = (dk_in, dv_in)

    def ring_copy(lane, step):
        array, way, steps = plan[lane]
        block = (z + way * (steps - step) + z_count) % z_count
        there = at(y, right if way == 1 else left)
        source = mine[array].at[block] if step == 0 else held.at[lane, step - 1]
        return remote(source, held.at[lane, step], ring_send.at[lane, step], ring_recv.at[lane, step], there)

    def forward(step):
        for lane, (array, way, steps) in enumerate(plan):
            if step < steps:
                if step > 0:
                    ring_copy(lane, step - 1).wait_recv()
                    block = (z + way * (steps - step) + z_count) % z_count
                    for g in range(y_count):
                        total = held[lane, step - 1, g].astype(f32) + mine[array][block, g].astype(f32)
                        held[lane, step - 1, g] = total.astype(bf16)
                ring_copy(lane, step).start()

    forward(0)
    own_in[2].start()
    own_in[2].wait()
    block_rows = dq_in.shape[2] // GROUP
    halves = dq_v.shape[1] // block_rows

    def turn_rows(b, carry):
        rows = pl.ds(pl.multiple_of(b % halves * block_rows, block_rows), block_rows)
        turned = (dq_in[b].T * (1.0 / math.sqrt(HD))).astype(bf16)
        for h in range(GROUP):
            dq_v[b // halves, rows, h * HD : (h + 1) * HD] = turned[h * block_rows : (h + 1) * block_rows, :]
        return carry

    lax.fori_loop(0, dq_in.shape[0], turn_rows, 0)
    sends = []
    for i, other in enumerate(y_peers):
        sends.append(remote(dq_v.at[other], wide(dq_out, y), q_send.at[i], q_recv.at[i], at(other, z)))
        sends[-1].start()
    own = [pltpu.make_async_copy(dq_v.at[y], wide(dq_out, y), own_sem.at[0])]
    own[0].start()

    def share(first, source_of, held_ref, peers_there, me):
        copies = []
        for i, there in enumerate(peers_there):
            copies.append(remote(source_of(i), held_ref.at[me], r_send.at[first + i], r_recv.at[first + i], there))
            copies[-1].start()
        return copies

    over_dp = share(0, lambda i: part.at[dp_peers[i]], dp_held, [{"dp": other} for other in dp_peers], dp)
    forward(1)
    for copy in over_dp:
        copy.wait()
    total = part[dp]
    for other in dp_peers:
        total = total + dp_held[other]
    dp_sum[...] = total
    over_y = share(dp_count - 1, lambda i: dp_sum, y_held, [at(other, z) for other in y_peers], y)
    forward(2)
    for copy in over_y:
        copy.wait()
    for other in y_peers:
        total = total + y_held[other]
    y_sum[...] = total
    over_z = share(
        dp_count + y_count - 2, lambda i: y_sum, z_held, [at(y, other) for other in z_peers], z
    )
    for step in range(3, max(p[2] for p in plan)):
        forward(step)
    for copy in over_z:
        copy.wait()
    for other in z_peers:
        total = total + z_held[other]
    first = lax.axis_index("seq") * router_out.shape[1]
    lane = lax.broadcasted_iota(jnp.int32, (1, HD), 1)
    here = jnp.zeros((1, HD), f32)
    for row in range(total.shape[0]):
        turned = pltpu.roll(total[row : row + 1, :], (HD - first % HD) % HD, 1)
        here = jnp.where((first + lane) // HD == row, turned, here)
    router_out[...] = here[:, : router_out.shape[1]]

    ends = []
    for array, target in ((0, dk_out), (1, dv_out)):
        lanes = [lane for lane in range(4) if plan[lane][0] == array]
        for lane in lanes:
            ring_copy(lane, plan[lane][2] - 1).wait_recv()
        for g in range(y_count):
            total = mine[array][z, g].astype(f32)
            for lane in lanes:
                total = total + held[lane, plan[lane][2] - 1, g].astype(f32)
            fin[array, g] = total.astype(bf16)
        for i, other in enumerate(y_peers):
            ends.append(
                remote(
                    fin.at[array, other],
                    narrow(target, y),
                    fin_send.at[array, i],
                    fin_recv.at[array, i],
                    at(other, z),
                )
            )
            ends[-1].start()
        own.append(pltpu.make_async_copy(fin.at[array, y], narrow(target, y), own_sem.at[1 + array]))
        own[-1].start()
    for lane, (array, way, steps) in enumerate(plan):
        for step in range(steps):
            ring_copy(lane, step).wait_send()
    for copy in own + sends + ends:
        copy.wait()


def scatter(y_count, z_count, dp_count, dq_in, dk_in, dv_in, part):
    share = part.shape[1] * HD // (y_count * z_count)
    cap = dk_in.shape[2]
    longer = z_count // 2
    small = part.shape[1:]
    anywhere = pl.BlockSpec(memory_space=pl.ANY)
    vmem = pl.BlockSpec(memory_space=pltpu.VMEM)
    bf16, f32 = jnp.bfloat16, jnp.float32
    shape = jax.ShapeDtypeStruct
    router_copies = dp_count + y_count + z_count - 3
    return pl.pallas_call(
        functools.partial(scatter_kernel, y_count, z_count, dp_count),
        out_shape=(
            shape((cap, HEADS * HD), bf16),
            shape((cap, KV * HD), bf16),
            shape((cap, KV * HD), bf16),
            shape((1, share), f32),
        ),
        in_specs=[anywhere, anywhere, anywhere, vmem],
        out_specs=(anywhere, anywhere, anywhere, vmem),
        scratch_shapes=[
            pltpu.VMEM(dq_in.shape, f32),
            pltpu.VMEM((z_count, y_count, cap, HD), bf16),
            pltpu.VMEM((z_count, y_count, cap, HD), bf16),
            pltpu.VMEM((4, longer, y_count, cap, HD), bf16),
            pltpu.VMEM((2, y_count, cap, HD), bf16),
            pltpu.VMEM((dp_count,) + small, f32),
            pltpu.VMEM((y_count,) + small, f32),
            pltpu.VMEM((z_count,) + small, f32),
            pltpu.VMEM(small, f32),
            pltpu.VMEM(small, f32),
            pltpu.VMEM((y_count, cap, WIDE), bf16),
            pltpu.SemaphoreType.DMA((3,)),
            pltpu.SemaphoreType.DMA((y_count - 1,)),
            pltpu.SemaphoreType.DMA((y_count - 1,)),
            pltpu.SemaphoreType.DMA((4, longer)),
            pltpu.SemaphoreType.DMA((4, longer)),
            pltpu.SemaphoreType.DMA((2, y_count - 1)),
            pltpu.SemaphoreType.DMA((2, y_count - 1)),
            pltpu.SemaphoreType.DMA((router_copies,)),
            pltpu.SemaphoreType.DMA((router_copies,)),
        ],
        compiler_params=pltpu.CompilerParams(
            collective_id=1, has_side_effects=True, vmem_limit_bytes=63 * MIB
        ),
        name="scatter",
    )(dq_in, dk_in, dv_in, part)


def result_kernel(
    dq_in, dk_in, dv_in, share_in, dq_out, dk_out, dv_out, share_out, dq_v, dk_v, dv_v, share_v, in_sem, out_sem
):
    moves = []
    rows = dq_v.shape[1]
    for i in range(dq_v.shape[0]):
        part = pl.ds(i * rows, rows)
        moves.append((dq_in.at[part], dq_v.at[i], dq_out.at[part]))
    moves += [(dk_in, dk_v, dk_out), (dv_in, dv_v, dv_out), (share_in, share_v, share_out)]
    loads = [pltpu.make_async_copy(a, b, in_sem.at[i]) for i, (a, b, _) in enumerate(moves)]
    stores = [pltpu.make_async_copy(b, c, out_sem.at[i]) for i, (_, b, c) in enumerate(moves)]
    for load in loads:
        load.start()
    for load, store in zip(loads, stores):
        load.wait()
        store.start()
    for store in stores:
        store.wait()


def results(dq, dk, dv, share):
    anywhere = pl.BlockSpec(memory_space=pl.ANY)
    pieces = 4
    shape = jax.ShapeDtypeStruct
    return pl.pallas_call(
        result_kernel,
        out_shape=tuple(shape(x.shape, x.dtype) for x in (dq, dk, dv, share)),
        in_specs=[anywhere] * 4,
        out_specs=(anywhere,) * 4,
        scratch_shapes=[
            pltpu.VMEM((pieces, dq.shape[0] // pieces, dq.shape[1]), dq.dtype),
            pltpu.VMEM(dk.shape, dk.dtype),
            pltpu.VMEM(dv.shape, dv.dtype),
            pltpu.VMEM(share.shape, share.dtype),
            pltpu.SemaphoreType.DMA((pieces + 3,)),
            pltpu.SemaphoreType.DMA((pieces + 3,)),
        ],
        compiler_params=pltpu.CompilerParams(vmem_limit_bytes=63 * MIB),
        name="results",
    )(dq, dk, dv, share)


def on_device(tokens, router_weight, routes, counts, query, key_in, value_in, attn_out, grad_out):
    y_count = KV
    z_count = lax.axis_size("seq") // y_count
    dp_count = lax.axis_size("dp")
    q_all, do_all, de_all, k_all, v_all, c_all, part = gather(
        y_count, z_count, dp_count, tokens[0], router_weight[None], routes, counts,
        query[0], key_in[0], value_in[0], attn_out[0], grad_out[0],
    )
    dq, dk, dv = attention(y_count, z_count, c_all, q_all, do_all, de_all, k_all, v_all)
    dq, dk, dv, router = scatter(y_count, z_count, dp_count, dq, dk, dv, part)
    dq, dk, dv, router = results(dq, dk, dv, router)
    return (dq[None], dk[None], dv[None], router[0])


def solution(mesh):
    rows = P("dp", "seq", None)
    return jax.shard_map(
        on_device,
        mesh=mesh,
        in_specs=(rows, P(), P("dp", "seq"), P("dp", "seq"), rows, rows, rows, rows, rows),
        out_specs=(rows, rows, rows, P(("dp", "seq"))),
        check_vma=False,
    )
```
